512 devices in a mesh: space: 64 (over x, y, z_hi), tm: 8 (over z_lo, core).
Axes of the slice: x: 4, y: 8, z: 8 (z_hi: 2, z_lo: 4; z = z_hi * 4 + z_lo), core: 2. Of those that a mesh axis runs over, the one named last changes fastest.
Arguments:
- links: float32 [4, 2, 3, 3, 128, 16, 128], P(None, None, None, None, 'space', 'tm'), as said below
- kernel: float32 [3, 3, 3, 3, 4, 8], replicated, may hold values from -0.25 to 0.25
- active: int32 [128, 16, 128], P('space', 'tm'), may hold values 0 or 1
- direction: int32 [128, 16, 128], P('space', 'tm'), may hold values from 0 to 3
- out_grad: float32 [4, 2, 3, 3, 128, 16, 128], P(None, None, None, None, 'space', 'tm'), may hold values from -6 to 6
Outputs:
- link_grad: float32 [4, 2, 3, 3, 128, 16, 128], P(None, None, None, None, 'space', 'tm')
- kernel_grad: float32 [3, 3, 3, 3, 4, 8], replicated
The draws below stay inside these ranges and needn't reach their ends.
Inputs may be any that keep to these rules, and one draw needn't show every extreme that they name: `links`: every link is special unitary: its rows are orthonormal and its third row is the complex conjugate of the cross product of its first two rows, up to float32 rounding.
All inputs are finite; a program needn't handle non-finite values. No bound on the sum of `active` on one device may be relied on, other than what follows from the above.
Results may differ from the reference program's by a relative error of at most 0.0003.
Values sent between devices are 32-bit elements; how exact they have to be, the bound alone decides.
A program may use at most 128 MiB of HBM per device.

```python
import math
import jax
import jax.numpy as jnp
from jax import lax

LY = 8
LZ = 16
DIRS = 4
CH = 8
KW = 3
LX = 128
LT = 16
YZ = 128
SITES = 262144


def complex_product(first, second):
    real_rows = []
    imag_rows = []
    for row in range(3):
        real_line = []
        imag_line = []
        for column in range(3):
            real_acc = first[0][row][0] * second[0][0][column] - first[1][row][0] * second[1][0][column]
            imag_acc = first[0][row][0] * second[1][0][column] + first[1][row][0] * second[0][0][column]
            for inner in range(1, 3):
                real_acc = real_acc + first[0][row][inner] * second[0][inner][column] - first[1][row][inner] * second[1][inner][column]
                imag_acc = imag_acc + first[0][row][inner] * second[1][inner][column] + first[1][row][inner] * second[0][inner][column]
            real_line.append(real_acc)
            imag_line.append(imag_acc)
        real_rows.append(real_line)
        imag_rows.append(imag_line)
    return (real_rows, imag_rows)


def embedded_rotation(key, shape, first_index, second_index):
    key_polar, key_azimuth, key_twist = jax.random.split(key, 3)
    polar = jnp.arccos(jax.random.uniform(key_polar, shape, jnp.float32, -0.98, 0.98)) * 0.5 + 0.3
    azimuth = jax.random.uniform(key_azimuth, shape, jnp.float32, -math.pi, math.pi)
    twist = jax.random.uniform(key_twist, shape, jnp.float32, -math.pi, math.pi)
    scalar_part = jnp.cos(polar)
    first_vec = jnp.sin(polar) * jnp.cos(azimuth)
    second_vec = jnp.sin(polar) * jnp.sin(azimuth) * jnp.cos(twist)
    third_vec = jnp.sin(polar) * jnp.sin(azimuth) * jnp.sin(twist)
    zeros = jnp.zeros(shape, jnp.float32)
    ones = jnp.ones(shape, jnp.float32)
    real_rows = [[ones if row == column else zeros for column in range(3)] for row in range(3)]
    imag_rows = [[zeros for column in range(3)] for row in range(3)]
    real_rows[first_index][first_index] = scalar_part
    imag_rows[first_index][first_index] = third_vec
    real_rows[first_index][second_index] = second_vec
    imag_rows[first_index][second_index] = first_vec
    real_rows[second_index][first_index] = -second_vec
    imag_rows[second_index][first_index] = first_vec
    real_rows[second_index][second_index] = scalar_part
    imag_rows[second_index][second_index] = -third_vec
    return (real_rows, imag_rows)


def draw_links(key, part):
    shape = (4, LX, LT, LY * LZ)
    key_one, key_two, key_three, key_phase = jax.random.split(jax.random.fold_in(key, 17), 4)
    phase_one = jax.random.uniform(jax.random.fold_in(key_phase, 1), shape, jnp.float32, -math.pi, math.pi)
    phase_two = jax.random.uniform(jax.random.fold_in(key_phase, 2), shape, jnp.float32, -math.pi, math.pi)
    phases = [phase_one, phase_two, -(phase_one + phase_two)]
    zeros = jnp.zeros(shape, jnp.float32)
    diagonal_real = [[jnp.cos(phases[row]) if row == column else zeros for column in range(3)] for row in range(3)]
    diagonal_imag = [[jnp.sin(phases[row]) if row == column else zeros for column in range(3)] for row in range(3)]
    product = (diagonal_real, diagonal_imag)
    product = complex_product(embedded_rotation(key_one, shape, 0, 1), product)
    product = complex_product(embedded_rotation(key_two, shape, 1, 2), product)
    product = complex_product(embedded_rotation(key_three, shape, 0, 1), product)
    real_block = jnp.stack([jnp.stack(line) for line in product[0]])
    imag_block = jnp.stack([jnp.stack(line) for line in product[1]])
    stacked = jnp.stack([real_block, imag_block])
    return jnp.moveaxis(stacked, 3, 0).astype(jnp.float32)


def set_ends(values, stream_key, low, high):
    spot = [jax.random.randint(jax.random.fold_in(stream_key, axis), (), 0, length) for axis, length in enumerate(values.shape)]
    main_axis = values.shape.index(max(values.shape))
    beside = spot[:main_axis] + [(spot[main_axis] + 1) % values.shape[main_axis]] + spot[main_axis + 1:]
    return values.at[tuple(spot)].set(low).at[tuple(beside)].set(high)


def block_scale(own_key, dims, cuts, least, top_value):
    def one(axis_at, parts):
        draws = jax.random.uniform(jax.random.fold_in(jax.random.fold_in(own_key, 6), axis_at), (parts,), jnp.float32, least / len(cuts), top_value / len(cuts))
        return jnp.repeat(jnp.exp(draws), dims[axis_at] // parts).reshape((-1,) + (1,) * (len(dims) - axis_at - 1))

    loudness = one(*cuts[0])
    for cut in cuts[1:]:
        loudness = loudness * one(*cut)
    return loudness


def normal_values(own_key, extent, scale, bound, pieces=(), kind=jnp.bfloat16):
    values = jax.random.normal(own_key, extent, jnp.float32) * scale
    if len(pieces) > 0:
        values = block_scale(own_key, extent, pieces, -0.22, 0.18) * values
    return jnp.clip(values, min=-bound, max=bound).astype(kind)


def setup_inputs(seed: int = 0) -> dict:
    key_of = jax.random.split(jax.random.key(seed), 6)
    links = draw_links(jax.random.fold_in(key_of[5], 71), 0)
    kernel = normal_values(key_of[1], (KW, KW, KW, KW, DIRS, CH), (CH * KW ** 4) ** -0.5, 0.25, (), jnp.float32)
    active = set_ends((jax.random.randint(key_of[2], (LX, LT, YZ), 0, 2) < 1).astype(jnp.int32), jax.random.fold_in(key_of[2], 1), 0, 1)
    direction = set_ends(jax.random.randint(key_of[3], (LX, LT, YZ), 0, DIRS), jax.random.fold_in(key_of[3], 1), 0, DIRS - 1).astype(jnp.int32)
    out_grad = normal_values(key_of[4], (DIRS, 2, 3, 3, LX, LT, YZ), 1.0, 6.0, ((4, 64), (5, 8)), jnp.float32)
    return dict(links=links, kernel=kernel, active=active, direction=direction, out_grad=out_grad)


def matrix_mul(first, second):
    real_part = lax.optimization_barrier(jnp.sum(first[0][:, :, None] * second[0][None], axis=1)) - lax.optimization_barrier(jnp.sum(first[1][:, :, None] * second[1][None], axis=1))
    imag_part = lax.optimization_barrier(jnp.sum(first[0][:, :, None] * second[1][None], axis=1)) + lax.optimization_barrier(jnp.sum(first[1][:, :, None] * second[0][None], axis=1))
    return jnp.stack([real_part, imag_part])

def adjoint(matrix):
    return jnp.stack([jnp.swapaxes(matrix[0], 0, 1), -jnp.swapaxes(matrix[1], 0, 1)])

def shift_yz(values, step_y, step_z):
    result = values
    if step_y != 0:
        result = jnp.roll(result, -step_y * LZ, axis=-1)
    z_coord = jnp.arange(values.shape[-1]) % LZ
    if step_z == 1:
        result = jnp.where(z_coord == LZ - 1, jnp.roll(result, LZ - 1, axis=-1), jnp.roll(result, -1, axis=-1))
    if step_z == -1:
        result = jnp.where(z_coord == 0, jnp.roll(result, 1 - LZ, axis=-1), jnp.roll(result, 1, axis=-1))
    return result

def unit_step(course, sign):
    return tuple((sign if coordinate == course else 0 for coordinate in range(4)))

def add_steps(first_step, second_step):
    return tuple((first_step[coordinate] + second_step[coordinate] for coordinate in range(4)))

def staple_sum(fetch, course):
    anchor = (0, 0, 0, 0)
    summed = None
    for across in range(4):
        if across == course:
            continue
        ahead = unit_step(course, 1)
        beside = unit_step(across, 1)
        behind = unit_step(across, -1)
        upper_loop = matrix_mul(matrix_mul(fetch(across, ahead), adjoint(fetch(course, beside))), adjoint(fetch(across, anchor)))
        lower_loop = matrix_mul(matrix_mul(adjoint(fetch(across, add_steps(ahead, behind))), adjoint(fetch(course, behind))), fetch(across, behind))
        paired = upper_loop + lower_loop
        summed = paired if summed is None else summed + paired
    return summed

def loop_features(cores, staples, active):
    frozen = 1.0 - active.astype(jnp.float32)
    channels = []
    for course in range(4):
        own_link = cores[course]
        flipped = jnp.swapaxes(staples[course], 1, 2)
        trace_real = lax.optimization_barrier(jnp.sum(own_link[0] * flipped[0] - own_link[1] * flipped[1], axis=(0, 1)))
        trace_imag = lax.optimization_barrier(jnp.sum(own_link[0] * flipped[1] + own_link[1] * flipped[0], axis=(0, 1)))
        channels.append(frozen * trace_real * (1.0 / 3.0))
        channels.append(frozen * trace_imag * (1.0 / 3.0))
    return jnp.stack(channels)

def kernel_conv(view_features, kernel_taps):
    summed = None
    half = KW // 2
    for shift_x in range(KW):
        for shift_t in range(KW):
            for shift_y in range(KW):
                for shift_z in range(KW):
                    taps = kernel_taps[shift_x, shift_t, shift_y, shift_z]
                    viewed = view_features((shift_x - half, shift_t - half, shift_y - half, shift_z - half))
                    term = jnp.einsum('oc,c...->o...', taps, viewed, precision=lax.Precision.HIGHEST)
                    summed = term if summed is None else summed + term
    return summed

def coupling(cores, staples, fields, active, direction):
    selector = [(direction == course).astype(jnp.float32) for course in range(4)]
    strength = jnp.tanh(selector[0] * fields[0] + selector[1] * fields[1] + selector[2] * fields[2] + selector[3] * fields[3]) * active.astype(jnp.float32)
    chosen = selector[0] * cores[0] + selector[1] * cores[1] + selector[2] * cores[2] + selector[3] * cores[3]
    chosen_staple = selector[0] * staples[0] + selector[1] * staples[1] + selector[2] * staples[2] + selector[3] * staples[3]
    closed = matrix_mul(chosen, chosen_staple)
    antiherm = (closed - adjoint(closed)) * 0.5
    trace_part = (antiherm[:, 0, 0] + antiherm[:, 1, 1] + antiherm[:, 2, 2]) * (1.0 / 3.0)
    identity = jnp.eye(3, dtype=jnp.float32).reshape(1, 3, 3, 1, 1, 1)
    generator = (antiherm - trace_part[:, None, None] * identity) * strength
    unit_matrix = jnp.concatenate([identity, jnp.zeros_like(identity)], axis=0)
    horner = unit_matrix + generator * 0.25
    horner = unit_matrix + matrix_mul(generator, horner) * (1.0 / 3.0)
    horner = unit_matrix + matrix_mul(generator, horner) * 0.5
    exponent = unit_matrix + matrix_mul(generator, horner)
    moved = matrix_mul(exponent, chosen)
    return jnp.stack([jnp.where(direction == course, moved, cores[course]) for course in range(4)])

def roll_view(values, offset):
    moved = jnp.roll(values, -offset[0], axis=values.ndim - 3)
    moved = jnp.roll(moved, -offset[1], axis=values.ndim - 2)
    return shift_yz(moved, offset[2], offset[3])

def reference(links, kernel, active, direction, out_grad):

    def forward(link_field, kernel_taps):

        def fetch(course, offset):
            return roll_view(link_field[course], offset)
        staples = jnp.stack([staple_sum(fetch, course) for course in range(4)])
        features = loop_features(link_field, staples, active)

        def view_features(offset):
            return roll_view(features, offset)
        fields = kernel_conv(view_features, kernel_taps)
        return coupling(link_field, staples, fields, active, direction)
    moved, pullback = jax.vjp(forward, links, kernel)
    link_grad, kernel_part = pullback(out_grad)
    return (link_grad, kernel_part * (1.0 / math.sqrt(SITES)))
```

```python
import functools
import math

import jax
import jax.numpy as jnp
from jax import lax
from jax.experimental import pallas as pl
from jax.experimental.pallas import tpu as pltpu
from jax.sharding import PartitionSpec as P

PAIR = (1, 0, 3, 2)
MESH = pl.DeviceIdType.MESH
F32 = jnp.float32
NEIGHBOURS = tuple((sx, st) for sx in (-1, 0, 1) for st in (-1, 0, 1) if (sx, st) != (0, 0))
FACES = ((-1, 0), (1, 0), (0, -1), (0, 1))
CORNERS = ((1, -1), (-1, 1))
GROWS = 24


def row_of(ext_x, ext_t):
    return 2 + 4 * ext_x + ext_t


def lane_iota(shape):
    return lax.broadcasted_iota(jnp.int32, shape, len(shape) - 1)


def half_mask(shape):
    return ((lax.broadcasted_iota(jnp.int32, shape, len(shape) - 2) >> 1) & 1) == 1


def roll_y(values, step):
    return pltpu.roll(values, (-16 * step) % 128, values.ndim - 1)


def roll_z(values, step):
    axis = values.ndim - 1
    z_coord = lane_iota(values.shape) & 15
    if step == 1:
        return jnp.where(z_coord == 15, pltpu.roll(values, 15, axis), pltpu.roll(values, 127, axis))
    return jnp.where(z_coord == 0, pltpu.roll(values, 113, axis), pltpu.roll(values, 1, axis))


def shift_yz(values, step_y, step_z):
    if step_y:
        values = roll_y(values, step_y)
    if step_z:
        values = roll_z(values, step_z)
    return values


def swap_halves(values):
    axis = values.ndim - 2
    return jnp.where(
        half_mask(values.shape), pltpu.roll(values, 2, axis), pltpu.roll(values, 6, axis)
    )


def split_roll(values, lead, step):
    along_y = roll_y(values, step)
    along_z = roll_z(values, step)
    first, second = (along_y, along_z) if lead == 2 else (along_z, along_y)
    return jnp.where(half_mask(values.shape), second, first)


def rolled(matrix, lead, step):
    return tuple(split_roll(part, lead, step) for part in matrix)


def mul(first, second, adj_first=False, adj_second=False):
    def column(part, k):
        return jnp.expand_dims(part[k] if adj_first else part[:, k], 1)

    def line(part, k):
        return jnp.expand_dims(part[:, k] if adj_second else part[k], 0)

    sums = [None] * 4
    for k in range(3):
        fr, fi = column(first[0], k), column(first[1], k)
        sr, si = line(second[0], k), line(second[1], k)
        terms = (fr * sr, fi * si, fr * si, fi * sr)
        sums = [t if s is None else s + t for s, t in zip(sums, terms)]
    rr, ii, ri, ir = sums
    real = rr + ii if adj_first != adj_second else rr - ii
    if adj_first and adj_second:
        imag = -(ri + ir)
    elif adj_first:
        imag = ri - ir
    elif adj_second:
        imag = ir - ri
    else:
        imag = ri + ir
    return (real, imag)


def add(first, second):
    return (first[0] + second[0], first[1] + second[1])


def scaled(matrix, factor):
    return (matrix[0] * factor, matrix[1] * factor)


def view(ref, course, dx, dt):
    start = row_of(1 + dx, 1 + dt)
    pair_start = row_of(1 + dt, 1 + dx) - 2
    parts = []
    for part in range(2):
        own = ref[course, part, :, :, pl.ds(start, 8), :]
        other = ref[PAIR[course], part, :, :, pl.ds(pair_start, 8), :]
        parts.append(jnp.where(half_mask(own.shape), other, own))
    return tuple(parts)


def view_at(ref, course, lead, step):
    if lead == 0:
        return view(ref, course, step, 0)
    if lead == 1:
        return view(ref, course, 0, step)
    return rolled(view(ref, course, 0, 0), lead, step)


ORDER = ((2, 3), (0, 1), (0, 2), (0, 3), (2, 0), (2, 1))


def legs_above(ref, course, across):
    return (
        view_at(ref, across, course, 1),
        view_at(ref, course, across, 1),
        view(ref, across, 0, 0),
    )


def legs_below(ref, course, across):
    if across >= 2:
        return (
            view(ref, course, 0, 0),
            view_at(ref, across, course, 1),
            view(ref, across, 0, 0),
        )
    back = (-1, 0) if across == 0 else (0, -1)
    base = view(ref, across, *back)
    if course >= 2:
        ahead = rolled(base, course, 1)
    else:
        step = (back[0] + (course == 0), back[1] + (course == 1))
        ahead = view(ref, across, *step)
    return (view(ref, course, *back), ahead, base)


def third_line(first, second):
    out = []
    for j in range(3):
        p, q = (j + 1) % 3, (j + 2) % 3
        (ar, ai), (br, bi) = first[p], second[q]
        (cr, ci), (dr, di) = first[q], second[p]
        real = (ar * br - ai * bi) - (cr * dr - ci * di)
        imag = (ar * bi + ai * br) - (cr * di + ci * dr)
        out.append((real, -imag))
    return out


def body(
    sizes, links, taps, active, direction, out_grad, link_grad, kernel_grad,
    ext, send_t0, send_t1, send_c, recv_x0, recv_x1, recv_t0, recv_t1, recv_c,
    mids, tap_rows, feats, feat_rows, trace_rows, small, k_rows, k_ext, g_ext, g_rows,
    code_ext, x_rows, x_mat, dressed, part, red_a, red_b, red_c, total,
    link_send, link_recv, feat_send, feat_recv, g_send, g_recv, k_send, k_recv,
    red_send, red_recv,
):
    n_space, n_tm, n_low, scale = sizes
    n_high = n_space // n_low
    my_x, my_t = lax.axis_index("space"), lax.axis_index("tm")
    low, high = lax.rem(my_x, n_low), lax.div(my_x, n_low)
    own_chunks = 8 // n_tm

    def device(sx, st):
        return (lax.rem(my_x + sx + n_space, n_space), lax.rem(my_t + st + n_tm, n_tm))

    def tm_peer(k):
        return (my_x, lax.rem(my_t + k, n_tm))

    def low_peer(k):
        return (high * n_low + lax.rem(low + k, n_low), my_t)

    def high_peer(k):
        return (lax.rem(high + k, n_high) * n_low + low, my_t)

    peers = [device(sx, st) for sx, st in NEIGHBOURS]
    peers += [tm_peer(k) for k in range(2, n_tm - 1)]
    peers += [low_peer(k) for k in range(1, n_low)]
    peers += [high_peer(k) for k in range(1, n_high)]
    barrier = pltpu.get_barrier_semaphore()
    for peer in peers:
        pl.semaphore_signal(barrier, inc=1, device_id=peer, device_id_type=MESH)

    for x in range(2):
        send_t0[:, :, :, :, x : x + 1, :] = links[:, :, 0:2, :, x, 1:2, :]
        send_t1[0:1, :, :, :, x : x + 1, :] = links[0:1, :, 0:2, :, x, 0:1, :]
        send_t1[1:3, :, :, :, x : x + 1, :] = links[2:4, :, 0:2, :, x, 0:1, :]
    send_c[0] = links[1, :, 0:2, :, 0, 1:2, :]
    send_c[1] = links[0, :, 0:2, :, 1, 0:1, :]

    pl.semaphore_wait(barrier, len(peers))

    def remote(source, target, send_sem, recv_sem, peer):
        return pltpu.make_async_remote_copy(
            src_ref=source, dst_ref=target, send_sem=send_sem, recv_sem=recv_sem,
            device_id=peer, device_id_type=MESH,
        )

    def start_all(copies):
        for copy in copies:
            copy.start()
        return copies

    def finish(copies):
        for copy in copies:
            copy.wait_recv()

    plan = (
        (links.at[:, :, 0:2, :, 1], recv_x0, (1, 0)),
        (links.at[1:4, :, 0:2, :, 0], recv_x1, (-1, 0)),
        (send_c.at[0], recv_c.at[0], (-1, 1)),
        (send_c.at[1], recv_c.at[1], (1, -1)),
        (send_t0, recv_t0, (0, 1)),
        (send_t1, recv_t1, (0, -1)),
    )
    link_copies = start_all(
        [
            remote(source, target, link_send.at[i], link_recv.at[i], device(*step))
            for i, (source, target, step) in enumerate(plan)
        ]
    )

    ext[:, :, :, :, pl.ds(row_of(1, 1), 2), :] = links[:, :, :, :, 0]
    ext[:, :, :, :, pl.ds(row_of(2, 1), 2), :] = links[:, :, :, :, 1]

    diagonal = lax.broadcasted_iota(jnp.int32, (8, 8), 0) == lax.broadcasted_iota(
        jnp.int32, (8, 8), 1
    )

    def spread_taps(j, carry):
        for dxdt in range(9):
            block = taps[dxdt * 9 + j]
            for o in range(4):
                line = jnp.broadcast_to(block[o : o + 1, :], (8, 8))
                column = jnp.sum(jnp.where(diagonal, line, 0.0), axis=1, keepdims=True)
                tap_rows[j, dxdt * 4 + o] = jnp.broadcast_to(column, (8, 128))
        return carry

    lax.fori_loop(0, 9, spread_taps, 0)

    hid = (lax.broadcasted_iota(jnp.int32, (8, 128), 0) >> 1) & 1
    course_of = jnp.concatenate([direction[0], direction[0], direction[1], direction[1]], axis=0)
    moving = jnp.concatenate([active[0], active[0], active[1], active[1]], axis=0)
    moves = moving.astype(F32)
    frozen_third = (1.0 - moves) * (1.0 / 3.0)
    chosen_of = {0: course_of == hid, 2: course_of == hid + 2}

    def stored(index):
        return (mids[index, 0], mids[index, 1])

    def store_mid(index, matrix):
        mids[index, 0] = matrix[0]
        mids[index, 1] = matrix[1]

    staples = {0: None, 2: None}

    def forward(number):
        course, across = ORDER[number]
        b, c, e = legs_above(ext, course, across)
        upper = mul(b, c, adj_second=True)
        store_mid(2 * number, upper)
        above = mul(upper, e, adj_second=True)
        a, b, e = legs_below(ext, course, across)
        lower = mul(a, b)
        store_mid(2 * number + 1, lower)
        below = mul(lower, e, adj_first=True)
        if across >= 2:
            below = rolled(below, across, -1)
        both = add(above, below)
        staples[course] = both if staples[course] is None else add(staples[course], both)

    forward(0)

    finish(link_copies)

    def fill(buffer, courses, put):
        lines = [
            [(buffer[:, 0, i, j], buffer[:, 1, i, j]) for j in range(3)] for i in range(2)
        ]
        lines.append(third_line(*lines))
        for i in range(3):
            for j in range(3):
                for k in range(2):
                    put(courses, k, i, j, lines[i][j][k])

    def put_x(ext_x):
        def put(courses, k, i, j, value):
            for n, course in enumerate(courses):
                ext[course, k, i, j, pl.ds(row_of(ext_x, 1), 2), :] = value[n]

        return put

    def put_t(ext_t):
        def put(courses, k, i, j, value):
            for n, course in enumerate(courses):
                for x in range(2):
                    ext[course, k, i, j, pl.ds(row_of(1 + x, ext_t), 1), :] = value[n, x : x + 1]

        return put

    def put_c(courses, k, i, j, value):
        ext[1, k, i, j, pl.ds(row_of(3, 0), 1), :] = value[0]
        ext[0, k, i, j, pl.ds(row_of(0, 3), 1), :] = value[1]

    fill(recv_x0, (0, 1, 2, 3), put_x(0))
    fill(recv_x1, (1, 2, 3), put_x(3))
    fill(recv_t0, (0, 1, 2, 3), put_t(0))
    fill(recv_t1, (0, 2, 3), put_t(3))
    fill(recv_c, (1, 0), put_c)

    for number in range(1, 6):
        forward(number)

    def trace(part):
        return part[0, 0] + part[1, 1] + part[2, 2]

    cores = {lead: view(ext, lead, 0, 0) for lead in (0, 2)}
    closed = {lead: mul(cores[lead], staples[lead]) for lead in (0, 2)}
    for lead in (0, 2):
        for k in range(2):
            value = trace(closed[lead][k]) * frozen_third
            trace_rows[pl.ds((2 * lead + k) * 8, 8), :] = value
            trace_rows[pl.ds((2 * lead + 2 + k) * 8, 8), :] = swap_halves(value)
    for x in range(2):
        for t in range(2):
            feats[1 + x, 1 + t] = trace_rows[pl.ds(4 * x + t, 8, 8), :]

    def edge(step):
        source = {1: pl.ds(2, 1), -1: pl.ds(1, 1), 0: pl.ds(1, 2)}[step]
        target = {1: pl.ds(0, 1), -1: pl.ds(3, 1), 0: pl.ds(1, 2)}[step]
        return source, target

    def edge_copies(ref, steps, send_sem, recv_sem):
        copies = []
        for i, (sx, st) in enumerate(steps):
            (from_x, to_x), (from_t, to_t) = edge(sx), edge(st)
            copies.append(
                remote(
                    ref.at[from_x, from_t], ref.at[to_x, to_t],
                    send_sem.at[i], recv_sem.at[i], device(sx, st),
                )
            )
        return start_all(copies)

    feat_copies = edge_copies(feats, NEIGHBOURS, feat_send, feat_recv)

    def roll_features(positions):
        for ext_x, ext_t in positions:
            value = feats[ext_x, ext_t]
            for dy in range(3):
                along_y = shift_yz(value, dy - 1, 0)
                for dz in range(3):
                    feat_rows[dy * 3 + dz, ext_x * 4 + ext_t] = shift_yz(along_y, 0, dz - 1)

    inner = [(x, t) for x in (1, 2) for t in (1, 2)]
    outer = [(x, t) for x in range(4) for t in range(4) if (x, t) not in inner]
    roll_features(inner)

    grads = {}
    for lead in (0, 2):
        grads[lead] = tuple(
            jnp.concatenate(
                [
                    out_grad[lead, k, :, :, 0],
                    out_grad[lead + 1, k, :, :, 0],
                    out_grad[lead, k, :, :, 1],
                    out_grad[lead + 1, k, :, :, 1],
                ],
                axis=2,
            )
            for k in range(2)
        )

    def choose(field):
        out = []
        for k in range(2):
            first, second = field[0][k], field[2][k]
            mask_first = jnp.broadcast_to(chosen_of[0].astype(F32), first.shape)
            mask_second = jnp.broadcast_to(chosen_of[2].astype(F32), first.shape)
            picked = first * mask_first + second * mask_second
            out.append(picked + swap_halves(picked))
        return tuple(out)

    def project(matrix):
        real, imag = matrix
        third = trace(imag) * (1.0 / 3.0)
        out = []
        for i, j in ((0, 1), (0, 2), (1, 2)):
            out.append((real[i, j] - real[j, i]) * 0.5)
            out.append((imag[i, j] + imag[j, i]) * 0.5)
        return out + [imag[0, 0] - third, imag[1, 1] - third]

    def expand(parts):
        r01, i01, r02, i02, r12, i12, d0, d1 = parts
        zero = jnp.zeros_like(d0)
        real = jnp.stack(
            [
                jnp.stack([zero, r01, r02]),
                jnp.stack([-r01, zero, r12]),
                jnp.stack([-r02, -r12, zero]),
            ]
        )
        imag = jnp.stack(
            [
                jnp.stack([d0, i01, i02]),
                jnp.stack([i01, d1, i12]),
                jnp.stack([i02, i12, -d0 - d1]),
            ]
        )
        return (real, imag)

    picked_link = choose(cores)
    generator = expand(project(choose(closed)))
    minus = scaled(generator, -1.0)
    powers = [mul(choose(grads), picked_link, adj_second=True)]
    for _ in range(4):
        powers.append(mul(minus, powers[-1]))
    series = [powers[0]]
    for k in range(3):
        series.append(add(powers[k + 1], mul(series[-1], minus)))

    def inner_product(first, second):
        total_sum = None
        for k in range(2):
            for i in range(3):
                for j in range(3):
                    term = first[k][i, j] * second[k][i, j]
                    total_sum = term if total_sum is None else total_sum + term
        return total_sum

    slopes = [inner_product(powers[k], generator) for k in range(4)]
    turns = [project(matrix) for matrix in series]

    small[0] = course_of.astype(F32)

    finish(feat_copies)
    roll_features(outer)

    def conv_step(j, acc):
        acc = list(acc)
        for dx in range(3):
            for dt in range(3):
                for o in range(4):
                    tap = tap_rows[j, (dx * 3 + dt) * 4 + o]
                    for n in range(4):
                        x, t = n // 2, n % 2
                        acc[o * 4 + n] = acc[o * 4 + n] + tap * feat_rows[j, (x + dx) * 4 + t + dt]
        return tuple(acc)

    acc = lax.fori_loop(0, 9, conv_step, tuple(jnp.zeros((8, 128), F32) for _ in range(16)))
    for n in range(4):
        s = 4 * (n // 2) + n % 2
        course_row = jnp.broadcast_to(small[0, pl.ds(s, 1), :], (8, 128))
        picked = jnp.where(course_row == 0.0, acc[n], 0.0)
        for o in range(1, 4):
            picked = picked + jnp.where(course_row == float(o), acc[o * 4 + n], 0.0)
        field_row = jnp.sum(picked, axis=0, keepdims=True)
        small[1, pl.ds(s, 1), :] = field_row
        small[1, pl.ds(s + 2, 1), :] = field_row
    bent = jnp.tanh(small[1])
    strength = bent * moves
    c1, c2, c3, c4 = slopes
    slope = c1 + strength * (c2 + strength * (c3 * 0.5 + strength * (c4 * (1.0 / 6.0))))
    field_grad = moves * (1.0 - bent * bent) * slope
    code = jnp.where(moving == 1, course_of, -1).astype(F32)
    g_ext[1, 1] = jnp.where(hid == 0, field_grad, code)
    t1, t2, t3, t4 = turns
    for k in range(8):
        poly = t1[k] + strength * (
            t2[k] * 0.5 + strength * (t3[k] * (1.0 / 6.0) + strength * (t4[k] * (1.0 / 24.0)))
        )
        k_rows[pl.ds(8 * k, 8), :] = -strength * poly
    for x in range(2):
        for t in range(2):
            k_ext[1 + x, 1 + t] = k_rows[pl.ds(4 * x + t, 8, 8), :]

    g_copies = start_all(
        [
            remote(
                g_ext.at[1, 1], g_ext.at[1 - sx, 1 - st],
                g_send.at[i], g_recv.at[i], device(sx, st),
            )
            for i, (sx, st) in enumerate(NEIGHBOURS)
        ]
    )
    k_copies = edge_copies(k_ext, FACES + CORNERS, k_send, k_recv)

    small[2] = field_grad
    sub = lax.broadcasted_iota(jnp.int32, (8, 128), 0).astype(F32)
    wide = []
    for n in range(4):
        s = 4 * (n // 2) + n % 2
        course_row = jnp.broadcast_to(small[0, pl.ds(s, 1), :], (8, 128))
        grad_row = jnp.broadcast_to(small[2, pl.ds(s, 1), :], (8, 128))
        wide.append(jnp.where(course_row == sub, grad_row, 0.0))
    wide = jnp.concatenate(wide, axis=1)

    def tap_grad(j):
        lines = []
        for dx in range(3):
            for dt in range(3):
                lines.append(
                    jnp.concatenate(
                        [
                            feat_rows[j, (n // 2 + dx) * 4 + n % 2 + dt]
                            for n in range(4)
                        ],
                        axis=1,
                    )
                )
        return lax.dot_general(
            wide, jnp.concatenate(lines, axis=0), (((1,), (1,)), ((), ())),
            precision=lax.Precision.HIGHEST, preferred_element_type=F32,
        )

    part[...] = jnp.zeros((8, 8, 128), F32)

    def tap_step(j, carry):
        part[j, :, 0:72] = tap_grad(j)
        return carry

    lax.fori_loop(0, 8, tap_step, 0)
    last = tap_grad(8)
    for o in range(4):
        part[o, 4:5, 0:72] = last[o : o + 1, :]

    red_a[my_t] = part[pl.ds(my_t * own_chunks, own_chunks)]
    base_a, base_b, base_c, base_d = 0, n_tm, n_tm + n_low, n_tm + n_low + n_high
    copies_a = []
    for k in range(1, n_tm):
        peer = tm_peer(k)
        copies_a.append(
            remote(
                part.at[pl.ds(peer[1] * own_chunks, own_chunks)], red_a.at[my_t],
                red_send.at[base_a + k], red_recv.at[base_a + k], peer,
            )
        )
    start_all(copies_a)

    decay = powers[4]
    blend = scaled(powers[4], 1.0 / 24.0)
    for k, factor in ((3, 1.0 / 6.0), (2, 0.5), (1, 1.0), (0, 1.0)):
        blend = add(scaled(blend, strength), scaled(powers[k], factor))
    straight = mul(blend, picked_link)

    finish(g_copies)

    whole = g_ext[...]
    axis = whole.ndim - 2
    mask = half_mask(whole.shape)
    values = jnp.where(mask, pltpu.roll(whole, 2, axis), whole)
    codes = jnp.where(mask, whole, pltpu.roll(whole, 6, axis))
    for pair in range(2):
        wanted = jnp.where(mask, 2.0 * pair + 1.0, 2.0 * pair)
        one = jnp.where(codes == wanted, values, 0.0)
        for dy in range(3):
            along_y = shift_yz(one, 1 - dy, 0)
            for dz in range(3):
                g_rows[dy * 3 + dz, pair] = shift_yz(along_y, 0, 1 - dz)

    spots = inner + [(0, 1), (0, 2), (3, 1), (3, 2), (1, 0), (2, 0), (1, 3), (2, 3), (3, 0), (0, 3)]

    def back_step(spot_list):
        def step(j, acc):
            acc = list(acc)
            for o in range(4):
                rows = {}
                for dx in range(3):
                    for dt in range(3):
                        tap = tap_rows[j, (dx * 3 + dt) * 4 + o]
                        for n, (ext_x, ext_t) in enumerate(spot_list):
                            px, pt = ext_x + 2 - dx, ext_t + 2 - dt
                            if (px, pt) not in rows:
                                s = 4 * (px % 2) + 2 * (o % 2) + pt % 2
                                rows[px, pt] = jnp.broadcast_to(
                                    g_rows[j, o // 2, px // 2, pt // 2, pl.ds(s, 1), :], (8, 128)
                                )
                            acc[n] = acc[n] + tap * rows[px, pt]
            return tuple(acc)

        return step

    spot_grad = lax.fori_loop(
        0, 9, back_step(spots), tuple(jnp.zeros((8, 128), F32) for _ in spots)
    )

    finish(k_copies)
    for n, (ext_x, ext_t) in enumerate(spots):
        block_x, block_t = (ext_x + 1) // 2, (ext_t + 1) // 2
        s = 4 * ((ext_x + 1) % 2) + 2 + (ext_t + 1) % 2
        code_row = g_ext[block_x, block_t, pl.ds(s, 1), :]
        code_ext[pl.ds(row_of(ext_x, ext_t), 1), :] = code_row
        merged = jnp.where(
            jnp.broadcast_to(code_row, (8, 128)) >= 0.0,
            k_ext[ext_x, ext_t],
            spot_grad[n] * (1.0 / 3.0),
        )
        x_rows[pl.ds(row_of(ext_x, ext_t), 8, GROWS), :] = merged

    for half in range(2):
        rows = pl.ds(2 + 8 * half, 8)
        code8 = code_ext[rows, :]
        parts = [x_rows[pl.ds(GROWS * k + 2 + 8 * half, 8), :] for k in range(8)]
        still = code8 < 0.0
        for course in range(4):
            turned = expand([jnp.where(code8 == float(course), p, 0.0) for p in parts])
            real, imag = turned
            one_real = jnp.where(still, parts[2 * course], 0.0)
            one_imag = jnp.where(still, parts[2 * course + 1], 0.0)
            zero = jnp.zeros_like(one_real)
            eye_real = jnp.stack(
                [jnp.stack([one_real if i == j else zero for j in range(3)]) for i in range(3)]
            )
            eye_imag = jnp.stack(
                [jnp.stack([one_imag if i == j else zero for j in range(3)]) for i in range(3)]
            )
            matrix = (real + eye_real, imag - eye_imag)
            product = mul(
                matrix, (ext[course, 0, :, :, rows, :], ext[course, 1, :, :, rows, :])
            )
            for k in range(2):
                x_mat[course, k, :, :, rows, :] = matrix[k]
                dressed[course, k, :, :, rows, :] = product[k]

    def reduce_step(copies, buffer):
        finish(copies)
        out = buffer[0]
        for k in range(1, buffer.shape[0]):
            out = out + buffer[k]
        return out

    red_b[low] = reduce_step(copies_a, red_a)
    copies_b = start_all(
        [
            remote(
                red_b.at[low], red_b.at[low],
                red_send.at[base_b + k], red_recv.at[base_b + k], low_peer(k),
            )
            for k in range(1, n_low)
        ]
    )

    link_sum = {0: None, 2: None}

    def backward(number):
        course, across = ORDER[number]
        b, c, e = legs_above(ext, course, across)
        db, dc, de = legs_above(dressed, course, across)
        upper = stored(2 * number)
        change = add(mul(db, c, adj_second=True), mul(b, dc, adj_second=True))
        above = add(mul(change, e, adj_second=True), mul(upper, de, adj_second=True))
        a, b, e = legs_below(ext, course, across)
        da, db, de = legs_below(dressed, course, across)
        lower = stored(2 * number + 1)
        change = add(mul(da, b), mul(a, db))
        below = add(mul(change, e, adj_first=True), mul(lower, de, adj_first=True))
        if across >= 2:
            below = rolled(below, across, -1)
        both = add(above, below)
        link_sum[course] = both if link_sum[course] is None else add(link_sum[course], both)

    for number in range(3):
        backward(number)

    red_c[high] = reduce_step(copies_b, red_b)
    copies_c = start_all(
        [
            remote(
                red_c.at[high], red_c.at[high],
                red_send.at[base_c + k], red_recv.at[base_c + k], high_peer(k),
            )
            for k in range(1, n_high)
        ]
    )

    for number in range(3, 6):
        backward(number)

    mine = pl.ds(my_t * own_chunks, own_chunks)
    total[mine] = reduce_step(copies_c, red_c) * scale
    copies_d = start_all(
        [
            remote(
                total.at[mine], total.at[mine],
                red_send.at[base_d + k], red_recv.at[base_d + k], tm_peer(k),
            )
            for k in range(1, n_tm)
        ]
    )

    for lead in (0, 2):
        both = add(link_sum[lead], mul(staples[lead], view(x_mat, lead, 0, 0)))
        for k in range(2):
            mask = chosen_of[lead]
            for i in range(3):
                for j in range(3):
                    value = jnp.where(mask, straight[k][i, j], grads[lead][k][i, j])
                    value = value + both[0][j, i] if k == 0 else value - both[1][j, i]
                    for x in range(2):
                        link_grad[lead, k, i, j, x] = value[4 * x : 4 * x + 2, :]
                        link_grad[lead + 1, k, i, j, x] = value[4 * x + 2 : 4 * x + 4, :]

    finish(copies_d)
    for dxdt in range(9):
        cut = slice(dxdt * 8, dxdt * 8 + 8)
        for j in range(8):
            kernel_grad[dxdt * 9 + j] = total[j, 0:4, cut]
        for o in range(4):
            kernel_grad[dxdt * 9 + 8, o : o + 1, :] = total[o, 4:5, cut]

    for copy in (
        link_copies + feat_copies + g_copies + k_copies
        + copies_a + copies_b + copies_c + copies_d
    ):
        copy.wait_send()


def shards(sizes, links, kernel, active, direction, out_grad):
    n_space, n_tm, n_low, scale = sizes
    n_high = n_space // n_low
    own_chunks = 8 // n_tm
    red_count = 2 * n_tm + n_low + n_high
    vmem = pl.BlockSpec(memory_space=pltpu.VMEM)

    def space(*shape):
        return pltpu.VMEM(shape, F32)

    def sems(count):
        return pltpu.SemaphoreType.DMA((count,))

    link_grad, kernel_grad = pl.pallas_call(
        functools.partial(body, sizes),
        out_shape=(
            jax.ShapeDtypeStruct(links.shape, F32),
            jax.ShapeDtypeStruct((81, 4, 8), F32),
        ),
        in_specs=[vmem] * 5,
        out_specs=(vmem, vmem),
        scratch_shapes=[
            space(4, 2, 3, 3, GROWS, 128),
            space(4, 2, 2, 3, 2, 128),
            space(3, 2, 2, 3, 2, 128),
            space(2, 2, 2, 3, 1, 128),
            space(4, 2, 2, 3, 2, 128),
            space(3, 2, 2, 3, 2, 128),
            space(4, 2, 2, 3, 2, 128),
            space(3, 2, 2, 3, 2, 128),
            space(2, 2, 2, 3, 1, 128),
            space(12, 2, 3, 3, 8, 128),
            space(9, 36, 8, 128),
            space(4, 4, 8, 128),
            space(9, 16, 8, 128),
            space(64, 128),
            space(3, 8, 128),
            space(64, 128),
            space(4, 4, 8, 128),
            space(3, 3, 8, 128),
            space(9, 2, 3, 3, 8, 128),
            space(GROWS, 128),
            space(8 * GROWS, 128),
            space(4, 2, 3, 3, GROWS, 128),
            space(4, 2, 3, 3, GROWS, 128),
            space(8, 8, 128),
            space(n_tm, own_chunks, 8, 128),
            space(n_low, own_chunks, 8, 128),
            space(n_high, own_chunks, 8, 128),
            space(8, 8, 128),
            sems(6), sems(6), sems(8), sems(8), sems(8), sems(8), sems(6), sems(6),
            sems(red_count), sems(red_count),
        ],
        compiler_params=pltpu.CompilerParams(
            collective_id=0, has_side_effects=True, vmem_limit_bytes=48 * 1024 * 1024
        ),
    )(links, kernel.reshape(81, 4, 8), active, direction, out_grad)
    return (link_grad, kernel_grad.reshape(kernel.shape))


def solution(mesh):
    n_space, n_tm = mesh.shape["space"], mesh.shape["tm"]
    n_low = 1 << ((n_space.bit_length() - 1) // 2)
    sites = n_space * n_tm * 4 * 128
    placed = (
        P(None, None, None, None, "space", "tm", None),
        P(),
        P("space", "tm", None),
        P("space", "tm", None),
        P(None, None, None, None, "space", "tm", None),
    )
    return jax.shard_map(
        functools.partial(shards, (n_space, n_tm, n_low, 1.0 / math.sqrt(sites))),
        mesh=mesh,
        in_specs=placed,
        out_specs=(P(None, None, None, None, "space", "tm", None), P()),
        check_vma=False,
    )
```

```python
import functools
import math

import jax
import jax.numpy as jnp
from jax import lax
from jax.experimental import pallas as pl
from jax.experimental.pallas import tpu as pltpu
from jax.sharding import PartitionSpec as P

PAIR = (1, 0, 3, 2)
MESH = pl.DeviceIdType.MESH
F32 = jnp.float32
NEIGHBOURS = tuple((sx, st) for sx in (-1, 0, 1) for st in (-1, 0, 1) if (sx, st) != (0, 0))
FACES = ((-1, 0), (1, 0), (0, -1), (0, 1))
CORNERS = ((1, -1), (-1, 1))
GROWS = 24


def row_of(ext_x, ext_t):
    return 2 + 4 * ext_x + ext_t


def lane_iota(shape):
    return lax.broadcasted_iota(jnp.int32, shape, len(shape) - 1)


def half_mask(shape):
    return ((lax.broadcasted_iota(jnp.int32, shape, len(shape) - 2) >> 1) & 1) == 1


def roll_y(values, step):
    return pltpu.roll(values, (-16 * step) % 128, values.ndim - 1)


def roll_z(values, step):
    axis = values.ndim - 1
    z_coord = lane_iota(values.shape) & 15
    if step == 1:
        return jnp.where(z_coord == 15, pltpu.roll(values, 15, axis), pltpu.roll(values, 127, axis))
    return jnp.where(z_coord == 0, pltpu.roll(values, 113, axis), pltpu.roll(values, 1, axis))


def shift_yz(values, step_y, step_z):
    if step_y:
        values = roll_y(values, step_y)
    if step_z:
        values = roll_z(values, step_z)
    return values


def swap_halves(values):
    axis = values.ndim - 2
    return jnp.where(
        half_mask(values.shape), pltpu.roll(values, 2, axis), pltpu.roll(values, 6, axis)
    )


def split_roll(values, lead, step):
    along_y = roll_y(values, step)
    along_z = roll_z(values, step)
    first, second = (along_y, along_z) if lead == 2 else (along_z, along_y)
    return jnp.where(half_mask(values.shape), second, first)


def rolled(matrix, lead, step):
    return tuple(split_roll(part, lead, step) for part in matrix)


def mul(first, second, adj_first=False, adj_second=False):
    def column(part, k):
        return jnp.expand_dims(part[k] if adj_first else part[:, k], 1)

    def line(part, k):
        return jnp.expand_dims(part[:, k] if adj_second else part[k], 0)

    sums = [None] * 4
    for k in range(3):
        fr, fi = column(first[0], k), column(first[1], k)
        sr, si = line(second[0], k), line(second[1], k)
        terms = (fr * sr, fi * si, fr * si, fi * sr)
        sums = [t if s is None else s + t for s, t in zip(sums, terms)]
    rr, ii, ri, ir = sums
    real = rr + ii if adj_first != adj_second else rr - ii
    if adj_first and adj_second:
        imag = -(ri + ir)
    elif adj_first:
        imag = ri - ir
    elif adj_second:
        imag = ir - ri
    else:
        imag = ri + ir
    return (real, imag)


def add(first, second):
    return (first[0] + second[0], first[1] + second[1])


def scaled(matrix, factor):
    return (matrix[0] * factor, matrix[1] * factor)


def view(ref, course, dx, dt):
    start = row_of(1 + dx, 1 + dt)
    pair_start = row_of(1 + dt, 1 + dx) - 2
    parts = []
    for part in range(2):
        own = ref[course, part, :, :, pl.ds(start, 8), :]
        other = ref[PAIR[course], part, :, :, pl.ds(pair_start, 8), :]
        parts.append(jnp.where(half_mask(own.shape), other, own))
    return tuple(parts)


def view_at(ref, course, lead, step):
    if lead == 0:
        return view(ref, course, step, 0)
    if lead == 1:
        return view(ref, course, 0, step)
    return rolled(view(ref, course, 0, 0), lead, step)


ORDER = ((2, 3), (0, 1), (0, 2), (0, 3), (2, 0), (2, 1))


def legs_above(ref, course, across):
    return (
        view_at(ref, across, course, 1),
        view_at(ref, course, across, 1),
        view(ref, across, 0, 0),
    )


def legs_below(ref, course, across):
    if across >= 2:
        return (
            view(ref, course, 0, 0),
            view_at(ref, across, course, 1),
            view(ref, across, 0, 0),
        )
    back = (-1, 0) if across == 0 else (0, -1)
    base = view(ref, across, *back)
    if course >= 2:
        ahead = rolled(base, course, 1)
    else:
        step = (back[0] + (course == 0), back[1] + (course == 1))
        ahead = view(ref, across, *step)
    return (view(ref, course, *back), ahead, base)


def third_line(first, second):
    out = []
    for j in range(3):
        p, q = (j + 1) % 3, (j + 2) % 3
        (ar, ai), (br, bi) = first[p], second[q]
        (cr, ci), (dr, di) = first[q], second[p]
        real = (ar * br - ai * bi) - (cr * dr - ci * di)
        imag = (ar * bi + ai * br) - (cr * di + ci * dr)
        out.append((real, -imag))
    return out


def body(
    sizes, links_in, taps_in, active_in, direction_in, out_grad_in, link_grad, kernel_grad,
    links, taps, active, direction, out_grad,
    ext, send_x0, send_x1, send_t0, send_t1, send_c, recv_x0, recv_x1, recv_t0, recv_t1, recv_c,
    mids, tap_rows, feats, feat_rows, trace_rows, small, k_rows, k_ext, g_ext, g_rows,
    code_ext, x_rows, x_mat, dressed, total, reds,
    in_sems, link_send, link_recv, feat_send, feat_recv, g_send, g_recv, k_send, k_recv,
    red_send, red_recv,
):
    n_space, n_tm, axes, scale = sizes
    n_x, n_y, n_far, n_near = axes
    n_z = n_far * n_near
    my_x, my_t = lax.axis_index("space"), lax.axis_index("tm")

    def device(sx, st):
        return (lax.rem(my_x + sx + n_space, n_space), lax.rem(my_t + st + n_tm, n_tm))

    at_core = lax.rem(my_t, 2)
    at_z = lax.rem(my_x, n_far) * n_near + lax.div(my_t, 2)
    at_y = lax.rem(lax.div(my_x, n_far), n_y)
    at_x = lax.div(my_x, n_far * n_y)

    def core_peer(k):
        return (my_x, my_t + 1 - 2 * at_core)

    def z_peer(k):
        z = lax.rem(at_z + k, n_z)
        space = lax.div(my_x, n_far) * n_far + lax.div(z, n_near)
        return (space, lax.rem(z, n_near) * 2 + at_core)

    def y_peer(k):
        y = lax.rem(at_y + k, n_y)
        return ((at_x * n_y + y) * n_far + lax.rem(my_x, n_far), my_t)

    def x_peer(k):
        return (lax.rem(at_x + k, n_x) * n_y * n_far + lax.rem(my_x, n_y * n_far), my_t)

    stages = [
        (core_peer, at_core, 2, 0),
        (z_peer, at_z, n_z, 2),
        (y_peer, at_y, n_y, 2 + n_z),
        (x_peer, at_x, n_x, 2 + n_z + n_y),
    ]
    peers = [device(sx, st) for sx, st in NEIGHBOURS]
    for peer_of, _, count, _ in stages:
        peers += [peer_of(k) for k in range(1, count)]
    barrier = pltpu.get_barrier_semaphore()
    for peer in peers:
        pl.semaphore_signal(barrier, inc=1, device_id=peer, device_id_type=MESH)

    loads = [
        pltpu.make_async_copy(source, target, in_sems.at[i])
        for i, (source, target) in enumerate(
            (
                (links_in, links), (taps_in, taps), (active_in, active),
                (direction_in, direction), (out_grad_in, out_grad),
            )
        )
    ]
    for load in loads:
        load.start()
    loads[0].wait()

    send_x0[...] = links[:, :, 0:2, :, 1]
    send_x1[...] = links[1:4, :, 0:2, :, 0]
    for x in range(2):
        send_t0[:, :, :, :, x : x + 1, :] = links[:, :, 0:2, :, x, 1:2, :]
        send_t1[0:1, :, :, :, x : x + 1, :] = links[0:1, :, 0:2, :, x, 0:1, :]
        send_t1[1:3, :, :, :, x : x + 1, :] = links[2:4, :, 0:2, :, x, 0:1, :]
    send_c[0] = links[1, :, 0:2, :, 0, 1:2, :]
    send_c[1] = links[0, :, 0:2, :, 1, 0:1, :]

    pl.semaphore_wait(barrier, len(peers))

    def remote(source, target, send_sem, recv_sem, peer):
        return pltpu.make_async_remote_copy(
            src_ref=source, dst_ref=target, send_sem=send_sem, recv_sem=recv_sem,
            device_id=peer, device_id_type=MESH,
        )

    def start_all(copies):
        for copy in copies:
            copy.start()
        return copies

    def finish(copies):
        for copy in copies:
            copy.wait_recv()

    plan = (
        (send_x0, recv_x0, (1, 0)),
        (send_x1, recv_x1, (-1, 0)),
        (send_c.at[0], recv_c.at[0], (-1, 1)),
        (send_c.at[1], recv_c.at[1], (1, -1)),
        (send_t0, recv_t0, (0, 1)),
        (send_t1, recv_t1, (0, -1)),
    )
    link_copies = start_all(
        [
            remote(source, target, link_send.at[i], link_recv.at[i], device(*step))
            for i, (source, target, step) in enumerate(plan)
        ]
    )

    ext[:, :, :, :, pl.ds(row_of(1, 1), 2), :] = links[:, :, :, :, 0]
    ext[:, :, :, :, pl.ds(row_of(2, 1), 2), :] = links[:, :, :, :, 1]

    for load in loads[1:]:
        load.wait()
    diagonal = lax.broadcasted_iota(jnp.int32, (8, 8), 0) == lax.broadcasted_iota(
        jnp.int32, (8, 8), 1
    )

    def spread_taps(j, carry):
        for dxdt in range(9):
            block = taps[dxdt * 9 + j]
            for o in range(4):
                line = jnp.broadcast_to(block[o : o + 1, :], (8, 8))
                column = jnp.sum(jnp.where(diagonal, line, 0.0), axis=1, keepdims=True)
                tap_rows[j, dxdt * 4 + o] = jnp.broadcast_to(column, (8, 128))
        return carry

    lax.fori_loop(0, 9, spread_taps, 0)

    hid = (lax.broadcasted_iota(jnp.int32, (8, 128), 0) >> 1) & 1
    course_of = jnp.concatenate([direction[0], direction[0], direction[1], direction[1]], axis=0)
    moving = jnp.concatenate([active[0], active[0], active[1], active[1]], axis=0)
    moves = moving.astype(F32)
    frozen_third = (1.0 - moves) * (1.0 / 3.0)
    chosen_of = {0: course_of == hid, 2: course_of == hid + 2}

    def stored(index):
        return (mids[index, 0], mids[index, 1])

    def store_mid(index, matrix):
        mids[index, 0] = matrix[0]
        mids[index, 1] = matrix[1]

    staples = {0: None, 2: None}

    def forward(number):
        course, across = ORDER[number]
        b, c, e = legs_above(ext, course, across)
        upper = mul(b, c, adj_second=True)
        store_mid(2 * number, upper)
        above = mul(upper, e, adj_second=True)
        a, b, e = legs_below(ext, course, across)
        lower = mul(a, b)
        store_mid(2 * number + 1, lower)
        below = mul(lower, e, adj_first=True)
        if across >= 2:
            below = rolled(below, across, -1)
        both = add(above, below)
        staples[course] = both if staples[course] is None else add(staples[course], both)

    forward(0)

    finish(link_copies)

    def fill(buffer, courses, put):
        lines = [
            [(buffer[:, 0, i, j], buffer[:, 1, i, j]) for j in range(3)] for i in range(2)
        ]
        lines.append(third_line(*lines))
        for i in range(3):
            for j in range(3):
                for k in range(2):
                    put(courses, k, i, j, lines[i][j][k])

    def put_x(ext_x):
        def put(courses, k, i, j, value):
            for n, course in enumerate(courses):
                ext[course, k, i, j, pl.ds(row_of(ext_x, 1), 2), :] = value[n]

        return put

    def put_t(ext_t):
        def put(courses, k, i, j, value):
            for n, course in enumerate(courses):
                for x in range(2):
                    ext[course, k, i, j, pl.ds(row_of(1 + x, ext_t), 1), :] = value[n, x : x + 1]

        return put

    def put_c(courses, k, i, j, value):
        ext[1, k, i, j, pl.ds(row_of(3, 0), 1), :] = value[0]
        ext[0, k, i, j, pl.ds(row_of(0, 3), 1), :] = value[1]

    fill(recv_x0, (0, 1, 2, 3), put_x(0))
    fill(recv_x1, (1, 2, 3), put_x(3))
    fill(recv_t0, (0, 1, 2, 3), put_t(0))
    fill(recv_t1, (0, 2, 3), put_t(3))
    fill(recv_c, (1, 0), put_c)

    for number in range(1, 6):
        forward(number)

    def trace(part):
        return part[0, 0] + part[1, 1] + part[2, 2]

    cores = {lead: view(ext, lead, 0, 0) for lead in (0, 2)}
    closed = {lead: mul(cores[lead], staples[lead]) for lead in (0, 2)}
    for lead in (0, 2):
        for k in range(2):
            value = trace(closed[lead][k]) * frozen_third
            trace_rows[pl.ds((2 * lead + k) * 8, 8), :] = value
            trace_rows[pl.ds((2 * lead + 2 + k) * 8, 8), :] = swap_halves(value)
    for x in range(2):
        for t in range(2):
            feats[1 + x, 1 + t] = trace_rows[pl.ds(4 * x + t, 8, 8), :]

    def edge(step):
        source = {1: pl.ds(2, 1), -1: pl.ds(1, 1), 0: pl.ds(1, 2)}[step]
        target = {1: pl.ds(0, 1), -1: pl.ds(3, 1), 0: pl.ds(1, 2)}[step]
        return source, target

    def edge_copies(ref, steps, send_sem, recv_sem):
        copies = []
        for i, (sx, st) in enumerate(steps):
            (from_x, to_x), (from_t, to_t) = edge(sx), edge(st)
            copies.append(
                remote(
                    ref.at[from_x, from_t], ref.at[to_x, to_t],
                    send_sem.at[i], recv_sem.at[i], device(sx, st),
                )
            )
        return start_all(copies)

    feat_copies = edge_copies(feats, NEIGHBOURS, feat_send, feat_recv)

    def roll_features(positions):
        for ext_x, ext_t in positions:
            value = feats[ext_x, ext_t]
            for dy in range(3):
                along_y = shift_yz(value, dy - 1, 0)
                for dz in range(3):
                    feat_rows[dy * 3 + dz, ext_x * 4 + ext_t] = shift_yz(along_y, 0, dz - 1)

    inner = [(x, t) for x in (1, 2) for t in (1, 2)]
    outer = [(x, t) for x in range(4) for t in range(4) if (x, t) not in inner]
    roll_features(inner)

    grads = {}
    for lead in (0, 2):
        grads[lead] = tuple(
            jnp.concatenate(
                [
                    out_grad[lead, k, :, :, 0],
                    out_grad[lead + 1, k, :, :, 0],
                    out_grad[lead, k, :, :, 1],
                    out_grad[lead + 1, k, :, :, 1],
                ],
                axis=2,
            )
            for k in range(2)
        )

    def choose(field):
        out = []
        for k in range(2):
            first, second = field[0][k], field[2][k]
            mask_first = jnp.broadcast_to(chosen_of[0].astype(F32), first.shape)
            mask_second = jnp.broadcast_to(chosen_of[2].astype(F32), first.shape)
            picked = first * mask_first + second * mask_second
            out.append(picked + swap_halves(picked))
        return tuple(out)

    def project(matrix):
        real, imag = matrix
        third = trace(imag) * (1.0 / 3.0)
        out = []
        for i, j in ((0, 1), (0, 2), (1, 2)):
            out.append((real[i, j] - real[j, i]) * 0.5)
            out.append((imag[i, j] + imag[j, i]) * 0.5)
        return out + [imag[0, 0] - third, imag[1, 1] - third]

    def expand(parts):
        r01, i01, r02, i02, r12, i12, d0, d1 = parts
        zero = jnp.zeros_like(d0)
        real = jnp.stack(
            [
                jnp.stack([zero, r01, r02]),
                jnp.stack([-r01, zero, r12]),
                jnp.stack([-r02, -r12, zero]),
            ]
        )
        imag = jnp.stack(
            [
                jnp.stack([d0, i01, i02]),
                jnp.stack([i01, d1, i12]),
                jnp.stack([i02, i12, -d0 - d1]),
            ]
        )
        return (real, imag)

    picked_link = choose(cores)
    generator = expand(project(choose(closed)))
    minus = scaled(generator, -1.0)
    powers = [mul(choose(grads), picked_link, adj_second=True)]
    for _ in range(4):
        powers.append(mul(minus, powers[-1]))
    series = [powers[0]]
    for k in range(3):
        series.append(add(powers[k + 1], mul(series[-1], minus)))

    def inner_product(first, second):
        total_sum = None
        for k in range(2):
            for i in range(3):
                for j in range(3):
                    term = first[k][i, j] * second[k][i, j]
                    total_sum = term if total_sum is None else total_sum + term
        return total_sum

    slopes = [inner_product(powers[k], generator) for k in range(4)]
    turns = [project(matrix) for matrix in series]

    small[0] = course_of.astype(F32)

    def conv_step(own):
        def step(j, acc):
            acc = list(acc)
            for dx in range(3):
                for dt in range(3):
                    for o in range(4):
                        tap = None
                        for n in range(4):
                            spot = (n // 2 + dx, n % 2 + dt)
                            if (spot in inner) != own:
                                continue
                            if tap is None:
                                tap = tap_rows[j, (dx * 3 + dt) * 4 + o]
                            term = tap * feat_rows[j, spot[0] * 4 + spot[1]]
                            acc[o * 4 + n] = acc[o * 4 + n] + term
            return tuple(acc)

        return step

    acc = tuple(jnp.zeros((8, 128), F32) for _ in range(16))
    acc = lax.fori_loop(0, 9, conv_step(True), acc)

    finish(feat_copies)
    roll_features(outer)

    acc = lax.fori_loop(0, 9, conv_step(False), acc)
    for n in range(4):
        s = 4 * (n // 2) + n % 2
        course_row = jnp.broadcast_to(small[0, pl.ds(s, 1), :], (8, 128))
        picked = jnp.where(course_row == 0.0, acc[n], 0.0)
        for o in range(1, 4):
            picked = picked + jnp.where(course_row == float(o), acc[o * 4 + n], 0.0)
        field_row = jnp.sum(picked, axis=0, keepdims=True)
        small[1, pl.ds(s, 1), :] = field_row
        small[1, pl.ds(s + 2, 1), :] = field_row
    bent = jnp.tanh(small[1])
    strength = bent * moves
    c1, c2, c3, c4 = slopes
    slope = c1 + strength * (c2 + strength * (c3 * 0.5 + strength * (c4 * (1.0 / 6.0))))
    field_grad = moves * (1.0 - bent * bent) * slope
    code = jnp.where(moving == 1, course_of, -1).astype(F32)
    g_ext[1, 1] = jnp.where(hid == 0, field_grad, code)
    t1, t2, t3, t4 = turns
    for k in range(8):
        poly = t1[k] + strength * (
            t2[k] * 0.5 + strength * (t3[k] * (1.0 / 6.0) + strength * (t4[k] * (1.0 / 24.0)))
        )
        k_rows[pl.ds(8 * k, 8), :] = -strength * poly
    for x in range(2):
        for t in range(2):
            k_ext[1 + x, 1 + t] = k_rows[pl.ds(4 * x + t, 8, 8), :]

    g_copies = start_all(
        [
            remote(
                g_ext.at[1, 1], g_ext.at[1 - sx, 1 - st],
                g_send.at[i], g_recv.at[i], device(sx, st),
            )
            for i, (sx, st) in enumerate(NEIGHBOURS)
        ]
    )
    k_copies = edge_copies(k_ext, FACES + CORNERS, k_send, k_recv)

    sub = lax.broadcasted_iota(jnp.int32, (8, 128), 0).astype(F32)
    rough = field_grad.astype(jnp.bfloat16).astype(F32)
    small[2] = rough
    small[1] = field_grad - rough
    wide = []
    for n in range(4):
        s = 4 * (n // 2) + n % 2
        course_row = jnp.broadcast_to(small[0, pl.ds(s, 1), :], (8, 128))
        rough_row = jnp.broadcast_to(small[2, pl.ds(s, 1), :], (8, 128))
        rest_row = jnp.broadcast_to(small[1, pl.ds(s, 1), :], (8, 128))
        wide.append(
            jnp.where(course_row == sub, rough_row, 0.0)
            + jnp.where(course_row + 4.0 == sub, rest_row, 0.0)
        )
    wide = jnp.concatenate(wide, axis=1).astype(jnp.bfloat16)
    lines = []
    for dx in range(3):
        for dt in range(3):
            for j in range(9):
                lines.append(
                    jnp.concatenate(
                        [feat_rows[j, (n // 2 + dx) * 4 + n % 2 + dt] for n in range(4)], axis=1
                    )
                )
    lines = jnp.concatenate(lines + [jnp.zeros((8, 512), F32)], axis=0)
    lines_high = lines.astype(jnp.bfloat16)
    lines_low = (lines - lines_high.astype(F32)).astype(jnp.bfloat16)
    contract = (((1,), (1,)), ((), ()))
    high_sum = lax.dot_general(wide, lines_high, contract, preferred_element_type=F32)
    low_sum = lax.dot_general(wide, lines_low, contract, preferred_element_type=F32)
    tap_sum = high_sum[0:4] + (high_sum[4:8] + low_sum[0:4])
    total[...] = jnp.zeros((4, 768), F32)
    total[:, 0:656] = tap_sum

    def send_stage(number, value):
        peer_of, place, count, base = stages[number]
        buffer = reds[number]
        buffer[place] = value
        return start_all(
            [
                remote(
                    buffer.at[place], buffer.at[place],
                    red_send.at[base + k], red_recv.at[base + k], peer_of(k),
                )
                for k in range(1, count)
            ]
        )

    def take_stage(number, copies):
        finish(copies)
        buffer = reds[number]
        out = buffer[0]
        for k in range(1, stages[number][2]):
            out = out + buffer[k]
        return out

    copies_a = send_stage(0, total[...])

    blend = scaled(powers[4], 1.0 / 24.0)
    for k, factor in ((3, 1.0 / 6.0), (2, 0.5), (1, 1.0), (0, 1.0)):
        blend = add(scaled(blend, strength), scaled(powers[k], factor))
    straight = mul(blend, picked_link)

    def spread_blocks(blocks, places):
        mask = half_mask(blocks.shape)
        axis = blocks.ndim - 2
        values = jnp.where(mask, pltpu.roll(blocks, 2, axis), blocks)
        codes = jnp.where(mask, blocks, pltpu.roll(blocks, 6, axis))
        for pair in range(2):
            wanted = jnp.where(mask, 2.0 * pair + 1.0, 2.0 * pair)
            one = jnp.where(codes == wanted, values, 0.0)
            for dy in range(3):
                along_y = shift_yz(one, 1 - dy, 0)
                for dz in range(3):
                    moved = shift_yz(along_y, 0, 1 - dz)
                    for n, (bx, bt) in enumerate(places):
                        g_rows[dy * 3 + dz, pair, bx, bt] = moved[n]

    spots = inner + [(0, 1), (0, 2), (3, 1), (3, 2), (1, 0), (2, 0), (1, 3), (2, 3), (3, 0), (0, 3)]

    def back_step(own):
        def step(j, acc):
            acc = list(acc)
            for o in range(4):
                rows = {}
                for dx in range(3):
                    for dt in range(3):
                        tap = None
                        for n, (ext_x, ext_t) in enumerate(spots):
                            px, pt = ext_x + 2 - dx, ext_t + 2 - dt
                            if (px // 2 == 1 and pt // 2 == 1) != own:
                                continue
                            if tap is None:
                                tap = tap_rows[j, (dx * 3 + dt) * 4 + o]
                            if (px, pt) not in rows:
                                s = 4 * (px % 2) + 2 * (o % 2) + pt % 2
                                rows[px, pt] = jnp.broadcast_to(
                                    g_rows[j, o // 2, px // 2, pt // 2, pl.ds(s, 1), :], (8, 128)
                                )
                            acc[n] = acc[n] + tap * rows[px, pt]
            return tuple(acc)

        return step

    around = [(bx, bt) for bx in range(3) for bt in range(3) if (bx, bt) != (1, 1)]
    spread_blocks(g_ext[1, 1:2], [(1, 1)])
    spot_grad = tuple(jnp.zeros((8, 128), F32) for _ in spots)
    spot_grad = lax.fori_loop(0, 9, back_step(True), spot_grad)

    copies_b = send_stage(1, take_stage(0, copies_a))

    finish(g_copies)
    spread_blocks(jnp.stack([g_ext[bx, bt] for bx, bt in around]), around)
    spot_grad = lax.fori_loop(0, 9, back_step(False), spot_grad)

    finish(k_copies)
    for n, (ext_x, ext_t) in enumerate(spots):
        block_x, block_t = (ext_x + 1) // 2, (ext_t + 1) // 2
        s = 4 * ((ext_x + 1) % 2) + 2 + (ext_t + 1) % 2
        code_row = g_ext[block_x, block_t, pl.ds(s, 1), :]
        code_ext[pl.ds(row_of(ext_x, ext_t), 1), :] = code_row
        merged = jnp.where(
            jnp.broadcast_to(code_row, (8, 128)) >= 0.0,
            k_ext[ext_x, ext_t],
            spot_grad[n] * (1.0 / 3.0),
        )
        x_rows[pl.ds(row_of(ext_x, ext_t), 8, GROWS), :] = merged

    for half in range(2):
        rows = pl.ds(2 + 8 * half, 8)
        code8 = code_ext[rows, :]
        parts = [x_rows[pl.ds(GROWS * k + 2 + 8 * half, 8), :] for k in range(8)]
        still = code8 < 0.0
        for course in range(4):
            turned = expand([jnp.where(code8 == float(course), p, 0.0) for p in parts])
            real, imag = turned
            one_real = jnp.where(still, parts[2 * course], 0.0)
            one_imag = jnp.where(still, parts[2 * course + 1], 0.0)
            zero = jnp.zeros_like(one_real)
            eye_real = jnp.stack(
                [jnp.stack([one_real if i == j else zero for j in range(3)]) for i in range(3)]
            )
            eye_imag = jnp.stack(
                [jnp.stack([one_imag if i == j else zero for j in range(3)]) for i in range(3)]
            )
            matrix = (real + eye_real, imag - eye_imag)
            product = mul(
                matrix, (ext[course, 0, :, :, rows, :], ext[course, 1, :, :, rows, :])
            )
            for k in range(2):
                x_mat[course, k, :, :, rows, :] = matrix[k]
                dressed[course, k, :, :, rows, :] = product[k]

    link_sum = {0: None, 2: None}

    def backward(number):
        course, across = ORDER[number]
        b, c, e = legs_above(ext, course, across)
        db, dc, de = legs_above(dressed, course, across)
        upper = stored(2 * number)
        change = add(mul(db, c, adj_second=True), mul(b, dc, adj_second=True))
        above = add(mul(change, e, adj_second=True), mul(upper, de, adj_second=True))
        a, b, e = legs_below(ext, course, across)
        da, db, de = legs_below(dressed, course, across)
        lower = stored(2 * number + 1)
        change = add(mul(da, b), mul(a, db))
        below = add(mul(change, e, adj_first=True), mul(lower, de, adj_first=True))
        if across >= 2:
            below = rolled(below, across, -1)
        both = add(above, below)
        link_sum[course] = both if link_sum[course] is None else add(link_sum[course], both)

    for number in range(4):
        backward(number)

    copies_c = send_stage(2, take_stage(1, copies_b))

    for number in range(4, 6):
        backward(number)

    for lead in (0, 2):
        both = add(link_sum[lead], mul(staples[lead], view(x_mat, lead, 0, 0)))
        for k in range(2):
            mask = chosen_of[lead]
            for i in range(3):
                for j in range(3):
                    value = jnp.where(mask, straight[k][i, j], grads[lead][k][i, j])
                    value = value + both[0][j, i] if k == 0 else value - both[1][j, i]
                    for x in range(2):
                        link_grad[lead, k, i, j, x] = value[4 * x : 4 * x + 2, :]
                        link_grad[lead + 1, k, i, j, x] = value[4 * x + 2 : 4 * x + 4, :]

    copies_d = send_stage(3, take_stage(2, copies_c))
    total[...] = take_stage(3, copies_d) * scale
    for d in range(81):
        kernel_grad[d] = total[:, d * 8 : d * 8 + 8]

    for copy in (
        link_copies + feat_copies + g_copies + k_copies
        + copies_a + copies_b + copies_c + copies_d
    ):
        copy.wait_send()


def shards(sizes, links, kernel, active, direction, out_grad):
    n_x, n_y, n_far, n_near = sizes[2]
    counts = (2, n_far * n_near, n_y, n_x)
    vmem = pl.BlockSpec(memory_space=pltpu.VMEM)

    def space(*shape):
        return pltpu.VMEM(shape, F32)

    def sems(count):
        return pltpu.SemaphoreType.DMA((count,))

    link_grad, kernel_grad = pl.pallas_call(
        functools.partial(body, sizes),
        out_shape=(
            jax.ShapeDtypeStruct(links.shape, F32),
            jax.ShapeDtypeStruct((81, 4, 8), F32),
        ),
        in_specs=[pl.BlockSpec(memory_space=pltpu.HBM)] * 5,
        out_specs=(vmem, vmem),
        scratch_shapes=[
            space(4, 2, 3, 3, 2, 2, 128),
            space(81, 4, 8),
            pltpu.VMEM((2, 2, 128), jnp.int32),
            pltpu.VMEM((2, 2, 128), jnp.int32),
            space(4, 2, 3, 3, 2, 2, 128),
            space(4, 2, 3, 3, GROWS, 128),
            space(4, 2, 2, 3, 2, 128),
            space(3, 2, 2, 3, 2, 128),
            space(4, 2, 2, 3, 2, 128),
            space(3, 2, 2, 3, 2, 128),
            space(2, 2, 2, 3, 1, 128),
            space(4, 2, 2, 3, 2, 128),
            space(3, 2, 2, 3, 2, 128),
            space(4, 2, 2, 3, 2, 128),
            space(3, 2, 2, 3, 2, 128),
            space(2, 2, 2, 3, 1, 128),
            space(12, 2, 3, 3, 8, 128),
            space(9, 36, 8, 128),
            space(4, 4, 8, 128),
            space(9, 16, 8, 128),
            space(64, 128),
            space(3, 8, 128),
            space(64, 128),
            space(4, 4, 8, 128),
            space(3, 3, 8, 128),
            space(9, 2, 3, 3, 8, 128),
            space(GROWS, 128),
            space(8 * GROWS, 128),
            space(4, 2, 3, 3, GROWS, 128),
            space(4, 2, 3, 3, GROWS, 128),
            space(4, 768),
            [space(count, 4, 768) for count in counts],
            sems(5),
            sems(6), sems(6), sems(8), sems(8), sems(8), sems(8), sems(6), sems(6),
            sems(sum(counts)), sems(sum(counts)),
        ],
        compiler_params=pltpu.CompilerParams(
            collective_id=0, has_side_effects=True, vmem_limit_bytes=60 * 1024 * 1024
        ),
    )(links, kernel.reshape(81, 4, 8), active, direction, out_grad)
    return (link_grad, kernel_grad.reshape(kernel.shape))


def solution(mesh):
    n_space, n_tm = mesh.shape["space"], mesh.shape["tm"]
    n_far = 2
    n_x = max(1, n_space // (8 * n_far))
    axes = (n_x, n_space // (n_x * n_far), n_far, n_tm // 2)
    sites = n_space * n_tm * 4 * 128
    placed = (
        P(None, None, None, None, "space", "tm", None),
        P(),
        P("space", "tm", None),
        P("space", "tm", None),
        P(None, None, None, None, "space", "tm", None),
    )
    return jax.shard_map(
        functools.partial(shards, (n_space, n_tm, axes, 1.0 / math.sqrt(sites))),
        mesh=mesh,
        in_specs=placed,
        out_specs=(P(None, None, None, None, "space", "tm", None), P()),
        check_vma=False,
    )
```

```python
import functools
import math

import jax
import jax.numpy as jnp
from jax import lax
from jax.experimental import pallas as pl
from jax.experimental.pallas import tpu as pltpu
from jax.sharding import PartitionSpec as P

PAIR = (1, 0, 3, 2)
MESH = pl.DeviceIdType.MESH
F32 = jnp.float32
NEIGHBOURS = tuple((sx, st) for sx in (-1, 0, 1) for st in (-1, 0, 1) if (sx, st) != (0, 0))
FACES = ((-1, 0), (1, 0), (0, -1), (0, 1))
CORNERS = ((1, -1), (-1, 1))
GROWS = 24


def row_of(ext_x, ext_t):
    return 2 + 4 * ext_x + ext_t


def lane_iota(shape):
    return lax.broadcasted_iota(jnp.int32, shape, len(shape) - 1)


def half_mask(shape):
    return ((lax.broadcasted_iota(jnp.int32, shape, len(shape) - 2) >> 1) & 1) == 1


def roll_y(values, step):
    return pltpu.roll(values, (-16 * step) % 128, values.ndim - 1)


def roll_z(values, step):
    axis = values.ndim - 1
    z_coord = lane_iota(values.shape) & 15
    if step == 1:
        return jnp.where(z_coord == 15, pltpu.roll(values, 15, axis), pltpu.roll(values, 127, axis))
    return jnp.where(z_coord == 0, pltpu.roll(values, 113, axis), pltpu.roll(values, 1, axis))


def shift_yz(values, step_y, step_z):
    if step_y:
        values = roll_y(values, step_y)
    if step_z:
        values = roll_z(values, step_z)
    return values


def swap_halves(values):
    axis = values.ndim - 2
    return jnp.where(
        half_mask(values.shape), pltpu.roll(values, 2, axis), pltpu.roll(values, 6, axis)
    )


def split_roll(values, lead, step):
    along_y = roll_y(values, step)
    along_z = roll_z(values, step)
    first, second = (along_y, along_z) if lead == 2 else (along_z, along_y)
    return jnp.where(half_mask(values.shape), second, first)


def rolled(matrix, lead, step):
    return tuple(split_roll(part, lead, step) for part in matrix)


def mul(first, second, adj_first=False, adj_second=False):
    def column(part, k):
        return jnp.expand_dims(part[k] if adj_first else part[:, k], 1)

    def line(part, k):
        return jnp.expand_dims(part[:, k] if adj_second else part[k], 0)

    sums = [None] * 4
    for k in range(3):
        fr, fi = column(first[0], k), column(first[1], k)
        sr, si = line(second[0], k), line(second[1], k)
        terms = (fr * sr, fi * si, fr * si, fi * sr)
        sums = [t if s is None else s + t for s, t in zip(sums, terms)]
    rr, ii, ri, ir = sums
    real = rr + ii if adj_first != adj_second else rr - ii
    if adj_first and adj_second:
        imag = -(ri + ir)
    elif adj_first:
        imag = ri - ir
    elif adj_second:
        imag = ir - ri
    else:
        imag = ri + ir
    return (real, imag)


def add(first, second):
    return (first[0] + second[0], first[1] + second[1])


def scaled(matrix, factor):
    return (matrix[0] * factor, matrix[1] * factor)


def view(ref, course, dx, dt):
    start = row_of(1 + dx, 1 + dt)
    pair_start = row_of(1 + dt, 1 + dx) - 2
    parts = []
    for part in range(2):
        own = ref[course, part, :, :, pl.ds(start, 8), :]
        other = ref[PAIR[course], part, :, :, pl.ds(pair_start, 8), :]
        parts.append(jnp.where(half_mask(own.shape), other, own))
    return tuple(parts)


def view_at(ref, course, lead, step):
    if lead == 0:
        return view(ref, course, step, 0)
    if lead == 1:
        return view(ref, course, 0, step)
    return rolled(view(ref, course, 0, 0), lead, step)


ORDER = ((2, 3), (0, 1), (0, 2), (0, 3), (2, 0), (2, 1))


def legs_above(ref, course, across):
    return (
        view_at(ref, across, course, 1),
        view_at(ref, course, across, 1),
        view(ref, across, 0, 0),
    )


def legs_below(ref, course, across):
    if across >= 2:
        return (
            view(ref, course, 0, 0),
            view_at(ref, across, course, 1),
            view(ref, across, 0, 0),
        )
    back = (-1, 0) if across == 0 else (0, -1)
    base = view(ref, across, *back)
    if course >= 2:
        ahead = rolled(base, course, 1)
    else:
        step = (back[0] + (course == 0), back[1] + (course == 1))
        ahead = view(ref, across, *step)
    return (view(ref, course, *back), ahead, base)


def third_line(first, second):
    out = []
    for j in range(3):
        p, q = (j + 1) % 3, (j + 2) % 3
        (ar, ai), (br, bi) = first[p], second[q]
        (cr, ci), (dr, di) = first[q], second[p]
        real = (ar * br - ai * bi) - (cr * dr - ci * di)
        imag = (ar * bi + ai * br) - (cr * di + ci * dr)
        out.append((real, -imag))
    return out


def body(
    sizes, links_in, taps_in, active_in, direction_in, out_grad_in, link_grad, kernel_grad,
    links, taps, active, direction, out_grad, grad_out, tap_out,
    ext, send_x0, send_x1, send_t0, send_t1, send_c, recv_x0, recv_x1, recv_t0, recv_t1, recv_c,
    mids, tap_rows, feats, feat_rows, trace_rows, small, k_rows, k_ext, g_ext, g_rows,
    code_ext, x_rows, x_mat, dressed, total, reds,
    in_sems, link_send, link_recv, feat_send, feat_recv, g_send, g_recv, k_send, k_recv,
    red_send, red_recv,
):
    n_space, n_tm, axes, scale = sizes
    n_x, n_y, n_far, n_near = axes
    n_z = n_far * n_near
    my_x, my_t = lax.axis_index("space"), lax.axis_index("tm")

    def device(sx, st):
        return (lax.rem(my_x + sx + n_space, n_space), lax.rem(my_t + st + n_tm, n_tm))

    at_core = lax.rem(my_t, 2)
    at_z = lax.rem(my_x, n_far) * n_near + lax.div(my_t, 2)
    at_y = lax.rem(lax.div(my_x, n_far), n_y)
    at_x = lax.div(my_x, n_far * n_y)

    def z_peer(k):
        z = lax.rem(at_z + k, n_z)
        space = lax.div(my_x, n_far) * n_far + lax.div(z, n_near)
        return (space, lax.rem(z, n_near) * 2 + at_core)

    def y_peer(k):
        y = lax.rem(at_y + k, n_y)
        return ((at_x * n_y + y) * n_far + lax.rem(my_x, n_far), my_t)

    def x_peer(k):
        place = lax.rem(at_x * 2 + at_core + k, 2 * n_x)
        space = lax.div(place, 2) * n_y * n_far + lax.rem(my_x, n_y * n_far)
        return (space, my_t - at_core + lax.rem(place, 2))

    along_z = (z_peer, at_z, n_z)
    along_y = (y_peer, at_y, n_y)
    along_x = (x_peer, at_x * 2 + at_core, 2 * n_x)
    stages = []
    base = 0
    for half in ((along_z, along_y, along_x), (along_y, along_z, along_x)):
        for peer_of, place, count in half:
            stages.append((peer_of, place, count, base))
            base += count
    peers = [device(sx, st) for sx, st in NEIGHBOURS]
    for peer_of, _, count in (along_z, along_y, along_x):
        peers += [peer_of(k) for k in range(1, count)]
    barrier = pltpu.get_barrier_semaphore()
    for peer in peers:
        pl.semaphore_signal(barrier, inc=1, device_id=peer, device_id_type=MESH)

    loads = [
        pltpu.make_async_copy(source, target, in_sems.at[i])
        for i, (source, target) in enumerate(
            (
                (links_in, links), (taps_in, taps), (active_in, active),
                (direction_in, direction), (out_grad_in, out_grad),
            )
        )
    ]
    for load in loads:
        load.start()
    loads[0].wait()

    send_x0[...] = links[:, :, 0:2, :, 1]
    send_x1[...] = links[1:4, :, 0:2, :, 0]
    for x in range(2):
        send_t0[:, :, :, :, x : x + 1, :] = links[:, :, 0:2, :, x, 1:2, :]
        send_t1[0:1, :, :, :, x : x + 1, :] = links[0:1, :, 0:2, :, x, 0:1, :]
        send_t1[1:3, :, :, :, x : x + 1, :] = links[2:4, :, 0:2, :, x, 0:1, :]
    send_c[0] = links[1, :, 0:2, :, 0, 1:2, :]
    send_c[1] = links[0, :, 0:2, :, 1, 0:1, :]

    pl.semaphore_wait(barrier, len(peers))

    def remote(source, target, send_sem, recv_sem, peer):
        return pltpu.make_async_remote_copy(
            src_ref=source, dst_ref=target, send_sem=send_sem, recv_sem=recv_sem,
            device_id=peer, device_id_type=MESH,
        )

    def start_all(copies):
        for copy in copies:
            copy.start()
        return copies

    def finish(copies):
        for copy in copies:
            copy.wait_recv()

    plan = (
        (send_x0, recv_x0, (1, 0)),
        (send_x1, recv_x1, (-1, 0)),
        (send_c.at[0], recv_c.at[0], (-1, 1)),
        (send_c.at[1], recv_c.at[1], (1, -1)),
        (send_t0, recv_t0, (0, 1)),
        (send_t1, recv_t1, (0, -1)),
    )
    link_copies = start_all(
        [
            remote(source, target, link_send.at[i], link_recv.at[i], device(*step))
            for i, (source, target, step) in enumerate(plan)
        ]
    )

    ext[:, :, :, :, pl.ds(row_of(1, 1), 2), :] = links[:, :, :, :, 0]
    ext[:, :, :, :, pl.ds(row_of(2, 1), 2), :] = links[:, :, :, :, 1]

    for load in loads[1:]:
        load.wait()
    diagonal = lax.broadcasted_iota(jnp.int32, (8, 8), 0) == lax.broadcasted_iota(
        jnp.int32, (8, 8), 1
    )

    def spread_taps(j, carry):
        for dxdt in range(9):
            block = taps[dxdt * 9 + j]
            for o in range(4):
                line = jnp.broadcast_to(block[o : o + 1, :], (8, 8))
                column = jnp.sum(jnp.where(diagonal, line, 0.0), axis=1, keepdims=True)
                tap_rows[j, dxdt * 4 + o] = jnp.broadcast_to(column, (8, 128))
        return carry

    lax.fori_loop(0, 9, spread_taps, 0)

    hid = (lax.broadcasted_iota(jnp.int32, (8, 128), 0) >> 1) & 1
    course_of = jnp.concatenate([direction[0], direction[0], direction[1], direction[1]], axis=0)
    moving = jnp.concatenate([active[0], active[0], active[1], active[1]], axis=0)
    moves = moving.astype(F32)
    frozen_third = (1.0 - moves) * (1.0 / 3.0)
    chosen_of = {0: course_of == hid, 2: course_of == hid + 2}

    def stored(index):
        return (mids[index, 0], mids[index, 1])

    def store_mid(index, matrix):
        mids[index, 0] = matrix[0]
        mids[index, 1] = matrix[1]

    staples = {0: None, 2: None}

    def forward(number):
        course, across = ORDER[number]
        b, c, e = legs_above(ext, course, across)
        upper = mul(b, c, adj_second=True)
        store_mid(2 * number, upper)
        above = mul(upper, e, adj_second=True)
        a, b, e = legs_below(ext, course, across)
        lower = mul(a, b)
        store_mid(2 * number + 1, lower)
        below = mul(lower, e, adj_first=True)
        if across >= 2:
            below = rolled(below, across, -1)
        both = add(above, below)
        staples[course] = both if staples[course] is None else add(staples[course], both)

    forward(0)

    finish(link_copies)

    def fill(buffer, courses, put):
        lines = [
            [(buffer[:, 0, i, j], buffer[:, 1, i, j]) for j in range(3)] for i in range(2)
        ]
        lines.append(third_line(*lines))
        for i in range(3):
            for j in range(3):
                for k in range(2):
                    put(courses, k, i, j, lines[i][j][k])

    def put_x(ext_x):
        def put(courses, k, i, j, value):
            for n, course in enumerate(courses):
                ext[course, k, i, j, pl.ds(row_of(ext_x, 1), 2), :] = value[n]

        return put

    def put_t(ext_t):
        def put(courses, k, i, j, value):
            for n, course in enumerate(courses):
                for x in range(2):
                    ext[course, k, i, j, pl.ds(row_of(1 + x, ext_t), 1), :] = value[n, x : x + 1]

        return put

    def put_c(courses, k, i, j, value):
        ext[1, k, i, j, pl.ds(row_of(3, 0), 1), :] = value[0]
        ext[0, k, i, j, pl.ds(row_of(0, 3), 1), :] = value[1]

    fill(recv_x0, (0, 1, 2, 3), put_x(0))
    fill(recv_x1, (1, 2, 3), put_x(3))
    fill(recv_t0, (0, 1, 2, 3), put_t(0))
    fill(recv_t1, (0, 2, 3), put_t(3))
    fill(recv_c, (1, 0), put_c)

    for number in range(1, 6):
        forward(number)

    def trace(part):
        return part[0, 0] + part[1, 1] + part[2, 2]

    cores = {lead: view(ext, lead, 0, 0) for lead in (0, 2)}
    closed = {lead: mul(cores[lead], staples[lead]) for lead in (0, 2)}
    for lead in (0, 2):
        for k in range(2):
            value = trace(closed[lead][k]) * frozen_third
            trace_rows[pl.ds((2 * lead + k) * 8, 8), :] = value
            trace_rows[pl.ds((2 * lead + 2 + k) * 8, 8), :] = swap_halves(value)
    for x in range(2):
        for t in range(2):
            feats[1 + x, 1 + t] = trace_rows[pl.ds(4 * x + t, 8, 8), :]

    def edge(step):
        source = {1: pl.ds(2, 1), -1: pl.ds(1, 1), 0: pl.ds(1, 2)}[step]
        target = {1: pl.ds(0, 1), -1: pl.ds(3, 1), 0: pl.ds(1, 2)}[step]
        return source, target

    def edge_copies(ref, steps, send_sem, recv_sem):
        copies = []
        for i, (sx, st) in enumerate(steps):
            (from_x, to_x), (from_t, to_t) = edge(sx), edge(st)
            copies.append(
                remote(
                    ref.at[from_x, from_t], ref.at[to_x, to_t],
                    send_sem.at[i], recv_sem.at[i], device(sx, st),
                )
            )
        return start_all(copies)

    feat_copies = edge_copies(feats, NEIGHBOURS, feat_send, feat_recv)

    def roll_features(positions):
        for ext_x, ext_t in positions:
            value = feats[ext_x, ext_t]
            for dy in range(3):
                along_y = shift_yz(value, dy - 1, 0)
                for dz in range(3):
                    feat_rows[dy * 3 + dz, ext_x * 4 + ext_t] = shift_yz(along_y, 0, dz - 1)

    inner = [(x, t) for x in (1, 2) for t in (1, 2)]
    outer = [(x, t) for x in range(4) for t in range(4) if (x, t) not in inner]
    roll_features(inner)

    grads = {}
    for lead in (0, 2):
        grads[lead] = tuple(
            jnp.concatenate(
                [
                    out_grad[lead, k, :, :, 0],
                    out_grad[lead + 1, k, :, :, 0],
                    out_grad[lead, k, :, :, 1],
                    out_grad[lead + 1, k, :, :, 1],
                ],
                axis=2,
            )
            for k in range(2)
        )

    def choose(field):
        out = []
        for k in range(2):
            first, second = field[0][k], field[2][k]
            mask_first = jnp.broadcast_to(chosen_of[0].astype(F32), first.shape)
            mask_second = jnp.broadcast_to(chosen_of[2].astype(F32), first.shape)
            picked = first * mask_first + second * mask_second
            out.append(picked + swap_halves(picked))
        return tuple(out)

    def project(matrix):
        real, imag = matrix
        third = trace(imag) * (1.0 / 3.0)
        out = []
        for i, j in ((0, 1), (0, 2), (1, 2)):
            out.append((real[i, j] - real[j, i]) * 0.5)
            out.append((imag[i, j] + imag[j, i]) * 0.5)
        return out + [imag[0, 0] - third, imag[1, 1] - third]

    def expand(parts):
        r01, i01, r02, i02, r12, i12, d0, d1 = parts
        zero = jnp.zeros_like(d0)
        real = jnp.stack(
            [
                jnp.stack([zero, r01, r02]),
                jnp.stack([-r01, zero, r12]),
                jnp.stack([-r02, -r12, zero]),
            ]
        )
        imag = jnp.stack(
            [
                jnp.stack([d0, i01, i02]),
                jnp.stack([i01, d1, i12]),
                jnp.stack([i02, i12, -d0 - d1]),
            ]
        )
        return (real, imag)

    picked_link = choose(cores)
    generator = expand(project(choose(closed)))
    minus = scaled(generator, -1.0)
    powers = [mul(choose(grads), picked_link, adj_second=True)]
    for _ in range(4):
        powers.append(mul(minus, powers[-1]))
    series = [powers[0]]
    for k in range(3):
        series.append(add(powers[k + 1], mul(series[-1], minus)))

    def inner_product(first, second):
        total_sum = None
        for k in range(2):
            for i in range(3):
                for j in range(3):
                    term = first[k][i, j] * second[k][i, j]
                    total_sum = term if total_sum is None else total_sum + term
        return total_sum

    slopes = [inner_product(powers[k], generator) for k in range(4)]
    turns = [project(matrix) for matrix in series]

    small[0] = course_of.astype(F32)

    def conv_step(own):
        def step(j, acc):
            acc = list(acc)
            for dx in range(3):
                for dt in range(3):
                    for o in range(4):
                        tap = None
                        for n in range(4):
                            spot = (n // 2 + dx, n % 2 + dt)
                            if (spot in inner) != own:
                                continue
                            if tap is None:
                                tap = tap_rows[j, (dx * 3 + dt) * 4 + o]
                            term = tap * feat_rows[j, spot[0] * 4 + spot[1]]
                            acc[o * 4 + n] = acc[o * 4 + n] + term
            return tuple(acc)

        return step

    acc = tuple(jnp.zeros((8, 128), F32) for _ in range(16))
    acc = lax.fori_loop(0, 9, conv_step(True), acc)

    finish(feat_copies)
    roll_features(outer)

    acc = lax.fori_loop(0, 9, conv_step(False), acc)
    for n in range(4):
        s = 4 * (n // 2) + n % 2
        course_row = jnp.broadcast_to(small[0, pl.ds(s, 1), :], (8, 128))
        picked = jnp.where(course_row == 0.0, acc[n], 0.0)
        for o in range(1, 4):
            picked = picked + jnp.where(course_row == float(o), acc[o * 4 + n], 0.0)
        field_row = jnp.sum(picked, axis=0, keepdims=True)
        small[1, pl.ds(s, 1), :] = field_row
        small[1, pl.ds(s + 2, 1), :] = field_row
    bent = jnp.tanh(small[1])
    strength = bent * moves
    c1, c2, c3, c4 = slopes
    slope = c1 + strength * (c2 + strength * (c3 * 0.5 + strength * (c4 * (1.0 / 6.0))))
    field_grad = moves * (1.0 - bent * bent) * slope
    code = jnp.where(moving == 1, course_of, -1).astype(F32)
    g_ext[1, 1] = jnp.where(hid == 0, field_grad, code)
    t1, t2, t3, t4 = turns
    for k in range(8):
        poly = t1[k] + strength * (
            t2[k] * 0.5 + strength * (t3[k] * (1.0 / 6.0) + strength * (t4[k] * (1.0 / 24.0)))
        )
        k_rows[pl.ds(8 * k, 8), :] = -strength * poly
    for x in range(2):
        for t in range(2):
            k_ext[1 + x, 1 + t] = k_rows[pl.ds(4 * x + t, 8, 8), :]

    g_copies = start_all(
        [
            remote(
                g_ext.at[1, 1], g_ext.at[1 - sx, 1 - st],
                g_send.at[i], g_recv.at[i], device(sx, st),
            )
            for i, (sx, st) in enumerate(NEIGHBOURS)
        ]
    )
    k_copies = edge_copies(k_ext, FACES + CORNERS, k_send, k_recv)

    sub = lax.broadcasted_iota(jnp.int32, (8, 128), 0).astype(F32)
    rough = field_grad.astype(jnp.bfloat16).astype(F32)
    small[2] = rough
    small[1] = field_grad - rough
    wide = []
    for n in range(4):
        s = 4 * (n // 2) + n % 2
        course_row = jnp.broadcast_to(small[0, pl.ds(s, 1), :], (8, 128))
        rough_row = jnp.broadcast_to(small[2, pl.ds(s, 1), :], (8, 128))
        rest_row = jnp.broadcast_to(small[1, pl.ds(s, 1), :], (8, 128))
        wide.append(
            jnp.where(course_row == sub, rough_row, 0.0)
            + jnp.where(course_row + 4.0 == sub, rest_row, 0.0)
        )
    wide = jnp.concatenate(wide, axis=1).astype(jnp.bfloat16)
    lines = []
    for dx in range(3):
        for dt in range(3):
            for j in range(9):
                lines.append(
                    jnp.concatenate(
                        [feat_rows[j, (n // 2 + dx) * 4 + n % 2 + dt] for n in range(4)], axis=1
                    )
                )
    lines = jnp.concatenate(lines + [jnp.zeros((8, 512), F32)], axis=0)
    lines_high = lines.astype(jnp.bfloat16)
    lines_low = (lines - lines_high.astype(F32)).astype(jnp.bfloat16)
    contract = (((1,), (1,)), ((), ()))
    high_sum = lax.dot_general(wide, lines_high, contract, preferred_element_type=F32)
    low_sum = lax.dot_general(wide, lines_low, contract, preferred_element_type=F32)
    tap_sum = high_sum[0:4] + (high_sum[4:8] + low_sum[0:4])
    total[...] = jnp.zeros((4, 768), F32)
    total[:, 0:656] = tap_sum

    def send_stage(number, value):
        peer_of, place, count, base = stages[number]
        buffer = reds[number]
        buffer[place] = value
        return start_all(
            [
                remote(
                    buffer.at[place], buffer.at[place],
                    red_send.at[base + k], red_recv.at[base + k], peer_of(k),
                )
                for k in range(1, count)
            ]
        )

    def take_stage(number, copies):
        finish(copies)
        buffer = reds[number]
        out = buffer[0]
        for k in range(1, stages[number][2]):
            out = out + buffer[k]
        return out

    copies_a = [send_stage(3 * h, total[:, 384 * h : 384 * h + 384]) for h in range(2)]

    blend = scaled(powers[4], 1.0 / 24.0)
    for k, factor in ((3, 1.0 / 6.0), (2, 0.5), (1, 1.0), (0, 1.0)):
        blend = add(scaled(blend, strength), scaled(powers[k], factor))
    straight = mul(blend, picked_link)

    def spread_blocks(blocks, places):
        mask = half_mask(blocks.shape)
        axis = blocks.ndim - 2
        values = jnp.where(mask, pltpu.roll(blocks, 2, axis), blocks)
        codes = jnp.where(mask, blocks, pltpu.roll(blocks, 6, axis))
        for pair in range(2):
            wanted = jnp.where(mask, 2.0 * pair + 1.0, 2.0 * pair)
            one = jnp.where(codes == wanted, values, 0.0)
            for dy in range(3):
                along_y = shift_yz(one, 1 - dy, 0)
                for dz in range(3):
                    moved = shift_yz(along_y, 0, 1 - dz)
                    for n, (bx, bt) in enumerate(places):
                        g_rows[dy * 3 + dz, pair, bx, bt] = moved[n]

    spots = inner + [(0, 1), (0, 2), (3, 1), (3, 2), (1, 0), (2, 0), (1, 3), (2, 3), (3, 0), (0, 3)]

    def back_step(own):
        def step(j, acc):
            acc = list(acc)
            for o in range(4):
                rows = {}
                for dx in range(3):
                    for dt in range(3):
                        tap = None
                        for n, (ext_x, ext_t) in enumerate(spots):
                            px, pt = ext_x + 2 - dx, ext_t + 2 - dt
                            if (px // 2 == 1 and pt // 2 == 1) != own:
                                continue
                            if tap is None:
                                tap = tap_rows[j, (dx * 3 + dt) * 4 + o]
                            if (px, pt) not in rows:
                                s = 4 * (px % 2) + 2 * (o % 2) + pt % 2
                                rows[px, pt] = jnp.broadcast_to(
                                    g_rows[j, o // 2, px // 2, pt // 2, pl.ds(s, 1), :], (8, 128)
                                )
                            acc[n] = acc[n] + tap * rows[px, pt]
            return tuple(acc)

        return step

    around = [(bx, bt) for bx in range(3) for bt in range(3) if (bx, bt) != (1, 1)]
    spread_blocks(g_ext[1, 1:2], [(1, 1)])
    spot_grad = tuple(jnp.zeros((8, 128), F32) for _ in spots)
    spot_grad = lax.fori_loop(0, 9, back_step(True), spot_grad)

    finish(g_copies)
    spread_blocks(jnp.stack([g_ext[bx, bt] for bx, bt in around]), around)
    copies_b = [send_stage(3 * h + 1, take_stage(3 * h, copies_a[h])) for h in range(2)]
    spot_grad = lax.fori_loop(0, 9, back_step(False), spot_grad)

    finish(k_copies)
    for n, (ext_x, ext_t) in enumerate(spots):
        block_x, block_t = (ext_x + 1) // 2, (ext_t + 1) // 2
        s = 4 * ((ext_x + 1) % 2) + 2 + (ext_t + 1) % 2
        code_row = g_ext[block_x, block_t, pl.ds(s, 1), :]
        code_ext[pl.ds(row_of(ext_x, ext_t), 1), :] = code_row
        merged = jnp.where(
            jnp.broadcast_to(code_row, (8, 128)) >= 0.0,
            k_ext[ext_x, ext_t],
            spot_grad[n] * (1.0 / 3.0),
        )
        x_rows[pl.ds(row_of(ext_x, ext_t), 8, GROWS), :] = merged

    for half in range(2):
        rows = pl.ds(2 + 8 * half, 8)
        code8 = code_ext[rows, :]
        parts = [x_rows[pl.ds(GROWS * k + 2 + 8 * half, 8), :] for k in range(8)]
        still = code8 < 0.0
        for course in range(4):
            turned = expand([jnp.where(code8 == float(course), p, 0.0) for p in parts])
            real, imag = turned
            one_real = jnp.where(still, parts[2 * course], 0.0)
            one_imag = jnp.where(still, parts[2 * course + 1], 0.0)
            zero = jnp.zeros_like(one_real)
            eye_real = jnp.stack(
                [jnp.stack([one_real if i == j else zero for j in range(3)]) for i in range(3)]
            )
            eye_imag = jnp.stack(
                [jnp.stack([one_imag if i == j else zero for j in range(3)]) for i in range(3)]
            )
            matrix = (real + eye_real, imag - eye_imag)
            product = mul(
                matrix, (ext[course, 0, :, :, rows, :], ext[course, 1, :, :, rows, :])
            )
            for k in range(2):
                x_mat[course, k, :, :, rows, :] = matrix[k]
                dressed[course, k, :, :, rows, :] = product[k]

    link_sum = {0: None, 2: None}

    def backward(number):
        course, across = ORDER[number]
        b, c, e = legs_above(ext, course, across)
        db, dc, de = legs_above(dressed, course, across)
        upper = stored(2 * number)
        change = add(mul(db, c, adj_second=True), mul(b, dc, adj_second=True))
        above = add(mul(change, e, adj_second=True), mul(upper, de, adj_second=True))
        a, b, e = legs_below(ext, course, across)
        da, db, de = legs_below(dressed, course, across)
        lower = stored(2 * number + 1)
        change = add(mul(da, b), mul(a, db))
        below = add(mul(change, e, adj_first=True), mul(lower, de, adj_first=True))
        if across >= 2:
            below = rolled(below, across, -1)
        both = add(above, below)
        link_sum[course] = both if link_sum[course] is None else add(link_sum[course], both)

    for number in range(6):
        backward(number)

    for lead in (0, 2):
        both = add(link_sum[lead], mul(staples[lead], view(x_mat, lead, 0, 0)))
        for k in range(2):
            mask = chosen_of[lead]
            for i in range(3):
                for j in range(3):
                    value = jnp.where(mask, straight[k][i, j], grads[lead][k][i, j])
                    value = value + both[0][j, i] if k == 0 else value - both[1][j, i]
                    for x in range(2):
                        grad_out[lead, k, i, j, x] = value[4 * x : 4 * x + 2, :]
                        grad_out[lead + 1, k, i, j, x] = value[4 * x + 2 : 4 * x + 4, :]

    store_links = pltpu.make_async_copy(grad_out, link_grad, in_sems.at[0])
    store_links.start()
    copies_c = [send_stage(3 * h + 2, take_stage(3 * h + 1, copies_b[h])) for h in range(2)]
    for h in range(2):
        total[:, 384 * h : 384 * h + 384] = take_stage(3 * h + 2, copies_c[h]) * scale
    for d in range(81):
        tap_out[d] = total[:, d * 8 : d * 8 + 8]
    store_taps = pltpu.make_async_copy(tap_out, kernel_grad, in_sems.at[1])
    store_taps.start()
    store_links.wait()
    store_taps.wait()

    for copy in (
        link_copies + feat_copies + g_copies + k_copies
        + sum(copies_a + copies_b + copies_c, [])
    ):
        copy.wait_send()


def shards(sizes, links, kernel, active, direction, out_grad):
    n_x, n_y, n_far, n_near = sizes[2]
    n_z = n_far * n_near
    counts = (n_z, n_y, 2 * n_x, n_y, n_z, 2 * n_x)
    hbm = pl.BlockSpec(memory_space=pltpu.HBM)

    def space(*shape):
        return pltpu.VMEM(shape, F32)

    def sems(count):
        return pltpu.SemaphoreType.DMA((count,))

    link_grad, kernel_grad = pl.pallas_call(
        functools.partial(body, sizes),
        out_shape=(
            jax.ShapeDtypeStruct(links.shape, F32),
            jax.ShapeDtypeStruct((81, 4, 8), F32),
        ),
        in_specs=[hbm] * 5,
        out_specs=(hbm, hbm),
        scratch_shapes=[
            space(4, 2, 3, 3, 2, 2, 128),
            space(81, 4, 8),
            pltpu.VMEM((2, 2, 128), jnp.int32),
            pltpu.VMEM((2, 2, 128), jnp.int32),
            space(4, 2, 3, 3, 2, 2, 128),
            space(4, 2, 3, 3, 2, 2, 128),
            space(81, 4, 8),
            space(4, 2, 3, 3, GROWS, 128),
            space(4, 2, 2, 3, 2, 128),
            space(3, 2, 2, 3, 2, 128),
            space(4, 2, 2, 3, 2, 128),
            space(3, 2, 2, 3, 2, 128),
            space(2, 2, 2, 3, 1, 128),
            space(4, 2, 2, 3, 2, 128),
            space(3, 2, 2, 3, 2, 128),
            space(4, 2, 2, 3, 2, 128),
            space(3, 2, 2, 3, 2, 128),
            space(2, 2, 2, 3, 1, 128),
            space(12, 2, 3, 3, 8, 128),
            space(9, 36, 8, 128),
            space(4, 4, 8, 128),
            space(9, 16, 8, 128),
            space(64, 128),
            space(3, 8, 128),
            space(64, 128),
            space(4, 4, 8, 128),
            space(3, 3, 8, 128),
            space(9, 2, 3, 3, 8, 128),
            space(GROWS, 128),
            space(8 * GROWS, 128),
            space(4, 2, 3, 3, GROWS, 128),
            space(4, 2, 3, 3, GROWS, 128),
            space(4, 768),
            [space(count, 4, 384) for count in counts],
            sems(5),
            sems(6), sems(6), sems(8), sems(8), sems(8), sems(8), sems(6), sems(6),
            sems(sum(counts)), sems(sum(counts)),
        ],
        compiler_params=pltpu.CompilerParams(
            collective_id=0, has_side_effects=True, vmem_limit_bytes=60 * 1024 * 1024
        ),
    )(links, kernel.reshape(81, 4, 8), active, direction, out_grad)
    return (link_grad, kernel_grad.reshape(kernel.shape))


def solution(mesh):
    n_space, n_tm = mesh.shape["space"], mesh.shape["tm"]
    n_far = 2
    n_x = max(1, n_space // (8 * n_far))
    axes = (n_x, n_space // (n_x * n_far), n_far, n_tm // 2)
    sites = n_space * n_tm * 4 * 128
    placed = (
        P(None, None, None, None, "space", "tm", None),
        P(),
        P("space", "tm", None),
        P("space", "tm", None),
        P(None, None, None, None, "space", "tm", None),
    )
    return jax.shard_map(
        functools.partial(shards, (n_space, n_tm, axes, 1.0 / math.sqrt(sites))),
        mesh=mesh,
        in_specs=placed,
        out_specs=(P(None, None, None, None, "space", "tm", None), P()),
        check_vma=False,
    )
```

```python
import functools
import math

import jax
import jax.numpy as jnp
from jax import lax
from jax.experimental import pallas as pl
from jax.experimental.pallas import tpu as pltpu
from jax.sharding import PartitionSpec as P

PAIR = (1, 0, 3, 2)
MESH = pl.DeviceIdType.MESH
F32 = jnp.float32
NEIGHBOURS = tuple((sx, st) for sx in (-1, 0, 1) for st in (-1, 0, 1) if (sx, st) != (0, 0))
FACES = ((-1, 0), (1, 0), (0, -1), (0, 1))
CORNERS = ((1, -1), (-1, 1))
GROWS = 24


def row_of(ext_x, ext_t):
    return 2 + 4 * ext_x + ext_t


def lane_iota(shape):
    return lax.broadcasted_iota(jnp.int32, shape, len(shape) - 1)


def half_mask(shape):
    return ((lax.broadcasted_iota(jnp.int32, shape, len(shape) - 2) >> 1) & 1) == 1


def roll_y(values, step):
    return pltpu.roll(values, (-16 * step) % 128, values.ndim - 1)


def roll_z(values, step):
    axis = values.ndim - 1
    z_coord = lane_iota(values.shape) & 15
    if step == 1:
        return jnp.where(z_coord == 15, pltpu.roll(values, 15, axis), pltpu.roll(values, 127, axis))
    return jnp.where(z_coord == 0, pltpu.roll(values, 113, axis), pltpu.roll(values, 1, axis))


def shift_yz(values, step_y, step_z):
    if step_y:
        values = roll_y(values, step_y)
    if step_z:
        values = roll_z(values, step_z)
    return values


def swap_halves(values):
    axis = values.ndim - 2
    return jnp.where(
        half_mask(values.shape), pltpu.roll(values, 2, axis), pltpu.roll(values, 6, axis)
    )


def split_roll(values, lead, step):
    along_y = roll_y(values, step)
    along_z = roll_z(values, step)
    first, second = (along_y, along_z) if lead == 2 else (along_z, along_y)
    return jnp.where(half_mask(values.shape), second, first)


def rolled(matrix, lead, step):
    return tuple(split_roll(part, lead, step) for part in matrix)


def mul(first, second, adj_first=False, adj_second=False):
    def column(part, k):
        return jnp.expand_dims(part[k] if adj_first else part[:, k], 1)

    def line(part, k):
        return jnp.expand_dims(part[:, k] if adj_second else part[k], 0)

    sums = [None] * 4
    for k in range(3):
        fr, fi = column(first[0], k), column(first[1], k)
        sr, si = line(second[0], k), line(second[1], k)
        terms = (fr * sr, fi * si, fr * si, fi * sr)
        sums = [t if s is None else s + t for s, t in zip(sums, terms)]
    rr, ii, ri, ir = sums
    real = rr + ii if adj_first != adj_second else rr - ii
    if adj_first and adj_second:
        imag = -(ri + ir)
    elif adj_first:
        imag = ri - ir
    elif adj_second:
        imag = ir - ri
    else:
        imag = ri + ir
    return (real, imag)


def add(first, second):
    return (first[0] + second[0], first[1] + second[1])


def scaled(matrix, factor):
    return (matrix[0] * factor, matrix[1] * factor)


def view(ref, course, dx, dt):
    start = row_of(1 + dx, 1 + dt)
    pair_start = row_of(1 + dt, 1 + dx) - 2
    parts = []
    for part in range(2):
        own = ref[course, part, :, :, pl.ds(start, 8), :]
        other = ref[PAIR[course], part, :, :, pl.ds(pair_start, 8), :]
        parts.append(jnp.where(half_mask(own.shape), other, own))
    return tuple(parts)


def view_at(ref, course, lead, step):
    if lead == 0:
        return view(ref, course, step, 0)
    if lead == 1:
        return view(ref, course, 0, step)
    return rolled(view(ref, course, 0, 0), lead, step)


ORDER = ((2, 3), (0, 1), (0, 2), (0, 3), (2, 0), (2, 1))


def legs_above(ref, course, across):
    return (
        view_at(ref, across, course, 1),
        view_at(ref, course, across, 1),
        view(ref, across, 0, 0),
    )


def legs_below(ref, course, across):
    if across >= 2:
        return (
            view(ref, course, 0, 0),
            view_at(ref, across, course, 1),
            view(ref, across, 0, 0),
        )
    back = (-1, 0) if across == 0 else (0, -1)
    base = view(ref, across, *back)
    if course >= 2:
        ahead = rolled(base, course, 1)
    else:
        step = (back[0] + (course == 0), back[1] + (course == 1))
        ahead = view(ref, across, *step)
    return (view(ref, course, *back), ahead, base)


def third_line(first, second):
    out = []
    for j in range(3):
        p, q = (j + 1) % 3, (j + 2) % 3
        (ar, ai), (br, bi) = first[p], second[q]
        (cr, ci), (dr, di) = first[q], second[p]
        real = (ar * br - ai * bi) - (cr * dr - ci * di)
        imag = (ar * bi + ai * br) - (cr * di + ci * dr)
        out.append((real, -imag))
    return out


def body(
    sizes, links_in, taps_in, active_in, direction_in, out_grad_in, link_grad, kernel_grad,
    links, taps, active, direction, out_grad, grad_out, tap_out,
    ext, send_x0, send_x1, send_t0, send_t1, send_c, recv_x0, recv_x1, recv_t0, recv_t1, recv_c,
    mids, tap_rows, feats, feat_rows, trace_rows, small, k_rows, k_ext, g_ext, g_rows,
    code_ext, x_rows, x_mat, dressed, total, reds,
    in_sems, link_send, link_recv, feat_send, feat_recv, g_send, g_recv, k_send, k_recv,
    red_send, red_recv,
):
    n_space, n_tm, axes, scale = sizes
    n_x, n_y, n_far, n_near = axes
    n_z = n_far * n_near
    my_x, my_t = lax.axis_index("space"), lax.axis_index("tm")

    def device(sx, st):
        return (lax.rem(my_x + sx + n_space, n_space), lax.rem(my_t + st + n_tm, n_tm))

    at_core = lax.rem(my_t, 2)
    at_z = lax.rem(my_x, n_far) * n_near + lax.div(my_t, 2)
    at_y = lax.rem(lax.div(my_x, n_far), n_y)
    at_x = lax.div(my_x, n_far * n_y)

    def z_peer(k):
        z = lax.rem(at_z + k, n_z)
        space = lax.div(my_x, n_far) * n_far + lax.div(z, n_near)
        return (space, lax.rem(z, n_near) * 2 + at_core)

    def y_peer(k):
        y = lax.rem(at_y + k, n_y)
        return ((at_x * n_y + y) * n_far + lax.rem(my_x, n_far), my_t)

    def x_peer(k):
        place = lax.rem(at_x * 2 + at_core + k, 2 * n_x)
        space = lax.div(place, 2) * n_y * n_far + lax.rem(my_x, n_y * n_far)
        return (space, my_t - at_core + lax.rem(place, 2))

    along_z = (z_peer, at_z, n_z)
    along_y = (y_peer, at_y, n_y)
    along_x = (x_peer, at_x * 2 + at_core, 2 * n_x)
    stages = []
    base = 0
    for half in ((along_x, along_z, along_y), (along_x, along_y, along_z)):
        for peer_of, place, count in half:
            stages.append((peer_of, place, count, base))
            base += count
    peers = [device(sx, st) for sx, st in NEIGHBOURS]
    for peer_of, _, count in (along_z, along_y, along_x):
        peers += [peer_of(k) for k in range(1, count)]
    barrier = pltpu.get_barrier_semaphore()
    for peer in peers:
        pl.semaphore_signal(barrier, inc=1, device_id=peer, device_id_type=MESH)

    loads = [
        pltpu.make_async_copy(source, target, in_sems.at[i])
        for i, (source, target) in enumerate(
            (
                (links_in, links), (taps_in, taps), (active_in, active),
                (direction_in, direction), (out_grad_in, out_grad),
            )
        )
    ]
    for load in loads:
        load.start()
    loads[0].wait()

    send_x0[...] = links[:, :, 0:2, :, 1]
    send_x1[...] = links[1:4, :, 0:2, :, 0]
    for x in range(2):
        send_t0[:, :, :, :, x : x + 1, :] = links[:, :, 0:2, :, x, 1:2, :]
        send_t1[0:1, :, :, :, x : x + 1, :] = links[0:1, :, 0:2, :, x, 0:1, :]
        send_t1[1:3, :, :, :, x : x + 1, :] = links[2:4, :, 0:2, :, x, 0:1, :]
    send_c[0] = links[1, :, 0:2, :, 0, 1:2, :]
    send_c[1] = links[0, :, 0:2, :, 1, 0:1, :]

    pl.semaphore_wait(barrier, len(peers))

    def remote(source, target, send_sem, recv_sem, peer):
        return pltpu.make_async_remote_copy(
            src_ref=source, dst_ref=target, send_sem=send_sem, recv_sem=recv_sem,
            device_id=peer, device_id_type=MESH,
        )

    def start_all(copies):
        for copy in copies:
            copy.start()
        return copies

    def finish(copies):
        for copy in copies:
            copy.wait_recv()

    plan = (
        (send_x0, recv_x0, (1, 0)),
        (send_x1, recv_x1, (-1, 0)),
        (send_c.at[0], recv_c.at[0], (-1, 1)),
        (send_c.at[1], recv_c.at[1], (1, -1)),
        (send_t0, recv_t0, (0, 1)),
        (send_t1, recv_t1, (0, -1)),
    )
    link_copies = start_all(
        [
            remote(source, target, link_send.at[i], link_recv.at[i], device(*step))
            for i, (source, target, step) in enumerate(plan)
        ]
    )

    ext[:, :, :, :, pl.ds(row_of(1, 1), 2), :] = links[:, :, :, :, 0]
    ext[:, :, :, :, pl.ds(row_of(2, 1), 2), :] = links[:, :, :, :, 1]

    for load in loads[1:]:
        load.wait()
    diagonal = lax.broadcasted_iota(jnp.int32, (8, 8), 0) == lax.broadcasted_iota(
        jnp.int32, (8, 8), 1
    )

    def spread_taps(j, carry):
        for dxdt in range(9):
            block = taps[dxdt * 9 + j]
            for o in range(4):
                line = jnp.broadcast_to(block[o : o + 1, :], (8, 8))
                column = jnp.sum(jnp.where(diagonal, line, 0.0), axis=1, keepdims=True)
                tap_rows[j, dxdt * 4 + o] = jnp.broadcast_to(column, (8, 128))
        return carry

    lax.fori_loop(0, 9, spread_taps, 0)

    hid = (lax.broadcasted_iota(jnp.int32, (8, 128), 0) >> 1) & 1
    course_of = jnp.concatenate([direction[0], direction[0], direction[1], direction[1]], axis=0)
    moving = jnp.concatenate([active[0], active[0], active[1], active[1]], axis=0)
    moves = moving.astype(F32)
    frozen_third = (1.0 - moves) * (1.0 / 3.0)
    chosen_of = {0: course_of == hid, 2: course_of == hid + 2}

    def stored(index):
        return (mids[index, 0], mids[index, 1])

    def store_mid(index, matrix):
        mids[index, 0] = matrix[0]
        mids[index, 1] = matrix[1]

    staples = {0: None, 2: None}

    def forward(number):
        course, across = ORDER[number]
        b, c, e = legs_above(ext, course, across)
        upper = mul(b, c, adj_second=True)
        store_mid(2 * number, upper)
        above = mul(upper, e, adj_second=True)
        a, b, e = legs_below(ext, course, across)
        lower = mul(a, b)
        store_mid(2 * number + 1, lower)
        below = mul(lower, e, adj_first=True)
        if across >= 2:
            below = rolled(below, across, -1)
        both = add(above, below)
        staples[course] = both if staples[course] is None else add(staples[course], both)

    forward(0)

    finish(link_copies)

    def fill(buffer, courses, put):
        lines = [
            [(buffer[:, 0, i, j], buffer[:, 1, i, j]) for j in range(3)] for i in range(2)
        ]
        lines.append(third_line(*lines))
        for i in range(3):
            for j in range(3):
                for k in range(2):
                    put(courses, k, i, j, lines[i][j][k])

    def put_x(ext_x):
        def put(courses, k, i, j, value):
            for n, course in enumerate(courses):
                ext[course, k, i, j, pl.ds(row_of(ext_x, 1), 2), :] = value[n]

        return put

    def put_t(ext_t):
        def put(courses, k, i, j, value):
            for n, course in enumerate(courses):
                for x in range(2):
                    ext[course, k, i, j, pl.ds(row_of(1 + x, ext_t), 1), :] = value[n, x : x + 1]

        return put

    def put_c(courses, k, i, j, value):
        ext[1, k, i, j, pl.ds(row_of(3, 0), 1), :] = value[0]
        ext[0, k, i, j, pl.ds(row_of(0, 3), 1), :] = value[1]

    fill(recv_x0, (0, 1, 2, 3), put_x(0))
    fill(recv_x1, (1, 2, 3), put_x(3))
    fill(recv_t0, (0, 1, 2, 3), put_t(0))
    fill(recv_t1, (0, 2, 3), put_t(3))
    fill(recv_c, (1, 0), put_c)

    for number in range(1, 6):
        forward(number)

    def trace(part):
        return part[0, 0] + part[1, 1] + part[2, 2]

    cores = {lead: view(ext, lead, 0, 0) for lead in (0, 2)}
    closed = {lead: mul(cores[lead], staples[lead]) for lead in (0, 2)}
    for lead in (0, 2):
        for k in range(2):
            value = trace(closed[lead][k]) * frozen_third
            trace_rows[pl.ds((2 * lead + k) * 8, 8), :] = value
            trace_rows[pl.ds((2 * lead + 2 + k) * 8, 8), :] = swap_halves(value)
    for x in range(2):
        for t in range(2):
            feats[1 + x, 1 + t] = trace_rows[pl.ds(4 * x + t, 8, 8), :]

    def edge(step):
        source = {1: pl.ds(2, 1), -1: pl.ds(1, 1), 0: pl.ds(1, 2)}[step]
        target = {1: pl.ds(0, 1), -1: pl.ds(3, 1), 0: pl.ds(1, 2)}[step]
        return source, target

    def edge_copies(ref, steps, send_sem, recv_sem):
        copies = []
        for i, (sx, st) in enumerate(steps):
            (from_x, to_x), (from_t, to_t) = edge(sx), edge(st)
            copies.append(
                remote(
                    ref.at[from_x, from_t], ref.at[to_x, to_t],
                    send_sem.at[i], recv_sem.at[i], device(sx, st),
                )
            )
        return start_all(copies)

    feat_copies = edge_copies(feats, NEIGHBOURS, feat_send, feat_recv)

    def roll_features(positions):
        for ext_x, ext_t in positions:
            value = feats[ext_x, ext_t]
            for dy in range(3):
                along_y = shift_yz(value, dy - 1, 0)
                for dz in range(3):
                    feat_rows[dy * 3 + dz, ext_x * 4 + ext_t] = shift_yz(along_y, 0, dz - 1)

    inner = [(x, t) for x in (1, 2) for t in (1, 2)]
    outer = [(x, t) for x in range(4) for t in range(4) if (x, t) not in inner]
    roll_features(inner)

    grads = {}
    for lead in (0, 2):
        grads[lead] = tuple(
            jnp.concatenate(
                [
                    out_grad[lead, k, :, :, 0],
                    out_grad[lead + 1, k, :, :, 0],
                    out_grad[lead, k, :, :, 1],
                    out_grad[lead + 1, k, :, :, 1],
                ],
                axis=2,
            )
            for k in range(2)
        )

    def choose(field):
        out = []
        for k in range(2):
            first, second = field[0][k], field[2][k]
            mask_first = jnp.broadcast_to(chosen_of[0].astype(F32), first.shape)
            mask_second = jnp.broadcast_to(chosen_of[2].astype(F32), first.shape)
            picked = first * mask_first + second * mask_second
            out.append(picked + swap_halves(picked))
        return tuple(out)

    def project(matrix):
        real, imag = matrix
        third = trace(imag) * (1.0 / 3.0)
        out = []
        for i, j in ((0, 1), (0, 2), (1, 2)):
            out.append((real[i, j] - real[j, i]) * 0.5)
            out.append((imag[i, j] + imag[j, i]) * 0.5)
        return out + [imag[0, 0] - third, imag[1, 1] - third]

    def expand(parts):
        r01, i01, r02, i02, r12, i12, d0, d1 = parts
        zero = jnp.zeros_like(d0)
        real = jnp.stack(
            [
                jnp.stack([zero, r01, r02]),
                jnp.stack([-r01, zero, r12]),
                jnp.stack([-r02, -r12, zero]),
            ]
        )
        imag = jnp.stack(
            [
                jnp.stack([d0, i01, i02]),
                jnp.stack([i01, d1, i12]),
                jnp.stack([i02, i12, -d0 - d1]),
            ]
        )
        return (real, imag)

    picked_link = choose(cores)
    generator = expand(project(choose(closed)))
    minus = scaled(generator, -1.0)
    powers = [mul(choose(grads), picked_link, adj_second=True)]
    for _ in range(4):
        powers.append(mul(minus, powers[-1]))
    series = [powers[0]]
    for k in range(3):
        series.append(add(powers[k + 1], mul(series[-1], minus)))

    def inner_product(first, second):
        total_sum = None
        for k in range(2):
            for i in range(3):
                for j in range(3):
                    term = first[k][i, j] * second[k][i, j]
                    total_sum = term if total_sum is None else total_sum + term
        return total_sum

    slopes = [inner_product(powers[k], generator) for k in range(4)]
    turns = [project(matrix) for matrix in series]

    small[0] = course_of.astype(F32)

    def conv_step(own):
        def step(j, acc):
            acc = list(acc)
            for dx in range(3):
                for dt in range(3):
                    for o in range(4):
                        tap = None
                        for n in range(4):
                            spot = (n // 2 + dx, n % 2 + dt)
                            if (spot in inner) != own:
                                continue
                            if tap is None:
                                tap = tap_rows[j, (dx * 3 + dt) * 4 + o]
                            term = tap * feat_rows[j, spot[0] * 4 + spot[1]]
                            acc[o * 4 + n] = acc[o * 4 + n] + term
            return tuple(acc)

        return step

    acc = tuple(jnp.zeros((8, 128), F32) for _ in range(16))
    acc = lax.fori_loop(0, 9, conv_step(True), acc)

    finish(feat_copies)
    roll_features(outer)

    acc = lax.fori_loop(0, 9, conv_step(False), acc, unroll=9)
    for n in range(4):
        s = 4 * (n // 2) + n % 2
        course_row = jnp.broadcast_to(small[0, pl.ds(s, 1), :], (8, 128))
        picked = jnp.where(course_row == 0.0, acc[n], 0.0)
        for o in range(1, 4):
            picked = picked + jnp.where(course_row == float(o), acc[o * 4 + n], 0.0)
        field_row = jnp.sum(picked, axis=0, keepdims=True)
        small[1, pl.ds(s, 1), :] = field_row
        small[1, pl.ds(s + 2, 1), :] = field_row
    bent = jnp.tanh(small[1])
    strength = bent * moves
    c1, c2, c3, c4 = slopes
    slope = c1 + strength * (c2 + strength * (c3 * 0.5 + strength * (c4 * (1.0 / 6.0))))
    field_grad = moves * (1.0 - bent * bent) * slope
    code = jnp.where(moving == 1, course_of, -1).astype(F32)
    g_ext[1, 1] = jnp.where(hid == 0, field_grad, code)
    t1, t2, t3, t4 = turns
    for k in range(8):
        poly = t1[k] + strength * (
            t2[k] * 0.5 + strength * (t3[k] * (1.0 / 6.0) + strength * (t4[k] * (1.0 / 24.0)))
        )
        k_rows[pl.ds(8 * k, 8), :] = -strength * poly
    for x in range(2):
        for t in range(2):
            k_ext[1 + x, 1 + t] = k_rows[pl.ds(4 * x + t, 8, 8), :]

    g_copies = start_all(
        [
            remote(
                g_ext.at[1, 1], g_ext.at[1 - sx, 1 - st],
                g_send.at[i], g_recv.at[i], device(sx, st),
            )
            for i, (sx, st) in enumerate(NEIGHBOURS)
        ]
    )
    k_copies = edge_copies(k_ext, FACES + CORNERS, k_send, k_recv)

    sub = lax.broadcasted_iota(jnp.int32, (8, 128), 0).astype(F32)
    rough = field_grad.astype(jnp.bfloat16).astype(F32)
    small[2] = rough
    small[1] = field_grad - rough
    wide = []
    for n in range(4):
        s = 4 * (n // 2) + n % 2
        course_row = jnp.broadcast_to(small[0, pl.ds(s, 1), :], (8, 128))
        rough_row = jnp.broadcast_to(small[2, pl.ds(s, 1), :], (8, 128))
        rest_row = jnp.broadcast_to(small[1, pl.ds(s, 1), :], (8, 128))
        wide.append(
            jnp.where(course_row == sub, rough_row, 0.0)
            + jnp.where(course_row + 4.0 == sub, rest_row, 0.0)
        )
    wide = jnp.concatenate(wide, axis=1).astype(jnp.bfloat16)
    lines = []
    for dx in range(3):
        for dt in range(3):
            for j in range(9):
                lines.append(
                    jnp.concatenate(
                        [feat_rows[j, (n // 2 + dx) * 4 + n % 2 + dt] for n in range(4)], axis=1
                    )
                )
    lines = jnp.concatenate(lines + [jnp.zeros((8, 512), F32)], axis=0)
    lines_high = lines.astype(jnp.bfloat16)
    lines_low = (lines - lines_high.astype(F32)).astype(jnp.bfloat16)
    contract = (((1,), (1,)), ((), ()))
    high_sum = lax.dot_general(wide, lines_high, contract, preferred_element_type=F32)
    low_sum = lax.dot_general(wide, lines_low, contract, preferred_element_type=F32)
    tap_sum = high_sum[0:4] + (high_sum[4:8] + low_sum[0:4])
    total[...] = jnp.zeros((4, 768), F32)
    total[:, 0:656] = tap_sum

    def send_stage(number, value):
        peer_of, place, count, base = stages[number]
        buffer = reds[number]
        buffer[place] = value
        return start_all(
            [
                remote(
                    buffer.at[place], buffer.at[place],
                    red_send.at[base + k], red_recv.at[base + k], peer_of(k),
                )
                for k in range(1, count)
            ]
        )

    def take_stage(number, copies):
        finish(copies)
        buffer = reds[number]
        out = buffer[0]
        for k in range(1, stages[number][2]):
            out = out + buffer[k]
        return out

    copies_a = [send_stage(3 * h, total[:, 384 * h : 384 * h + 384]) for h in range(2)]

    blend = scaled(powers[4], 1.0 / 24.0)
    for k, factor in ((3, 1.0 / 6.0), (2, 0.5), (1, 1.0), (0, 1.0)):
        blend = add(scaled(blend, strength), scaled(powers[k], factor))
    straight = mul(blend, picked_link)

    def spread_blocks(blocks, places):
        mask = half_mask(blocks.shape)
        axis = blocks.ndim - 2
        values = jnp.where(mask, pltpu.roll(blocks, 2, axis), blocks)
        codes = jnp.where(mask, blocks, pltpu.roll(blocks, 6, axis))
        for pair in range(2):
            wanted = jnp.where(mask, 2.0 * pair + 1.0, 2.0 * pair)
            one = jnp.where(codes == wanted, values, 0.0)
            for dy in range(3):
                along_y = shift_yz(one, 1 - dy, 0)
                for dz in range(3):
                    moved = shift_yz(along_y, 0, 1 - dz)
                    for n, (bx, bt) in enumerate(places):
                        g_rows[dy * 3 + dz, pair, bx, bt] = moved[n]

    spots = inner + [(0, 1), (0, 2), (3, 1), (3, 2), (1, 0), (2, 0), (1, 3), (2, 3), (3, 0), (0, 3)]

    def back_step(own):
        def step(j, acc):
            acc = list(acc)
            for o in range(4):
                rows = {}
                for dx in range(3):
                    for dt in range(3):
                        tap = None
                        for n, (ext_x, ext_t) in enumerate(spots):
                            px, pt = ext_x + 2 - dx, ext_t + 2 - dt
                            if (px // 2 == 1 and pt // 2 == 1) != own:
                                continue
                            if tap is None:
                                tap = tap_rows[j, (dx * 3 + dt) * 4 + o]
                            if (px, pt) not in rows:
                                s = 4 * (px % 2) + 2 * (o % 2) + pt % 2
                                rows[px, pt] = jnp.broadcast_to(
                                    g_rows[j, o // 2, px // 2, pt // 2, pl.ds(s, 1), :], (8, 128)
                                )
                            acc[n] = acc[n] + tap * rows[px, pt]
            return tuple(acc)

        return step

    around = [(bx, bt) for bx in range(3) for bt in range(3) if (bx, bt) != (1, 1)]
    spread_blocks(g_ext[1, 1:2], [(1, 1)])
    spot_grad = tuple(jnp.zeros((8, 128), F32) for _ in spots)
    spot_grad = lax.fori_loop(0, 9, back_step(True), spot_grad)

    copies_b = [send_stage(3 * h + 1, take_stage(3 * h, copies_a[h])) for h in range(2)]

    finish(g_copies)
    spread_blocks(jnp.stack([g_ext[bx, bt] for bx, bt in around]), around)
    spot_grad = lax.fori_loop(0, 9, back_step(False), spot_grad, unroll=3)

    finish(k_copies)
    for n, (ext_x, ext_t) in enumerate(spots):
        block_x, block_t = (ext_x + 1) // 2, (ext_t + 1) // 2
        s = 4 * ((ext_x + 1) % 2) + 2 + (ext_t + 1) % 2
        code_row = g_ext[block_x, block_t, pl.ds(s, 1), :]
        code_ext[pl.ds(row_of(ext_x, ext_t), 1), :] = code_row
        merged = jnp.where(
            jnp.broadcast_to(code_row, (8, 128)) >= 0.0,
            k_ext[ext_x, ext_t],
            spot_grad[n] * (1.0 / 3.0),
        )
        x_rows[pl.ds(row_of(ext_x, ext_t), 8, GROWS), :] = merged

    for half in range(2):
        rows = pl.ds(2 + 8 * half, 8)
        code8 = code_ext[rows, :]
        parts = [x_rows[pl.ds(GROWS * k + 2 + 8 * half, 8), :] for k in range(8)]
        still = code8 < 0.0
        for course in range(4):
            turned = expand([jnp.where(code8 == float(course), p, 0.0) for p in parts])
            real, imag = turned
            one_real = jnp.where(still, parts[2 * course], 0.0)
            one_imag = jnp.where(still, parts[2 * course + 1], 0.0)
            zero = jnp.zeros_like(one_real)
            eye_real = jnp.stack(
                [jnp.stack([one_real if i == j else zero for j in range(3)]) for i in range(3)]
            )
            eye_imag = jnp.stack(
                [jnp.stack([one_imag if i == j else zero for j in range(3)]) for i in range(3)]
            )
            matrix = (real + eye_real, imag - eye_imag)
            product = mul(
                matrix, (ext[course, 0, :, :, rows, :], ext[course, 1, :, :, rows, :])
            )
            for k in range(2):
                x_mat[course, k, :, :, rows, :] = matrix[k]
                dressed[course, k, :, :, rows, :] = product[k]

    link_sum = {0: None, 2: None}

    def backward(number):
        course, across = ORDER[number]
        b, c, e = legs_above(ext, course, across)
        db, dc, de = legs_above(dressed, course, across)
        upper = stored(2 * number)
        change = add(mul(db, c, adj_second=True), mul(b, dc, adj_second=True))
        above = add(mul(change, e, adj_second=True), mul(upper, de, adj_second=True))
        a, b, e = legs_below(ext, course, across)
        da, db, de = legs_below(dressed, course, across)
        lower = stored(2 * number + 1)
        change = add(mul(da, b), mul(a, db))
        below = add(mul(change, e, adj_first=True), mul(lower, de, adj_first=True))
        if across >= 2:
            below = rolled(below, across, -1)
        both = add(above, below)
        link_sum[course] = both if link_sum[course] is None else add(link_sum[course], both)

    for number in range(6):
        backward(number)

    for lead in (0, 2):
        both = add(link_sum[lead], mul(staples[lead], view(x_mat, lead, 0, 0)))
        for k in range(2):
            mask = chosen_of[lead]
            for i in range(3):
                for j in range(3):
                    value = jnp.where(mask, straight[k][i, j], grads[lead][k][i, j])
                    value = value + both[0][j, i] if k == 0 else value - both[1][j, i]
                    for x in range(2):
                        grad_out[lead, k, i, j, x] = value[4 * x : 4 * x + 2, :]
                        grad_out[lead + 1, k, i, j, x] = value[4 * x + 2 : 4 * x + 4, :]

    store_links = pltpu.make_async_copy(grad_out, link_grad, in_sems.at[0])
    store_links.start()
    copies_c = [send_stage(3 * h + 2, take_stage(3 * h + 1, copies_b[h])) for h in range(2)]
    for h in range(2):
        total[:, 384 * h : 384 * h + 384] = take_stage(3 * h + 2, copies_c[h]) * scale
    for d in range(81):
        tap_out[d // 27, d // 9 % 3, d // 3 % 3, d % 3] = total[:, d * 8 : d * 8 + 8]
    store_taps = pltpu.make_async_copy(tap_out, kernel_grad, in_sems.at[1])
    store_taps.start()
    store_links.wait()
    store_taps.wait()

    for copy in (
        link_copies + feat_copies + g_copies + k_copies
        + sum(copies_a + copies_b + copies_c, [])
    ):
        copy.wait_send()


def shards(sizes, links, kernel, active, direction, out_grad):
    n_x, n_y, n_far, n_near = sizes[2]
    n_z = n_far * n_near
    counts = (2 * n_x, n_z, n_y, 2 * n_x, n_y, n_z)
    hbm = pl.BlockSpec(memory_space=pltpu.HBM)

    def space(*shape):
        return pltpu.VMEM(shape, F32)

    def sems(count):
        return pltpu.SemaphoreType.DMA((count,))

    link_grad, kernel_grad = pl.pallas_call(
        functools.partial(body, sizes),
        out_shape=(
            jax.ShapeDtypeStruct(links.shape, F32),
            jax.ShapeDtypeStruct(kernel.shape, F32),
        ),
        in_specs=[hbm] * 5,
        out_specs=(hbm, hbm),
        scratch_shapes=[
            space(4, 2, 3, 3, 2, 2, 128),
            space(81, 4, 8),
            pltpu.VMEM((2, 2, 128), jnp.int32),
            pltpu.VMEM((2, 2, 128), jnp.int32),
            space(4, 2, 3, 3, 2, 2, 128),
            space(4, 2, 3, 3, 2, 2, 128),
            space(*kernel.shape),
            space(4, 2, 3, 3, GROWS, 128),
            space(4, 2, 2, 3, 2, 128),
            space(3, 2, 2, 3, 2, 128),
            space(4, 2, 2, 3, 2, 128),
            space(3, 2, 2, 3, 2, 128),
            space(2, 2, 2, 3, 1, 128),
            space(4, 2, 2, 3, 2, 128),
            space(3, 2, 2, 3, 2, 128),
            space(4, 2, 2, 3, 2, 128),
            space(3, 2, 2, 3, 2, 128),
            space(2, 2, 2, 3, 1, 128),
            space(12, 2, 3, 3, 8, 128),
            space(9, 36, 8, 128),
            space(4, 4, 8, 128),
            space(9, 16, 8, 128),
            space(64, 128),
            space(3, 8, 128),
            space(64, 128),
            space(4, 4, 8, 128),
            space(3, 3, 8, 128),
            space(9, 2, 3, 3, 8, 128),
            space(GROWS, 128),
            space(8 * GROWS, 128),
            space(4, 2, 3, 3, GROWS, 128),
            space(4, 2, 3, 3, GROWS, 128),
            space(4, 768),
            [space(count, 4, 384) for count in counts],
            sems(5),
            sems(6), sems(6), sems(8), sems(8), sems(8), sems(8), sems(6), sems(6),
            sems(sum(counts)), sems(sum(counts)),
        ],
        compiler_params=pltpu.CompilerParams(
            collective_id=0, has_side_effects=True, vmem_limit_bytes=60 * 1024 * 1024
        ),
    )(links, kernel.reshape(81, 4, 8), active, direction, out_grad)
    return (link_grad, kernel_grad)


def solution(mesh):
    n_space, n_tm = mesh.shape["space"], mesh.shape["tm"]
    n_far = 2
    n_x = max(1, n_space // (8 * n_far))
    axes = (n_x, n_space // (n_x * n_far), n_far, n_tm // 2)
    sites = n_space * n_tm * 4 * 128
    placed = (
        P(None, None, None, None, "space", "tm", None),
        P(),
        P("space", "tm", None),
        P("space", "tm", None),
        P(None, None, None, None, "space", "tm", None),
    )
    return jax.shard_map(
        functools.partial(shards, (n_space, n_tm, axes, 1.0 / math.sqrt(sites))),
        mesh=mesh,
        in_specs=placed,
        out_specs=(P(None, None, None, None, "space", "tm", None), P()),
        check_vma=False,
    )
```

```python
import functools
import math

import jax
import jax.numpy as jnp
from jax import lax
from jax.experimental import pallas as pl
from jax.experimental.pallas import tpu as pltpu
from jax.sharding import PartitionSpec as P

PAIR = (1, 0, 3, 2)
MESH = pl.DeviceIdType.MESH
F32 = jnp.float32
NEIGHBOURS = tuple((sx, st) for sx in (-1, 0, 1) for st in (-1, 0, 1) if (sx, st) != (0, 0))
FACES = ((-1, 0), (1, 0), (0, -1), (0, 1))
CORNERS = ((1, -1), (-1, 1))
GROWS = 24


def row_of(ext_x, ext_t):
    return 2 + 4 * ext_x + ext_t


def lane_iota(shape):
    return lax.broadcasted_iota(jnp.int32, shape, len(shape) - 1)


def half_mask(shape):
    return ((lax.broadcasted_iota(jnp.int32, shape, len(shape) - 2) >> 1) & 1) == 1


def roll_y(values, step):
    return pltpu.roll(values, (-16 * step) % 128, values.ndim - 1)


def roll_z(values, step):
    axis = values.ndim - 1
    z_coord = lane_iota(values.shape) & 15
    if step == 1:
        return jnp.where(z_coord == 15, pltpu.roll(values, 15, axis), pltpu.roll(values, 127, axis))
    return jnp.where(z_coord == 0, pltpu.roll(values, 113, axis), pltpu.roll(values, 1, axis))


def shift_yz(values, step_y, step_z):
    if step_y:
        values = roll_y(values, step_y)
    if step_z:
        values = roll_z(values, step_z)
    return values


def swap_halves(values):
    axis = values.ndim - 2
    return jnp.where(
        half_mask(values.shape), pltpu.roll(values, 2, axis), pltpu.roll(values, 6, axis)
    )


def split_roll(values, lead, step):
    along_y = roll_y(values, step)
    along_z = roll_z(values, step)
    first, second = (along_y, along_z) if lead == 2 else (along_z, along_y)
    return jnp.where(half_mask(values.shape), second, first)


def rolled(matrix, lead, step):
    return tuple(split_roll(part, lead, step) for part in matrix)


def mul(first, second, adj_first=False, adj_second=False):
    def column(part, k):
        return jnp.expand_dims(part[k] if adj_first else part[:, k], 1)

    def line(part, k):
        return jnp.expand_dims(part[:, k] if adj_second else part[k], 0)

    sums = [None] * 4
    for k in range(3):
        fr, fi = column(first[0], k), column(first[1], k)
        sr, si = line(second[0], k), line(second[1], k)
        terms = (fr * sr, fi * si, fr * si, fi * sr)
        sums = [t if s is None else s + t for s, t in zip(sums, terms)]
    rr, ii, ri, ir = sums
    real = rr + ii if adj_first != adj_second else rr - ii
    if adj_first and adj_second:
        imag = -(ri + ir)
    elif adj_first:
        imag = ri - ir
    elif adj_second:
        imag = ir - ri
    else:
        imag = ri + ir
    return (real, imag)


def add(first, second):
    return (first[0] + second[0], first[1] + second[1])


def scaled(matrix, factor):
    return (matrix[0] * factor, matrix[1] * factor)


def view(ref, course, dx, dt):
    start = row_of(1 + dx, 1 + dt)
    pair_start = row_of(1 + dt, 1 + dx) - 2
    parts = []
    for part in range(2):
        own = ref[course, part, :, :, pl.ds(start, 8), :]
        other = ref[PAIR[course], part, :, :, pl.ds(pair_start, 8), :]
        parts.append(jnp.where(half_mask(own.shape), other, own))
    return tuple(parts)


def view_at(ref, course, lead, step):
    if lead == 0:
        return view(ref, course, step, 0)
    if lead == 1:
        return view(ref, course, 0, step)
    return rolled(view(ref, course, 0, 0), lead, step)


ORDER = ((2, 3), (0, 1), (0, 2), (0, 3), (2, 0), (2, 1))


def legs_above(ref, course, across):
    return (
        view_at(ref, across, course, 1),
        view_at(ref, course, across, 1),
        view(ref, across, 0, 0),
    )


def legs_below(ref, course, across):
    if across >= 2:
        return (
            view(ref, course, 0, 0),
            view_at(ref, across, course, 1),
            view(ref, across, 0, 0),
        )
    back = (-1, 0) if across == 0 else (0, -1)
    base = view(ref, across, *back)
    if course >= 2:
        ahead = rolled(base, course, 1)
    else:
        step = (back[0] + (course == 0), back[1] + (course == 1))
        ahead = view(ref, across, *step)
    return (view(ref, course, *back), ahead, base)


def third_line(first, second):
    out = []
    for j in range(3):
        p, q = (j + 1) % 3, (j + 2) % 3
        (ar, ai), (br, bi) = first[p], second[q]
        (cr, ci), (dr, di) = first[q], second[p]
        real = (ar * br - ai * bi) - (cr * dr - ci * di)
        imag = (ar * bi + ai * br) - (cr * di + ci * dr)
        out.append((real, -imag))
    return out


def body(
    sizes, links_in, taps_in, active_in, direction_in, out_grad_in, link_grad, kernel_grad,
    links, taps, active, direction, out_grad, grad_out, tap_out,
    ext, send_x0, send_x1, send_t0, send_t1, send_c, recv_x0, recv_x1, recv_t0, recv_t1, recv_c,
    mids, tap_rows, feats, feat_rows, trace_rows, small, k_rows, k_ext, g_ext, g_rows,
    code_ext, x_rows, x_mat, dressed, total, reds,
    in_sems, link_send, link_recv, feat_send, feat_recv, g_send, g_recv, k_send, k_recv,
    red_send, red_recv,
):
    n_space, n_tm, axes, scale = sizes
    n_x, n_y, n_far, n_near = axes
    n_z = n_far * n_near
    my_x, my_t = lax.axis_index("space"), lax.axis_index("tm")

    def device(sx, st):
        return (lax.rem(my_x + sx + n_space, n_space), lax.rem(my_t + st + n_tm, n_tm))

    at_core = lax.rem(my_t, 2)
    at_z = lax.rem(my_x, n_far) * n_near + lax.div(my_t, 2)
    at_y = lax.rem(lax.div(my_x, n_far), n_y)
    at_x = lax.div(my_x, n_far * n_y)

    def z_peer(k):
        z = lax.rem(at_z + k, n_z)
        space = lax.div(my_x, n_far) * n_far + lax.div(z, n_near)
        return (space, lax.rem(z, n_near) * 2 + at_core)

    def y_peer(k):
        y = lax.rem(at_y + k, n_y)
        return ((at_x * n_y + y) * n_far + lax.rem(my_x, n_far), my_t)

    def x_peer(k):
        place = lax.rem(at_x * 2 + at_core + k, 2 * n_x)
        space = lax.div(place, 2) * n_y * n_far + lax.rem(my_x, n_y * n_far)
        return (space, my_t - at_core + lax.rem(place, 2))

    along_z = (z_peer, at_z, n_z)
    along_y = (y_peer, at_y, n_y)
    along_x = (x_peer, at_x * 2 + at_core, 2 * n_x)
    stages = []
    base = 0
    for half in ((along_x, along_z, along_y), (along_x, along_y, along_z)):
        for peer_of, place, count in half:
            stages.append((peer_of, place, count, base))
            base += count
    peers = [device(sx, st) for sx, st in NEIGHBOURS]
    for peer_of, _, count in (along_z, along_y, along_x):
        peers += [peer_of(k) for k in range(1, count)]
    barrier = pltpu.get_barrier_semaphore()
    for peer in peers:
        pl.semaphore_signal(barrier, inc=1, device_id=peer, device_id_type=MESH)

    loads = [
        pltpu.make_async_copy(source, target, in_sems.at[i])
        for i, (source, target) in enumerate(
            (
                (links_in, links), (taps_in, taps), (active_in, active),
                (direction_in, direction), (out_grad_in, out_grad),
            )
        )
    ]
    for load in loads:
        load.start()
    loads[0].wait()

    send_x0[...] = links[:, :, 0:2, :, 1]
    send_x1[...] = links[1:4, :, 0:2, :, 0]
    for x in range(2):
        send_t0[:, :, :, :, x : x + 1, :] = links[:, :, 0:2, :, x, 1:2, :]
        send_t1[0:1, :, :, :, x : x + 1, :] = links[0:1, :, 0:2, :, x, 0:1, :]
        send_t1[1:3, :, :, :, x : x + 1, :] = links[2:4, :, 0:2, :, x, 0:1, :]
    send_c[0] = links[1, :, 0:2, :, 0, 1:2, :]
    send_c[1] = links[0, :, 0:2, :, 1, 0:1, :]

    pl.semaphore_wait(barrier, len(peers))

    def remote(source, target, send_sem, recv_sem, peer):
        return pltpu.make_async_remote_copy(
            src_ref=source, dst_ref=target, send_sem=send_sem, recv_sem=recv_sem,
            device_id=peer, device_id_type=MESH,
        )

    def start_all(copies):
        for copy in copies:
            copy.start()
        return copies

    def finish(copies):
        for copy in copies:
            copy.wait_recv()

    plan = (
        (send_x0, recv_x0, (1, 0)),
        (send_x1, recv_x1, (-1, 0)),
        (send_c.at[0], recv_c.at[0], (-1, 1)),
        (send_c.at[1], recv_c.at[1], (1, -1)),
        (send_t0, recv_t0, (0, 1)),
        (send_t1, recv_t1, (0, -1)),
    )
    link_copies = start_all(
        [
            remote(source, target, link_send.at[i], link_recv.at[i], device(*step))
            for i, (source, target, step) in enumerate(plan)
        ]
    )

    ext[:, :, :, :, pl.ds(row_of(1, 1), 2), :] = links[:, :, :, :, 0]
    ext[:, :, :, :, pl.ds(row_of(2, 1), 2), :] = links[:, :, :, :, 1]

    for load in loads[1:]:
        load.wait()
    diagonal = lax.broadcasted_iota(jnp.int32, (8, 8), 0) == lax.broadcasted_iota(
        jnp.int32, (8, 8), 1
    )

    def spread_taps(j, carry):
        for dxdt in range(9):
            block = taps[dxdt * 9 + j]
            for o in range(4):
                line = jnp.broadcast_to(block[o : o + 1, :], (8, 8))
                column = jnp.sum(jnp.where(diagonal, line, 0.0), axis=1, keepdims=True)
                tap_rows[j, dxdt * 4 + o] = jnp.broadcast_to(column, (8, 128))
        return carry

    lax.fori_loop(0, 9, spread_taps, 0)

    hid = (lax.broadcasted_iota(jnp.int32, (8, 128), 0) >> 1) & 1
    course_of = jnp.concatenate([direction[0], direction[0], direction[1], direction[1]], axis=0)
    moving = jnp.concatenate([active[0], active[0], active[1], active[1]], axis=0)
    moves = moving.astype(F32)
    frozen_third = (1.0 - moves) * (1.0 / 3.0)
    chosen_of = {0: course_of == hid, 2: course_of == hid + 2}

    def stored(index):
        return (mids[index, 0], mids[index, 1])

    def store_mid(index, matrix):
        mids[index, 0] = matrix[0]
        mids[index, 1] = matrix[1]

    staples = {0: None, 2: None}

    def forward(number):
        course, across = ORDER[number]
        b, c, e = legs_above(ext, course, across)
        upper = mul(b, c, adj_second=True)
        store_mid(2 * number, upper)
        above = mul(upper, e, adj_second=True)
        a, b, e = legs_below(ext, course, across)
        lower = mul(a, b)
        store_mid(2 * number + 1, lower)
        below = mul(lower, e, adj_first=True)
        if across >= 2:
            below = rolled(below, across, -1)
        both = add(above, below)
        staples[course] = both if staples[course] is None else add(staples[course], both)

    forward(0)

    finish(link_copies)

    def fill(buffer, courses, put):
        lines = [
            [(buffer[:, 0, i, j], buffer[:, 1, i, j]) for j in range(3)] for i in range(2)
        ]
        lines.append(third_line(*lines))
        for i in range(3):
            for j in range(3):
                for k in range(2):
                    put(courses, k, i, j, lines[i][j][k])

    def put_x(ext_x):
        def put(courses, k, i, j, value):
            for n, course in enumerate(courses):
                ext[course, k, i, j, pl.ds(row_of(ext_x, 1), 2), :] = value[n]

        return put

    def put_t(ext_t):
        def put(courses, k, i, j, value):
            for n, course in enumerate(courses):
                for x in range(2):
                    ext[course, k, i, j, pl.ds(row_of(1 + x, ext_t), 1), :] = value[n, x : x + 1]

        return put

    def put_c(courses, k, i, j, value):
        ext[1, k, i, j, pl.ds(row_of(3, 0), 1), :] = value[0]
        ext[0, k, i, j, pl.ds(row_of(0, 3), 1), :] = value[1]

    fill(recv_x0, (0, 1, 2, 3), put_x(0))
    fill(recv_x1, (1, 2, 3), put_x(3))
    fill(recv_t0, (0, 1, 2, 3), put_t(0))
    fill(recv_t1, (0, 2, 3), put_t(3))
    fill(recv_c, (1, 0), put_c)

    for number in range(1, 6):
        forward(number)

    def trace(part):
        return part[0, 0] + part[1, 1] + part[2, 2]

    cores = {lead: view(ext, lead, 0, 0) for lead in (0, 2)}
    closed = {lead: mul(cores[lead], staples[lead]) for lead in (0, 2)}
    for lead in (0, 2):
        for k in range(2):
            value = trace(closed[lead][k]) * frozen_third
            trace_rows[pl.ds((2 * lead + k) * 8, 8), :] = value
            trace_rows[pl.ds((2 * lead + 2 + k) * 8, 8), :] = swap_halves(value)
    for x in range(2):
        for t in range(2):
            feats[1 + x, 1 + t] = trace_rows[pl.ds(4 * x + t, 8, 8), :]

    def edge(step):
        source = {1: pl.ds(2, 1), -1: pl.ds(1, 1), 0: pl.ds(1, 2)}[step]
        target = {1: pl.ds(0, 1), -1: pl.ds(3, 1), 0: pl.ds(1, 2)}[step]
        return source, target

    def edge_copies(ref, steps, send_sem, recv_sem):
        copies = []
        for i, (sx, st) in enumerate(steps):
            (from_x, to_x), (from_t, to_t) = edge(sx), edge(st)
            copies.append(
                remote(
                    ref.at[from_x, from_t], ref.at[to_x, to_t],
                    send_sem.at[i], recv_sem.at[i], device(sx, st),
                )
            )
        return start_all(copies)

    feat_copies = edge_copies(feats, NEIGHBOURS, feat_send, feat_recv)

    def roll_features(positions):
        for ext_x, ext_t in positions:
            value = feats[ext_x, ext_t]
            for dy in range(3):
                along_y = shift_yz(value, dy - 1, 0)
                for dz in range(3):
                    feat_rows[dy * 3 + dz, ext_x * 4 + ext_t] = shift_yz(along_y, 0, dz - 1)

    inner = [(x, t) for x in (1, 2) for t in (1, 2)]
    outer = [(x, t) for x in range(4) for t in range(4) if (x, t) not in inner]
    roll_features(inner)

    grads = {}
    for lead in (0, 2):
        grads[lead] = tuple(
            jnp.concatenate(
                [
                    out_grad[lead, k, :, :, 0],
                    out_grad[lead + 1, k, :, :, 0],
                    out_grad[lead, k, :, :, 1],
                    out_grad[lead + 1, k, :, :, 1],
                ],
                axis=2,
            )
            for k in range(2)
        )

    def choose(field):
        out = []
        for k in range(2):
            first, second = field[0][k], field[2][k]
            mask_first = jnp.broadcast_to(chosen_of[0].astype(F32), first.shape)
            mask_second = jnp.broadcast_to(chosen_of[2].astype(F32), first.shape)
            picked = first * mask_first + second * mask_second
            out.append(picked + swap_halves(picked))
        return tuple(out)

    def project(matrix):
        real, imag = matrix
        third = trace(imag) * (1.0 / 3.0)
        out = []
        for i, j in ((0, 1), (0, 2), (1, 2)):
            out.append((real[i, j] - real[j, i]) * 0.5)
            out.append((imag[i, j] + imag[j, i]) * 0.5)
        return out + [imag[0, 0] - third, imag[1, 1] - third]

    def expand(parts):
        r01, i01, r02, i02, r12, i12, d0, d1 = parts
        zero = jnp.zeros_like(d0)
        real = jnp.stack(
            [
                jnp.stack([zero, r01, r02]),
                jnp.stack([-r01, zero, r12]),
                jnp.stack([-r02, -r12, zero]),
            ]
        )
        imag = jnp.stack(
            [
                jnp.stack([d0, i01, i02]),
                jnp.stack([i01, d1, i12]),
                jnp.stack([i02, i12, -d0 - d1]),
            ]
        )
        return (real, imag)

    picked_link = choose(cores)
    generator = expand(project(choose(closed)))
    minus = scaled(generator, -1.0)
    powers = [mul(choose(grads), picked_link, adj_second=True)]
    for _ in range(4):
        powers.append(mul(minus, powers[-1]))
    series = [powers[0]]
    for k in range(3):
        series.append(add(powers[k + 1], mul(series[-1], minus)))

    def inner_product(first, second):
        total_sum = None
        for k in range(2):
            for i in range(3):
                for j in range(3):
                    term = first[k][i, j] * second[k][i, j]
                    total_sum = term if total_sum is None else total_sum + term
        return total_sum

    slopes = [inner_product(powers[k], generator) for k in range(4)]
    turns = [project(matrix) for matrix in series]

    small[0] = course_of.astype(F32)

    def conv_step(own):
        def step(j, acc):
            acc = list(acc)
            for dx in range(3):
                for dt in range(3):
                    for o in range(4):
                        tap = None
                        for n in range(4):
                            spot = (n // 2 + dx, n % 2 + dt)
                            if (spot in inner) != own:
                                continue
                            if tap is None:
                                tap = tap_rows[j, (dx * 3 + dt) * 4 + o]
                            term = tap * feat_rows[j, spot[0] * 4 + spot[1]]
                            acc[o * 4 + n] = acc[o * 4 + n] + term
            return tuple(acc)

        return step

    acc = tuple(jnp.zeros((8, 128), F32) for _ in range(16))
    acc = lax.fori_loop(0, 9, conv_step(True), acc)

    finish(feat_copies)
    roll_features(outer)

    acc = lax.fori_loop(0, 9, conv_step(False), acc, unroll=9)
    for n in range(4):
        s = 4 * (n // 2) + n % 2
        course_row = jnp.broadcast_to(small[0, pl.ds(s, 1), :], (8, 128))
        picked = jnp.where(course_row == 0.0, acc[n], 0.0)
        for o in range(1, 4):
            picked = picked + jnp.where(course_row == float(o), acc[o * 4 + n], 0.0)
        field_row = jnp.sum(picked, axis=0, keepdims=True)
        small[1, pl.ds(s, 1), :] = field_row
        small[1, pl.ds(s + 2, 1), :] = field_row
    bent = jnp.tanh(small[1])
    strength = bent * moves
    c1, c2, c3, c4 = slopes
    slope = c1 + strength * (c2 + strength * (c3 * 0.5 + strength * (c4 * (1.0 / 6.0))))
    field_grad = moves * (1.0 - bent * bent) * slope
    code = jnp.where(moving == 1, course_of, -1).astype(F32)
    g_ext[1, 1] = jnp.where(hid == 0, field_grad, code)
    t1, t2, t3, t4 = turns
    for k in range(8):
        poly = t1[k] + strength * (
            t2[k] * 0.5 + strength * (t3[k] * (1.0 / 6.0) + strength * (t4[k] * (1.0 / 24.0)))
        )
        k_rows[pl.ds(8 * k, 8), :] = -strength * poly
    for x in range(2):
        for t in range(2):
            k_ext[1 + x, 1 + t] = k_rows[pl.ds(4 * x + t, 8, 8), :]

    g_copies = start_all(
        [
            remote(
                g_ext.at[1, 1], g_ext.at[1 - sx, 1 - st],
                g_send.at[i], g_recv.at[i], device(sx, st),
            )
            for i, (sx, st) in enumerate(NEIGHBOURS)
        ]
    )
    k_copies = edge_copies(k_ext, FACES + CORNERS, k_send, k_recv)

    sub = lax.broadcasted_iota(jnp.int32, (8, 128), 0).astype(F32)
    rough = field_grad.astype(jnp.bfloat16).astype(F32)
    small[2] = rough
    small[1] = field_grad - rough
    wide = []
    for n in range(4):
        s = 4 * (n // 2) + n % 2
        course_row = jnp.broadcast_to(small[0, pl.ds(s, 1), :], (8, 128))
        rough_row = jnp.broadcast_to(small[2, pl.ds(s, 1), :], (8, 128))
        rest_row = jnp.broadcast_to(small[1, pl.ds(s, 1), :], (8, 128))
        wide.append(
            jnp.where(course_row == sub, rough_row, 0.0)
            + jnp.where(course_row + 4.0 == sub, rest_row, 0.0)
        )
    wide = jnp.concatenate(wide, axis=1).astype(jnp.bfloat16)
    lines = []
    for dx in range(3):
        for dt in range(3):
            for j in range(9):
                lines.append(
                    jnp.concatenate(
                        [feat_rows[j, (n // 2 + dx) * 4 + n % 2 + dt] for n in range(4)], axis=1
                    )
                )
    lines = jnp.concatenate(lines + [jnp.zeros((8, 512), F32)], axis=0)
    lines_high = lines.astype(jnp.bfloat16)
    lines_low = (lines - lines_high.astype(F32)).astype(jnp.bfloat16)
    contract = (((1,), (1,)), ((), ()))
    high_sum = lax.dot_general(wide, lines_high, contract, preferred_element_type=F32)
    low_sum = lax.dot_general(wide, lines_low, contract, preferred_element_type=F32)
    tap_sum = high_sum[0:4] + (high_sum[4:8] + low_sum[0:4])
    total[...] = jnp.zeros((4, 768), F32)
    total[:, 0:656] = tap_sum

    def send_stage(number, value):
        peer_of, place, count, base = stages[number]
        buffer = reds[number]
        buffer[place] = value
        return start_all(
            [
                remote(
                    buffer.at[place], buffer.at[place],
                    red_send.at[base + k], red_recv.at[base + k], peer_of(k),
                )
                for k in range(1, count)
            ]
        )

    def take_stage(number, copies):
        finish(copies)
        buffer = reds[number]
        out = buffer[0]
        for k in range(1, stages[number][2]):
            out = out + buffer[k]
        return out

    copies_a = [send_stage(3 * h, total[:, 384 * h : 384 * h + 384]) for h in range(2)]

    blend = scaled(powers[4], 1.0 / 24.0)
    for k, factor in ((3, 1.0 / 6.0), (2, 0.5), (1, 1.0), (0, 1.0)):
        blend = add(scaled(blend, strength), scaled(powers[k], factor))
    straight = mul(blend, picked_link)

    def spread_blocks(blocks, places):
        mask = half_mask(blocks.shape)
        axis = blocks.ndim - 2
        values = jnp.where(mask, pltpu.roll(blocks, 2, axis), blocks)
        codes = jnp.where(mask, blocks, pltpu.roll(blocks, 6, axis))
        for pair in range(2):
            wanted = jnp.where(mask, 2.0 * pair + 1.0, 2.0 * pair)
            one = jnp.where(codes == wanted, values, 0.0)
            for dy in range(3):
                along_y = shift_yz(one, 1 - dy, 0)
                for dz in range(3):
                    moved = shift_yz(along_y, 0, 1 - dz)
                    for n, (bx, bt) in enumerate(places):
                        g_rows[dy * 3 + dz, pair, bx, bt] = moved[n]

    spots = inner + [(0, 1), (0, 2), (3, 1), (3, 2), (1, 0), (2, 0), (1, 3), (2, 3), (3, 0), (0, 3)]

    def back_step(own):
        def step(j, acc):
            acc = list(acc)
            for o in range(4):
                rows = {}
                for dx in range(3):
                    for dt in range(3):
                        tap = None
                        for n, (ext_x, ext_t) in enumerate(spots):
                            px, pt = ext_x + 2 - dx, ext_t + 2 - dt
                            if (px // 2 == 1 and pt // 2 == 1) != own:
                                continue
                            if tap is None:
                                tap = tap_rows[j, (dx * 3 + dt) * 4 + o]
                            if (px, pt) not in rows:
                                s = 4 * (px % 2) + 2 * (o % 2) + pt % 2
                                rows[px, pt] = jnp.broadcast_to(
                                    g_rows[j, o // 2, px // 2, pt // 2, pl.ds(s, 1), :], (8, 128)
                                )
                            acc[n] = acc[n] + tap * rows[px, pt]
            return tuple(acc)

        return step

    around = [(bx, bt) for bx in range(3) for bt in range(3) if (bx, bt) != (1, 1)]
    spread_blocks(g_ext[1, 1:2], [(1, 1)])
    spot_grad = tuple(jnp.zeros((8, 128), F32) for _ in spots)
    spot_grad = lax.fori_loop(0, 9, back_step(True), spot_grad)

    copies_b = [send_stage(3 * h + 1, take_stage(3 * h, copies_a[h])) for h in range(2)]

    finish(g_copies)
    spread_blocks(jnp.stack([g_ext[bx, bt] for bx, bt in around]), around)
    spot_grad = lax.fori_loop(0, 9, back_step(False), spot_grad, unroll=3)

    finish(k_copies)
    for n, (ext_x, ext_t) in enumerate(spots):
        block_x, block_t = (ext_x + 1) // 2, (ext_t + 1) // 2
        s = 4 * ((ext_x + 1) % 2) + 2 + (ext_t + 1) % 2
        code_row = g_ext[block_x, block_t, pl.ds(s, 1), :]
        code_ext[pl.ds(row_of(ext_x, ext_t), 1), :] = code_row
        merged = jnp.where(
            jnp.broadcast_to(code_row, (8, 128)) >= 0.0,
            k_ext[ext_x, ext_t],
            spot_grad[n] * (1.0 / 3.0),
        )
        x_rows[pl.ds(row_of(ext_x, ext_t), 8, GROWS), :] = merged

    for half in range(2):
        rows = pl.ds(2 + 8 * half, 8)
        code8 = code_ext[rows, :]
        parts = [x_rows[pl.ds(GROWS * k + 2 + 8 * half, 8), :] for k in range(8)]
        still = code8 < 0.0
        for course in range(4):
            turned = expand([jnp.where(code8 == float(course), p, 0.0) for p in parts])
            real, imag = turned
            one_real = jnp.where(still, parts[2 * course], 0.0)
            one_imag = jnp.where(still, parts[2 * course + 1], 0.0)
            zero = jnp.zeros_like(one_real)
            eye_real = jnp.stack(
                [jnp.stack([one_real if i == j else zero for j in range(3)]) for i in range(3)]
            )
            eye_imag = jnp.stack(
                [jnp.stack([one_imag if i == j else zero for j in range(3)]) for i in range(3)]
            )
            matrix = (real + eye_real, imag - eye_imag)
            product = mul(
                matrix, (ext[course, 0, :, :, rows, :], ext[course, 1, :, :, rows, :])
            )
            for k in range(2):
                x_mat[course, k, :, :, rows, :] = matrix[k]
                dressed[course, k, :, :, rows, :] = product[k]

    link_sum = {0: None, 2: None}

    def backward(number):
        course, across = ORDER[number]
        b, c, e = legs_above(ext, course, across)
        db, dc, de = legs_above(dressed, course, across)
        upper = stored(2 * number)
        change = add(mul(db, c, adj_second=True), mul(b, dc, adj_second=True))
        above = add(mul(change, e, adj_second=True), mul(upper, de, adj_second=True))
        a, b, e = legs_below(ext, course, across)
        da, db, de = legs_below(dressed, course, across)
        lower = stored(2 * number + 1)
        change = add(mul(da, b), mul(a, db))
        below = add(mul(change, e, adj_first=True), mul(lower, de, adj_first=True))
        if across >= 2:
            below = rolled(below, across, -1)
        both = add(above, below)
        link_sum[course] = both if link_sum[course] is None else add(link_sum[course], both)

    for number in range(6):
        backward(number)

    for lead in (0, 2):
        both = add(link_sum[lead], mul(staples[lead], view(x_mat, lead, 0, 0)))
        for k in range(2):
            mask = chosen_of[lead]
            for i in range(3):
                for j in range(3):
                    value = jnp.where(mask, straight[k][i, j], grads[lead][k][i, j])
                    value = value + both[0][j, i] if k == 0 else value - both[1][j, i]
                    for x in range(2):
                        grad_out[lead, k, i, j, x] = value[4 * x : 4 * x + 2, :]
                        grad_out[lead + 1, k, i, j, x] = value[4 * x + 2 : 4 * x + 4, :]

    store_links = pltpu.make_async_copy(grad_out, link_grad, in_sems.at[0])
    store_links.start()
    copies_c = [send_stage(3 * h + 2, take_stage(3 * h + 1, copies_b[h])) for h in range(2)]
    for h in range(2):
        total[:, 384 * h : 384 * h + 384] = take_stage(3 * h + 2, copies_c[h]) * scale
    for d in range(81):
        tap_out[d // 27, d // 9 % 3, d // 3 % 3, d % 3] = total[:, d * 8 : d * 8 + 8]
    store_taps = pltpu.make_async_copy(tap_out, kernel_grad, in_sems.at[1])
    store_taps.start()
    store_links.wait()
    store_taps.wait()

    for copy in (
        link_copies + feat_copies + g_copies + k_copies
        + sum(copies_a + copies_b + copies_c, [])
    ):
        copy.wait_send()


def hand_on(link_in, kernel_in, link_out, kernel_out, link_held, kernel_held, sems):
    loads = [
        pltpu.make_async_copy(link_in, link_held, sems.at[0]),
        pltpu.make_async_copy(kernel_in, kernel_held, sems.at[1]),
    ]
    stores = [
        pltpu.make_async_copy(link_held, link_out, sems.at[2]),
        pltpu.make_async_copy(kernel_held, kernel_out, sems.at[3]),
    ]
    for load in loads:
        load.start()
    for load, store in zip(loads, stores):
        load.wait()
        store.start()
    for store in stores:
        store.wait()


def shards(sizes, links, kernel, active, direction, out_grad):
    n_x, n_y, n_far, n_near = sizes[2]
    n_z = n_far * n_near
    counts = (2 * n_x, n_z, n_y, 2 * n_x, n_y, n_z)
    hbm = pl.BlockSpec(memory_space=pltpu.HBM)

    def space(*shape):
        return pltpu.VMEM(shape, F32)

    def sems(count):
        return pltpu.SemaphoreType.DMA((count,))

    link_grad, kernel_grad = pl.pallas_call(
        functools.partial(body, sizes),
        out_shape=(
            jax.ShapeDtypeStruct(links.shape, F32),
            jax.ShapeDtypeStruct(kernel.shape, F32),
        ),
        in_specs=[hbm] * 5,
        out_specs=(hbm, hbm),
        scratch_shapes=[
            space(4, 2, 3, 3, 2, 2, 128),
            space(81, 4, 8),
            pltpu.VMEM((2, 2, 128), jnp.int32),
            pltpu.VMEM((2, 2, 128), jnp.int32),
            space(4, 2, 3, 3, 2, 2, 128),
            space(4, 2, 3, 3, 2, 2, 128),
            space(*kernel.shape),
            space(4, 2, 3, 3, GROWS, 128),
            space(4, 2, 2, 3, 2, 128),
            space(3, 2, 2, 3, 2, 128),
            space(4, 2, 2, 3, 2, 128),
            space(3, 2, 2, 3, 2, 128),
            space(2, 2, 2, 3, 1, 128),
            space(4, 2, 2, 3, 2, 128),
            space(3, 2, 2, 3, 2, 128),
            space(4, 2, 2, 3, 2, 128),
            space(3, 2, 2, 3, 2, 128),
            space(2, 2, 2, 3, 1, 128),
            space(12, 2, 3, 3, 8, 128),
            space(9, 36, 8, 128),
            space(4, 4, 8, 128),
            space(9, 16, 8, 128),
            space(64, 128),
            space(3, 8, 128),
            space(64, 128),
            space(4, 4, 8, 128),
            space(3, 3, 8, 128),
            space(9, 2, 3, 3, 8, 128),
            space(GROWS, 128),
            space(8 * GROWS, 128),
            space(4, 2, 3, 3, GROWS, 128),
            space(4, 2, 3, 3, GROWS, 128),
            space(4, 768),
            [space(count, 4, 384) for count in counts],
            sems(5),
            sems(6), sems(6), sems(8), sems(8), sems(8), sems(8), sems(6), sems(6),
            sems(sum(counts)), sems(sum(counts)),
        ],
        compiler_params=pltpu.CompilerParams(
            collective_id=0, has_side_effects=True, vmem_limit_bytes=60 * 1024 * 1024
        ),
    )(links, kernel.reshape(81, 4, 8), active, direction, out_grad)
    return pl.pallas_call(
        hand_on,
        out_shape=(
            jax.ShapeDtypeStruct(links.shape, F32),
            jax.ShapeDtypeStruct(kernel.shape, F32),
        ),
        in_specs=[hbm] * 2,
        out_specs=(hbm, hbm),
        scratch_shapes=[space(*links.shape), space(*kernel.shape), sems(4)],
        compiler_params=pltpu.CompilerParams(vmem_limit_bytes=60 * 1024 * 1024),
    )(link_grad, kernel_grad)


def solution(mesh):
    n_space, n_tm = mesh.shape["space"], mesh.shape["tm"]
    n_far = 2
    n_x = max(1, n_space // (8 * n_far))
    axes = (n_x, n_space // (n_x * n_far), n_far, n_tm // 2)
    sites = n_space * n_tm * 4 * 128
    placed = (
        P(None, None, None, None, "space", "tm", None),
        P(),
        P("space", "tm", None),
        P("space", "tm", None),
        P(None, None, None, None, "space", "tm", None),
    )
    return jax.shard_map(
        functools.partial(shards, (n_space, n_tm, axes, 1.0 / math.sqrt(sites))),
        mesh=mesh,
        in_specs=placed,
        out_specs=(P(None, None, None, None, "space", "tm", None), P()),
        check_vma=False,
    )
```

```python
import functools
import math

import jax
import jax.numpy as jnp
from jax import lax
from jax.experimental import pallas as pl
from jax.experimental.pallas import tpu as pltpu
from jax.sharding import PartitionSpec as P

PAIR = (1, 0, 3, 2)
MESH = pl.DeviceIdType.MESH
F32 = jnp.float32
NEIGHBOURS = tuple((sx, st) for sx in (-1, 0, 1) for st in (-1, 0, 1) if (sx, st) != (0, 0))
FACES = ((-1, 0), (1, 0), (0, -1), (0, 1))
CORNERS = ((1, -1), (-1, 1))
GROWS = 24


def row_of(ext_x, ext_t):
    return 2 + 4 * ext_x + ext_t


def lane_iota(shape):
    return lax.broadcasted_iota(jnp.int32, shape, len(shape) - 1)


def half_mask(shape):
    return ((lax.broadcasted_iota(jnp.int32, shape, len(shape) - 2) >> 1) & 1) == 1


def roll_y(values, step):
    return pltpu.roll(values, (-16 * step) % 128, values.ndim - 1)


def roll_z(values, step):
    axis = values.ndim - 1
    z_coord = lane_iota(values.shape) & 15
    if step == 1:
        return jnp.where(z_coord == 15, pltpu.roll(values, 15, axis), pltpu.roll(values, 127, axis))
    return jnp.where(z_coord == 0, pltpu.roll(values, 113, axis), pltpu.roll(values, 1, axis))


def shift_yz(values, step_y, step_z):
    if step_y:
        values = roll_y(values, step_y)
    if step_z:
        values = roll_z(values, step_z)
    return values


def swap_halves(values):
    axis = values.ndim - 2
    return jnp.where(
        half_mask(values.shape), pltpu.roll(values, 2, axis), pltpu.roll(values, 6, axis)
    )


def split_roll(values, lead, step):
    along_y = roll_y(values, step)
    along_z = roll_z(values, step)
    first, second = (along_y, along_z) if lead == 2 else (along_z, along_y)
    return jnp.where(half_mask(values.shape), second, first)


def rolled(matrix, lead, step):
    return tuple(split_roll(part, lead, step) for part in matrix)


def mul(first, second, adj_first=False, adj_second=False):
    def column(part, k):
        return jnp.expand_dims(part[k] if adj_first else part[:, k], 1)

    def line(part, k):
        return jnp.expand_dims(part[:, k] if adj_second else part[k], 0)

    sums = [None] * 4
    for k in range(3):
        fr, fi = column(first[0], k), column(first[1], k)
        sr, si = line(second[0], k), line(second[1], k)
        terms = (fr * sr, fi * si, fr * si, fi * sr)
        sums = [t if s is None else s + t for s, t in zip(sums, terms)]
    rr, ii, ri, ir = sums
    real = rr + ii if adj_first != adj_second else rr - ii
    if adj_first and adj_second:
        imag = -(ri + ir)
    elif adj_first:
        imag = ri - ir
    elif adj_second:
        imag = ir - ri
    else:
        imag = ri + ir
    return (real, imag)


def add(first, second):
    return (first[0] + second[0], first[1] + second[1])


def scaled(matrix, factor):
    return (matrix[0] * factor, matrix[1] * factor)


def view(ref, course, dx, dt):
    start = row_of(1 + dx, 1 + dt)
    pair_start = row_of(1 + dt, 1 + dx) - 2
    parts = []
    for part in range(2):
        own = ref[course, part, :, :, pl.ds(start, 8), :]
        other = ref[PAIR[course], part, :, :, pl.ds(pair_start, 8), :]
        parts.append(jnp.where(half_mask(own.shape), other, own))
    return tuple(parts)


def view_at(ref, course, lead, step):
    if lead == 0:
        return view(ref, course, step, 0)
    if lead == 1:
        return view(ref, course, 0, step)
    return rolled(view(ref, course, 0, 0), lead, step)


ORDER = ((2, 3), (0, 1), (0, 2), (0, 3), (2, 0), (2, 1))


def legs_above(ref, course, across):
    return (
        view_at(ref, across, course, 1),
        view_at(ref, course, across, 1),
        view(ref, across, 0, 0),
    )


def legs_below(ref, course, across):
    if across >= 2:
        return (
            view(ref, course, 0, 0),
            view_at(ref, across, course, 1),
            view(ref, across, 0, 0),
        )
    back = (-1, 0) if across == 0 else (0, -1)
    base = view(ref, across, *back)
    if course >= 2:
        ahead = rolled(base, course, 1)
    else:
        step = (back[0] + (course == 0), back[1] + (course == 1))
        ahead = view(ref, across, *step)
    return (view(ref, course, *back), ahead, base)


def third_line(first, second):
    out = []
    for j in range(3):
        p, q = (j + 1) % 3, (j + 2) % 3
        (ar, ai), (br, bi) = first[p], second[q]
        (cr, ci), (dr, di) = first[q], second[p]
        real = (ar * br - ai * bi) - (cr * dr - ci * di)
        imag = (ar * bi + ai * br) - (cr * di + ci * dr)
        out.append((real, -imag))
    return out


def body(
    sizes, links_in, taps_in, active_in, direction_in, out_grad_in, link_grad, kernel_grad,
    links, taps, active, direction, out_grad, grad_out, tap_out,
    ext, send_x0, send_x1, send_t0, send_t1, send_c, recv_x0, recv_x1, recv_t0, recv_t1, recv_c,
    mids, tap_rows, feats, feat_rows, trace_rows, small, k_rows, k_ext, g_ext, g_rows,
    code_ext, x_rows, x_mat, dressed, total, reds,
    in_sems, link_send, link_recv, feat_send, feat_recv, g_send, g_recv, k_send, k_recv,
    red_send, red_recv,
):
    n_space, n_tm, axes, scale = sizes
    n_x, n_y, n_far, n_near = axes
    n_z = n_far * n_near
    my_x, my_t = lax.axis_index("space"), lax.axis_index("tm")

    def device(sx, st):
        return (lax.rem(my_x + sx + n_space, n_space), lax.rem(my_t + st + n_tm, n_tm))

    at_core = lax.rem(my_t, 2)
    at_z = lax.rem(my_x, n_far) * n_near + lax.div(my_t, 2)
    at_y = lax.rem(lax.div(my_x, n_far), n_y)
    at_x = lax.div(my_x, n_far * n_y)

    def z_peer(k):
        z = lax.rem(at_z + k, n_z)
        space = lax.div(my_x, n_far) * n_far + lax.div(z, n_near)
        return (space, lax.rem(z, n_near) * 2 + at_core)

    def y_peer(k):
        y = lax.rem(at_y + k, n_y)
        return ((at_x * n_y + y) * n_far + lax.rem(my_x, n_far), my_t)

    def x_peer(k):
        place = lax.rem(at_x * 2 + at_core + k, 2 * n_x)
        space = lax.div(place, 2) * n_y * n_far + lax.rem(my_x, n_y * n_far)
        return (space, my_t - at_core + lax.rem(place, 2))

    along_z = (z_peer, at_z, n_z)
    along_y = (y_peer, at_y, n_y)
    along_x = (x_peer, at_x * 2 + at_core, 2 * n_x)
    stages = []
    base = 0
    for half in ((along_x, along_z, along_y), (along_x, along_y, along_z)):
        for peer_of, place, count in half:
            stages.append((peer_of, place, count, base))
            base += count
    peers = [device(sx, st) for sx, st in NEIGHBOURS]
    for peer_of, _, count in (along_z, along_y, along_x):
        peers += [peer_of(k) for k in range(1, count)]
    barrier = pltpu.get_barrier_semaphore()
    for peer in peers:
        pl.semaphore_signal(barrier, inc=1, device_id=peer, device_id_type=MESH)

    loads = [
        pltpu.make_async_copy(source, target, in_sems.at[i])
        for i, (source, target) in enumerate(
            (
                (links_in, links), (taps_in, taps), (active_in, active),
                (direction_in, direction), (out_grad_in, out_grad),
            )
        )
    ]
    for load in loads:
        load.start()
    loads[0].wait()

    send_x0[...] = links[:, :, 0:2, :, 1]
    send_x1[...] = links[1:4, :, 0:2, :, 0]
    for x in range(2):
        send_t0[:, :, :, :, x : x + 1, :] = links[:, :, 0:2, :, x, 1:2, :]
        send_t1[0:1, :, :, :, x : x + 1, :] = links[0:1, :, 0:2, :, x, 0:1, :]
        send_t1[1:3, :, :, :, x : x + 1, :] = links[2:4, :, 0:2, :, x, 0:1, :]
    send_c[0] = links[1, :, 0:2, :, 0, 1:2, :]
    send_c[1] = links[0, :, 0:2, :, 1, 0:1, :]

    pl.semaphore_wait(barrier, len(peers))

    def remote(source, target, send_sem, recv_sem, peer):
        return pltpu.make_async_remote_copy(
            src_ref=source, dst_ref=target, send_sem=send_sem, recv_sem=recv_sem,
            device_id=peer, device_id_type=MESH,
        )

    def start_all(copies):
        for copy in copies:
            copy.start()
        return copies

    def finish(copies):
        for copy in copies:
            copy.wait_recv()

    plan = (
        (send_x0, recv_x0, (1, 0)),
        (send_x1, recv_x1, (-1, 0)),
        (send_c.at[0], recv_c.at[0], (-1, 1)),
        (send_c.at[1], recv_c.at[1], (1, -1)),
        (send_t0, recv_t0, (0, 1)),
        (send_t1, recv_t1, (0, -1)),
    )
    link_copies = start_all(
        [
            remote(source, target, link_send.at[i], link_recv.at[i], device(*step))
            for i, (source, target, step) in enumerate(plan)
        ]
    )

    ext[:, :, :, :, pl.ds(row_of(1, 1), 2), :] = links[:, :, :, :, 0]
    ext[:, :, :, :, pl.ds(row_of(2, 1), 2), :] = links[:, :, :, :, 1]

    for load in loads[1:]:
        load.wait()
    diagonal = lax.broadcasted_iota(jnp.int32, (8, 8), 0) == lax.broadcasted_iota(
        jnp.int32, (8, 8), 1
    )

    def spread_taps(j, carry):
        for dxdt in range(9):
            block = taps[dxdt * 9 + j]
            for o in range(4):
                line = jnp.broadcast_to(block[o : o + 1, :], (8, 8))
                column = jnp.sum(jnp.where(diagonal, line, 0.0), axis=1, keepdims=True)
                tap_rows[j, dxdt * 4 + o] = jnp.broadcast_to(column, (8, 128))
        return carry

    lax.fori_loop(0, 9, spread_taps, 0)

    hid = (lax.broadcasted_iota(jnp.int32, (8, 128), 0) >> 1) & 1
    course_of = jnp.concatenate([direction[0], direction[0], direction[1], direction[1]], axis=0)
    moving = jnp.concatenate([active[0], active[0], active[1], active[1]], axis=0)
    moves = moving.astype(F32)
    frozen_third = (1.0 - moves) * (1.0 / 3.0)
    chosen_of = {0: course_of == hid, 2: course_of == hid + 2}

    def stored(index):
        return (mids[index, 0], mids[index, 1])

    def store_mid(index, matrix):
        mids[index, 0] = matrix[0]
        mids[index, 1] = matrix[1]

    staples = {0: None, 2: None}

    def forward(number):
        course, across = ORDER[number]
        b, c, e = legs_above(ext, course, across)
        upper = mul(b, c, adj_second=True)
        store_mid(2 * number, upper)
        above = mul(upper, e, adj_second=True)
        a, b, e = legs_below(ext, course, across)
        lower = mul(a, b)
        store_mid(2 * number + 1, lower)
        below = mul(lower, e, adj_first=True)
        if across >= 2:
            below = rolled(below, across, -1)
        both = add(above, below)
        staples[course] = both if staples[course] is None else add(staples[course], both)

    forward(0)

    finish(link_copies)

    def fill(buffer, courses, put):
        lines = [
            [(buffer[:, 0, i, j], buffer[:, 1, i, j]) for j in range(3)] for i in range(2)
        ]
        lines.append(third_line(*lines))
        for i in range(3):
            for j in range(3):
                for k in range(2):
                    put(courses, k, i, j, lines[i][j][k])

    def put_x(ext_x):
        def put(courses, k, i, j, value):
            for n, course in enumerate(courses):
                ext[course, k, i, j, pl.ds(row_of(ext_x, 1), 2), :] = value[n]

        return put

    def put_t(ext_t):
        def put(courses, k, i, j, value):
            for n, course in enumerate(courses):
                for x in range(2):
                    ext[course, k, i, j, pl.ds(row_of(1 + x, ext_t), 1), :] = value[n, x : x + 1]

        return put

    def put_c(courses, k, i, j, value):
        ext[1, k, i, j, pl.ds(row_of(3, 0), 1), :] = value[0]
        ext[0, k, i, j, pl.ds(row_of(0, 3), 1), :] = value[1]

    fill(recv_x0, (0, 1, 2, 3), put_x(0))
    fill(recv_x1, (1, 2, 3), put_x(3))
    fill(recv_t0, (0, 1, 2, 3), put_t(0))
    fill(recv_t1, (0, 2, 3), put_t(3))
    fill(recv_c, (1, 0), put_c)

    for number in range(1, 6):
        forward(number)

    def trace(part):
        return part[0, 0] + part[1, 1] + part[2, 2]

    cores = {lead: view(ext, lead, 0, 0) for lead in (0, 2)}
    closed = {lead: mul(cores[lead], staples[lead]) for lead in (0, 2)}
    for lead in (0, 2):
        for k in range(2):
            value = trace(closed[lead][k]) * frozen_third
            trace_rows[pl.ds((2 * lead + k) * 8, 8), :] = value
            trace_rows[pl.ds((2 * lead + 2 + k) * 8, 8), :] = swap_halves(value)
    for x in range(2):
        for t in range(2):
            feats[1 + x, 1 + t] = trace_rows[pl.ds(4 * x + t, 8, 8), :]

    def edge(step):
        source = {1: pl.ds(2, 1), -1: pl.ds(1, 1), 0: pl.ds(1, 2)}[step]
        target = {1: pl.ds(0, 1), -1: pl.ds(3, 1), 0: pl.ds(1, 2)}[step]
        return source, target

    def edge_copies(ref, steps, send_sem, recv_sem):
        copies = []
        for i, (sx, st) in enumerate(steps):
            (from_x, to_x), (from_t, to_t) = edge(sx), edge(st)
            copies.append(
                remote(
                    ref.at[from_x, from_t], ref.at[to_x, to_t],
                    send_sem.at[i], recv_sem.at[i], device(sx, st),
                )
            )
        return start_all(copies)

    feat_copies = edge_copies(feats, NEIGHBOURS, feat_send, feat_recv)

    def roll_features(positions):
        for ext_x, ext_t in positions:
            value = feats[ext_x, ext_t]
            for dy in range(3):
                along_y = shift_yz(value, dy - 1, 0)
                for dz in range(3):
                    feat_rows[dy * 3 + dz, ext_x * 4 + ext_t] = shift_yz(along_y, 0, dz - 1)

    inner = [(x, t) for x in (1, 2) for t in (1, 2)]
    outer = [(x, t) for x in range(4) for t in range(4) if (x, t) not in inner]
    roll_features(inner)

    grads = {}
    for lead in (0, 2):
        grads[lead] = tuple(
            jnp.concatenate(
                [
                    out_grad[lead, k, :, :, 0],
                    out_grad[lead + 1, k, :, :, 0],
                    out_grad[lead, k, :, :, 1],
                    out_grad[lead + 1, k, :, :, 1],
                ],
                axis=2,
            )
            for k in range(2)
        )

    def choose(field):
        out = []
        for k in range(2):
            first, second = field[0][k], field[2][k]
            mask_first = jnp.broadcast_to(chosen_of[0].astype(F32), first.shape)
            mask_second = jnp.broadcast_to(chosen_of[2].astype(F32), first.shape)
            picked = first * mask_first + second * mask_second
            out.append(picked + swap_halves(picked))
        return tuple(out)

    def project(matrix):
        real, imag = matrix
        third = trace(imag) * (1.0 / 3.0)
        out = []
        for i, j in ((0, 1), (0, 2), (1, 2)):
            out.append((real[i, j] - real[j, i]) * 0.5)
            out.append((imag[i, j] + imag[j, i]) * 0.5)
        return out + [imag[0, 0] - third, imag[1, 1] - third]

    def expand(parts):
        r01, i01, r02, i02, r12, i12, d0, d1 = parts
        zero = jnp.zeros_like(d0)
        real = jnp.stack(
            [
                jnp.stack([zero, r01, r02]),
                jnp.stack([-r01, zero, r12]),
                jnp.stack([-r02, -r12, zero]),
            ]
        )
        imag = jnp.stack(
            [
                jnp.stack([d0, i01, i02]),
                jnp.stack([i01, d1, i12]),
                jnp.stack([i02, i12, -d0 - d1]),
            ]
        )
        return (real, imag)

    picked_link = choose(cores)
    generator = expand(project(choose(closed)))
    minus = scaled(generator, -1.0)
    powers = [mul(choose(grads), picked_link, adj_second=True)]
    for _ in range(4):
        powers.append(mul(minus, powers[-1]))
    series = [powers[0]]
    for k in range(3):
        series.append(add(powers[k + 1], mul(series[-1], minus)))

    def inner_product(first, second):
        total_sum = None
        for k in range(2):
            for i in range(3):
                for j in range(3):
                    term = first[k][i, j] * second[k][i, j]
                    total_sum = term if total_sum is None else total_sum + term
        return total_sum

    slopes = [inner_product(powers[k], generator) for k in range(4)]
    turns = [project(matrix) for matrix in series]

    small[0] = course_of.astype(F32)

    def conv_step(own):
        def step(j, acc):
            acc = list(acc)
            for dx in range(3):
                for dt in range(3):
                    for o in range(4):
                        tap = None
                        for n in range(4):
                            spot = (n // 2 + dx, n % 2 + dt)
                            if (spot in inner) != own:
                                continue
                            if tap is None:
                                tap = tap_rows[j, (dx * 3 + dt) * 4 + o]
                            term = tap * feat_rows[j, spot[0] * 4 + spot[1]]
                            acc[o * 4 + n] = acc[o * 4 + n] + term
            return tuple(acc)

        return step

    acc = tuple(jnp.zeros((8, 128), F32) for _ in range(16))
    acc = lax.fori_loop(0, 9, conv_step(True), acc)

    finish(feat_copies)
    roll_features(outer)

    acc = lax.fori_loop(0, 9, conv_step(False), acc, unroll=9)
    for n in range(4):
        s = 4 * (n // 2) + n % 2
        course_row = jnp.broadcast_to(small[0, pl.ds(s, 1), :], (8, 128))
        picked = jnp.where(course_row == 0.0, acc[n], 0.0)
        for o in range(1, 4):
            picked = picked + jnp.where(course_row == float(o), acc[o * 4 + n], 0.0)
        field_row = jnp.sum(picked, axis=0, keepdims=True)
        small[1, pl.ds(s, 1), :] = field_row
        small[1, pl.ds(s + 2, 1), :] = field_row
    bent = jnp.tanh(small[1])
    strength = bent * moves
    c1, c2, c3, c4 = slopes
    slope = c1 + strength * (c2 + strength * (c3 * 0.5 + strength * (c4 * (1.0 / 6.0))))
    field_grad = moves * (1.0 - bent * bent) * slope
    code = jnp.where(moving == 1, course_of, -1).astype(F32)
    sub = lax.broadcasted_iota(jnp.int32, (8, 128), 0).astype(F32)
    rough = field_grad.astype(jnp.bfloat16).astype(F32)
    small[2] = rough
    small[1] = field_grad - rough
    wide = []
    for n in range(4):
        s = 4 * (n // 2) + n % 2
        course_row = jnp.broadcast_to(small[0, pl.ds(s, 1), :], (8, 128))
        rough_row = jnp.broadcast_to(small[2, pl.ds(s, 1), :], (8, 128))
        rest_row = jnp.broadcast_to(small[1, pl.ds(s, 1), :], (8, 128))
        wide.append(
            jnp.where(course_row == sub, rough_row, 0.0)
            + jnp.where(course_row + 4.0 == sub, rest_row, 0.0)
        )
    wide = jnp.concatenate(wide, axis=1).astype(jnp.bfloat16)
    lines = []
    for dx in range(3):
        for dt in range(3):
            for j in range(9):
                lines.append(
                    jnp.concatenate(
                        [feat_rows[j, (n // 2 + dx) * 4 + n % 2 + dt] for n in range(4)], axis=1
                    )
                )
    lines = jnp.concatenate(lines + [jnp.zeros((8, 512), F32)], axis=0)
    lines_high = lines.astype(jnp.bfloat16)
    lines_low = (lines - lines_high.astype(F32)).astype(jnp.bfloat16)
    contract = (((1,), (1,)), ((), ()))
    high_sum = lax.dot_general(wide, lines_high, contract, preferred_element_type=F32)
    low_sum = lax.dot_general(wide, lines_low, contract, preferred_element_type=F32)
    tap_sum = high_sum[0:4] + (high_sum[4:8] + low_sum[0:4])
    total[...] = jnp.zeros((4, 768), F32)
    total[:, 0:656] = tap_sum

    def send_stage(number, value):
        peer_of, place, count, base = stages[number]
        buffer = reds[number]
        buffer[place] = value
        return start_all(
            [
                remote(
                    buffer.at[place], buffer.at[place],
                    red_send.at[base + k], red_recv.at[base + k], peer_of(k),
                )
                for k in range(1, count)
            ]
        )

    def take_stage(number, copies):
        finish(copies)
        buffer = reds[number]
        out = buffer[0]
        for k in range(1, stages[number][2]):
            out = out + buffer[k]
        return out

    copies_a = [send_stage(3 * h, total[:, 384 * h : 384 * h + 384]) for h in range(2)]

    g_ext[1, 1] = jnp.where(hid == 0, field_grad, code)
    t1, t2, t3, t4 = turns
    for k in range(8):
        poly = t1[k] + strength * (
            t2[k] * 0.5 + strength * (t3[k] * (1.0 / 6.0) + strength * (t4[k] * (1.0 / 24.0)))
        )
        k_rows[pl.ds(8 * k, 8), :] = -strength * poly
    for x in range(2):
        for t in range(2):
            k_ext[1 + x, 1 + t] = k_rows[pl.ds(4 * x + t, 8, 8), :]

    g_copies = start_all(
        [
            remote(
                g_ext.at[1, 1], g_ext.at[1 - sx, 1 - st],
                g_send.at[i], g_recv.at[i], device(sx, st),
            )
            for i, (sx, st) in enumerate(NEIGHBOURS)
        ]
    )
    k_copies = edge_copies(k_ext, FACES + CORNERS, k_send, k_recv)

    blend = scaled(powers[4], 1.0 / 24.0)
    for k, factor in ((3, 1.0 / 6.0), (2, 0.5), (1, 1.0), (0, 1.0)):
        blend = add(scaled(blend, strength), scaled(powers[k], factor))
    straight = mul(blend, picked_link)

    def spread_blocks(blocks, places):
        mask = half_mask(blocks.shape)
        axis = blocks.ndim - 2
        values = jnp.where(mask, pltpu.roll(blocks, 2, axis), blocks)
        codes = jnp.where(mask, blocks, pltpu.roll(blocks, 6, axis))
        for pair in range(2):
            wanted = jnp.where(mask, 2.0 * pair + 1.0, 2.0 * pair)
            one = jnp.where(codes == wanted, values, 0.0)
            for dy in range(3):
                along_y = shift_yz(one, 1 - dy, 0)
                for dz in range(3):
                    moved = shift_yz(along_y, 0, 1 - dz)
                    for n, (bx, bt) in enumerate(places):
                        g_rows[dy * 3 + dz, pair, bx, bt] = moved[n]

    spots = inner + [(0, 1), (0, 2), (3, 1), (3, 2), (1, 0), (2, 0), (1, 3), (2, 3), (3, 0), (0, 3)]

    def back_step(own):
        def step(j, acc):
            acc = list(acc)
            for o in range(4):
                rows = {}
                for dx in range(3):
                    for dt in range(3):
                        tap = None
                        for n, (ext_x, ext_t) in enumerate(spots):
                            px, pt = ext_x + 2 - dx, ext_t + 2 - dt
                            if (px // 2 == 1 and pt // 2 == 1) != own:
                                continue
                            if tap is None:
                                tap = tap_rows[j, (dx * 3 + dt) * 4 + o]
                            if (px, pt) not in rows:
                                s = 4 * (px % 2) + 2 * (o % 2) + pt % 2
                                rows[px, pt] = jnp.broadcast_to(
                                    g_rows[j, o // 2, px // 2, pt // 2, pl.ds(s, 1), :], (8, 128)
                                )
                            acc[n] = acc[n] + tap * rows[px, pt]
            return tuple(acc)

        return step

    around = [(bx, bt) for bx in range(3) for bt in range(3) if (bx, bt) != (1, 1)]
    spread_blocks(g_ext[1, 1:2], [(1, 1)])
    spot_grad = tuple(jnp.zeros((8, 128), F32) for _ in spots)
    spot_grad = lax.fori_loop(0, 9, back_step(True), spot_grad)

    copies_b = [send_stage(3 * h + 1, take_stage(3 * h, copies_a[h])) for h in range(2)]

    finish(g_copies)
    spread_blocks(jnp.stack([g_ext[bx, bt] for bx, bt in around]), around)
    spot_grad = lax.fori_loop(0, 9, back_step(False), spot_grad, unroll=3)

    finish(k_copies)
    for n, (ext_x, ext_t) in enumerate(spots):
        block_x, block_t = (ext_x + 1) // 2, (ext_t + 1) // 2
        s = 4 * ((ext_x + 1) % 2) + 2 + (ext_t + 1) % 2
        code_row = g_ext[block_x, block_t, pl.ds(s, 1), :]
        code_ext[pl.ds(row_of(ext_x, ext_t), 1), :] = code_row
        merged = jnp.where(
            jnp.broadcast_to(code_row, (8, 128)) >= 0.0,
            k_ext[ext_x, ext_t],
            spot_grad[n] * (1.0 / 3.0),
        )
        x_rows[pl.ds(row_of(ext_x, ext_t), 8, GROWS), :] = merged

    for half in range(2):
        rows = pl.ds(2 + 8 * half, 8)
        code8 = code_ext[rows, :]
        parts = [x_rows[pl.ds(GROWS * k + 2 + 8 * half, 8), :] for k in range(8)]
        still = code8 < 0.0
        for course in range(4):
            turned = expand([jnp.where(code8 == float(course), p, 0.0) for p in parts])
            real, imag = turned
            one_real = jnp.where(still, parts[2 * course], 0.0)
            one_imag = jnp.where(still, parts[2 * course + 1], 0.0)
            zero = jnp.zeros_like(one_real)
            eye_real = jnp.stack(
                [jnp.stack([one_real if i == j else zero for j in range(3)]) for i in range(3)]
            )
            eye_imag = jnp.stack(
                [jnp.stack([one_imag if i == j else zero for j in range(3)]) for i in range(3)]
            )
            matrix = (real + eye_real, imag - eye_imag)
            product = mul(
                matrix, (ext[course, 0, :, :, rows, :], ext[course, 1, :, :, rows, :])
            )
            for k in range(2):
                x_mat[course, k, :, :, rows, :] = matrix[k]
                dressed[course, k, :, :, rows, :] = product[k]

    link_sum = {0: None, 2: None}

    def backward(number):
        course, across = ORDER[number]
        b, c, e = legs_above(ext, course, across)
        db, dc, de = legs_above(dressed, course, across)
        upper = stored(2 * number)
        change = add(mul(db, c, adj_second=True), mul(b, dc, adj_second=True))
        above = add(mul(change, e, adj_second=True), mul(upper, de, adj_second=True))
        a, b, e = legs_below(ext, course, across)
        da, db, de = legs_below(dressed, course, across)
        lower = stored(2 * number + 1)
        change = add(mul(da, b), mul(a, db))
        below = add(mul(change, e, adj_first=True), mul(lower, de, adj_first=True))
        if across >= 2:
            below = rolled(below, across, -1)
        both = add(above, below)
        link_sum[course] = both if link_sum[course] is None else add(link_sum[course], both)

    for number in range(5):
        backward(number)

    copies_c = [send_stage(3 * h + 2, take_stage(3 * h + 1, copies_b[h])) for h in range(2)]

    backward(5)

    for lead in (0, 2):
        both = add(link_sum[lead], mul(staples[lead], view(x_mat, lead, 0, 0)))
        for k in range(2):
            mask = chosen_of[lead]
            for i in range(3):
                for j in range(3):
                    value = jnp.where(mask, straight[k][i, j], grads[lead][k][i, j])
                    value = value + both[0][j, i] if k == 0 else value - both[1][j, i]
                    for x in range(2):
                        grad_out[lead, k, i, j, x] = value[4 * x : 4 * x + 2, :]
                        grad_out[lead + 1, k, i, j, x] = value[4 * x + 2 : 4 * x + 4, :]

    store_links = pltpu.make_async_copy(grad_out, link_grad, in_sems.at[0])
    store_links.start()
    for h in range(2):
        total[:, 384 * h : 384 * h + 384] = take_stage(3 * h + 2, copies_c[h]) * scale
    for d in range(81):
        tap_out[d // 27, d // 9 % 3, d // 3 % 3, d % 3] = total[:, d * 8 : d * 8 + 8]
    store_taps = pltpu.make_async_copy(tap_out, kernel_grad, in_sems.at[1])
    store_taps.start()
    store_links.wait()
    store_taps.wait()

    for copy in (
        link_copies + feat_copies + g_copies + k_copies
        + sum(copies_a + copies_b + copies_c, [])
    ):
        copy.wait_send()


def hand_on(link_in, kernel_in, link_out, kernel_out, link_held, kernel_held, sems):
    loads = [
        pltpu.make_async_copy(link_in, link_held, sems.at[0]),
        pltpu.make_async_copy(kernel_in, kernel_held, sems.at[1]),
    ]
    stores = [
        pltpu.make_async_copy(link_held, link_out, sems.at[2]),
        pltpu.make_async_copy(kernel_held, kernel_out, sems.at[3]),
    ]
    for load in loads:
        load.start()
    for load, store in zip(loads, stores):
        load.wait()
        store.start()
    for store in stores:
        store.wait()


def shards(sizes, links, kernel, active, direction, out_grad):
    n_x, n_y, n_far, n_near = sizes[2]
    n_z = n_far * n_near
    counts = (2 * n_x, n_z, n_y, 2 * n_x, n_y, n_z)
    hbm = pl.BlockSpec(memory_space=pltpu.HBM)

    def space(*shape):
        return pltpu.VMEM(shape, F32)

    def sems(count):
        return pltpu.SemaphoreType.DMA((count,))

    link_grad, kernel_grad = pl.pallas_call(
        functools.partial(body, sizes),
        out_shape=(
            jax.ShapeDtypeStruct(links.shape, F32),
            jax.ShapeDtypeStruct(kernel.shape, F32),
        ),
        in_specs=[hbm] * 5,
        out_specs=(hbm, hbm),
        scratch_shapes=[
            space(4, 2, 3, 3, 2, 2, 128),
            space(81, 4, 8),
            pltpu.VMEM((2, 2, 128), jnp.int32),
            pltpu.VMEM((2, 2, 128), jnp.int32),
            space(4, 2, 3, 3, 2, 2, 128),
            space(4, 2, 3, 3, 2, 2, 128),
            space(*kernel.shape),
            space(4, 2, 3, 3, GROWS, 128),
            space(4, 2, 2, 3, 2, 128),
            space(3, 2, 2, 3, 2, 128),
            space(4, 2, 2, 3, 2, 128),
            space(3, 2, 2, 3, 2, 128),
            space(2, 2, 2, 3, 1, 128),
            space(4, 2, 2, 3, 2, 128),
            space(3, 2, 2, 3, 2, 128),
            space(4, 2, 2, 3, 2, 128),
            space(3, 2, 2, 3, 2, 128),
            space(2, 2, 2, 3, 1, 128),
            space(12, 2, 3, 3, 8, 128),
            space(9, 36, 8, 128),
            space(4, 4, 8, 128),
            space(9, 16, 8, 128),
            space(64, 128),
            space(3, 8, 128),
            space(64, 128),
            space(4, 4, 8, 128),
            space(3, 3, 8, 128),
            space(9, 2, 3, 3, 8, 128),
            space(GROWS, 128),
            space(8 * GROWS, 128),
            space(4, 2, 3, 3, GROWS, 128),
            space(4, 2, 3, 3, GROWS, 128),
            space(4, 768),
            [space(count, 4, 384) for count in counts],
            sems(5),
            sems(6), sems(6), sems(8), sems(8), sems(8), sems(8), sems(6), sems(6),
            sems(sum(counts)), sems(sum(counts)),
        ],
        compiler_params=pltpu.CompilerParams(
            collective_id=0, has_side_effects=True, vmem_limit_bytes=60 * 1024 * 1024
        ),
    )(links, kernel.reshape(81, 4, 8), active, direction, out_grad)
    return pl.pallas_call(
        hand_on,
        out_shape=(
            jax.ShapeDtypeStruct(links.shape, F32),
            jax.ShapeDtypeStruct(kernel.shape, F32),
        ),
        in_specs=[hbm] * 2,
        out_specs=(hbm, hbm),
        scratch_shapes=[space(*links.shape), space(*kernel.shape), sems(4)],
        compiler_params=pltpu.CompilerParams(vmem_limit_bytes=60 * 1024 * 1024),
    )(link_grad, kernel_grad)


def solution(mesh):
    n_space, n_tm = mesh.shape["space"], mesh.shape["tm"]
    n_far = 2
    n_x = max(1, n_space // (8 * n_far))
    axes = (n_x, n_space // (n_x * n_far), n_far, n_tm // 2)
    sites = n_space * n_tm * 4 * 128
    placed = (
        P(None, None, None, None, "space", "tm", None),
        P(),
        P("space", "tm", None),
        P("space", "tm", None),
        P(None, None, None, None, "space", "tm", None),
    )
    return jax.shard_map(
        functools.partial(shards, (n_space, n_tm, axes, 1.0 / math.sqrt(sites))),
        mesh=mesh,
        in_specs=placed,
        out_specs=(P(None, None, None, None, "space", "tm", None), P()),
        check_vma=False,
    )
```
